32 devices in a mesh: dp: 2 (over x), fsdp: 16 (over z, y, core).
Axes of the slice: x: 2, y: 2, z: 4, core: 2. Of those that a mesh axis runs over, the one named last changes fastest.
Arguments:
- tokens: bfloat16 [49152, 768], P(('dp', 'fsdp')), may hold values from -14 to 14
- masked_pos: int32 [96, 104], P(('dp', 'fsdp')), may hold values from 0 to 511, as said below
- masked_count: int32 [96], P(('dp', 'fsdp')), may hold values from 52 to 104, as said below
- out_grad: bfloat16 [96, 104, 768], P(('dp', 'fsdp')), may hold values from -6 to 6
- weights: bfloat16 [9216, 768], P('fsdp'), may hold values from -5 to 5
- vectors: float32 [12, 768], replicated, may hold values from -2 to 2
- owner_list: int32 [192], replicated, may hold values from 0 to 15, as said below
- master_slots: float32 [384, 48, 768], P('fsdp'), may hold values from -5 to 5
- first_slots: float32 [384, 48, 768], P('fsdp')
- second_slots: float32 [384, 48, 768], P('fsdp'), as said below
- vector_first: float32 [12, 768], replicated
- vector_second: float32 [12, 768], replicated, as said below
Outputs:
- layer_out: bfloat16 [49152, 768], P(('dp', 'fsdp'))
- token_grad: float32 [49152, 768], P(('dp', 'fsdp'))
- new_weights: float32 [9216, 768], P('fsdp')
- new_first: float32 [384, 48, 768], P('fsdp')
- new_second: float32 [384, 48, 768], P('fsdp')
- new_vectors: float32 [12, 768], replicated
- new_vector_first: float32 [12, 768], replicated
- new_vector_second: float32 [12, 768], replicated
The draws below stay inside these ranges and needn't reach their ends.
Inputs may be any that keep to these rules, and one draw needn't show every extreme that they name: `masked_pos`: within a page the 104 positions are distinct; only the first masked_count of them are used. `masked_count`: some page of every draw uses exactly 104. `owner_list`: each fsdp index owns at most 24 blocks, and some index owns exactly 24. `second_slots`: Positive. `vector_second`: Positive.
All inputs are finite; a program needn't handle non-finite values.
Results may differ from the reference program's by a relative error of at most 0.011.
Values may be sent and summed in bfloat16 or wider, within the bound.
No kernel may reach another device: no remote copies, remote signals or barrier semaphores. Data moves between devices by JAX's collectives and lax.ppermute only.
A program may use at most 320 MiB of HBM per device.

```python
import math
import jax
import jax.numpy as jnp
from jax import lax

MODEL_WIDTH = 768
HEADS = 12
HD = 64
FF = 3072
PAGE = 512
PAGES_DEV = 3
MASKM = 104
BLOCK_ROWS = 48
STEP = 10
PAGES = 96
TOKENS = 49152
WROWS = 9216
NBLK = 192
CAP = 24
SLOT_COUNT = 384
VEC = 12


def coarse_noise(noise_key, shape):
    return jnp.clip(jax.random.normal(noise_key, shape, jnp.float32), -4.0, 4.0)


def row_kinds(first_rows):
    kinds = (first_rows >= MODEL_WIDTH).astype(jnp.int32) + (first_rows >= 2 * MODEL_WIDTH).astype(jnp.int32)
    kinds = kinds + (first_rows >= 3 * MODEL_WIDTH).astype(jnp.int32) + (first_rows >= 4 * MODEL_WIDTH).astype(jnp.int32)
    return kinds + (first_rows >= 4 * MODEL_WIDTH + FF).astype(jnp.int32)


def spread_table():
    inner = 1.0 / math.sqrt(MODEL_WIDTH)
    return jnp.array([0.8 * inner, 0.8 * inner, inner, 8.0 * inner, inner, 1.5 / math.sqrt(FF)], jnp.float32)


def grad_table():
    root_count = math.sqrt(PAGES * MASKM * 3.0 / 4.0)
    return root_count * jnp.array([0.8, 2.0, 1.5, 0.1, 0.4, 0.65], jnp.float32)


def owner_table(key):
    base_key = jax.random.fold_in(key, 7)
    owners = 2 * NBLK // CAP
    half_cap = CAP // 2
    shuffled = jax.random.permutation(jax.random.fold_in(base_key, 1), owners)
    offset = jax.random.randint(jax.random.fold_in(base_key, 2), (owners // 2,), 0, half_cap + 1)
    offset = jnp.where(jnp.arange(owners // 2) == 0, half_cap, offset)
    paired = jnp.stack([half_cap + offset, half_cap - offset], axis=1).reshape(owners).astype(jnp.int32)
    counts = jnp.zeros((owners,), jnp.int32).at[shuffled].set(paired)
    bounds = jnp.cumsum(counts)
    sorted_owner = jnp.sum((bounds[None, :] <= jnp.arange(NBLK, dtype=jnp.int32)[:, None]).astype(jnp.int32), axis=1)
    return sorted_owner[jax.random.permutation(jax.random.fold_in(base_key, 3), NBLK)].astype(jnp.int32)


def slot_kinds(key):
    owner_list = owner_table(key)
    block_ids = jnp.arange(NBLK, dtype=jnp.int32)
    same_owner = owner_list[:, None] == owner_list[None, :]
    block_rank = jnp.sum((same_owner & (block_ids[None, :] < block_ids[:, None])).astype(jnp.int32), axis=1)
    block_slot_map = owner_list * CAP + block_rank
    match_flags = block_slot_map[:, None] == jnp.arange(SLOT_COUNT, dtype=jnp.int32)[None, :]
    chosen = jnp.sum(jnp.where(match_flags, block_ids[:, None], 0), axis=0)
    return row_kinds(chosen * BLOCK_ROWS)


def draw_owner_list(key, part):
    return owner_table(key)


def draw_tokens(key, part):
    base_key = jax.random.fold_in(key, 31)
    row_scale = jnp.exp(jax.random.uniform(jax.random.fold_in(base_key, 1), (TOKENS, 1), jnp.float32, math.log(0.5), math.log(2.0)))
    column_scale = jnp.exp(jax.random.uniform(jax.random.fold_in(base_key, 2), (1, MODEL_WIDTH), jnp.float32, math.log(0.6), math.log(1.7)))
    noise = coarse_noise(jax.random.fold_in(base_key, 3), (TOKENS, MODEL_WIDTH))
    return (noise * row_scale * column_scale).astype(jnp.bfloat16)


def draw_masked_pos(key, part):
    page_keys = jax.random.split(jax.random.fold_in(key, 21), PAGES)
    chosen = jax.vmap(lambda page_key: jax.random.permutation(page_key, PAGE)[:MASKM])(page_keys)
    return jnp.sort(chosen, axis=1).astype(jnp.int32)


def draw_masked_count(key, part):
    counts = jax.random.randint(jax.random.fold_in(key, 22), (PAGES,), MASKM // 2, MASKM + 1)
    fullest = jax.random.randint(jax.random.fold_in(key, 23), (), 0, PAGES)
    return jnp.where(jnp.arange(PAGES) == fullest, MASKM, counts).astype(jnp.int32)


def draw_weights(key, part):
    base_key = jax.random.fold_in(key, 41)
    scale_value = jnp.take(spread_table(), row_kinds(jnp.arange(WROWS, dtype=jnp.int32)))[:, None]
    return (coarse_noise(base_key, (WROWS, MODEL_WIDTH)) * scale_value).astype(jnp.bfloat16)


def draw_vectors(key, part):
    base_key = jax.random.fold_in(key, 51)
    row_index = jnp.arange(VEC, dtype=jnp.int32)[:, None]
    up_rows = FF // MODEL_WIDTH
    gain_rows = (row_index == 4 + up_rows) | (row_index == 6 + up_rows)
    gains = jax.random.uniform(jax.random.fold_in(base_key, 1), (VEC, MODEL_WIDTH), jnp.float32, 0.6, 1.6)
    shifts = 0.3 * coarse_noise(jax.random.fold_in(base_key, 2), (VEC, MODEL_WIDTH))
    return jnp.where(gain_rows, gains, shifts).astype(jnp.float32)


def draw_master_slots(key, part):
    scale_value = jnp.take(spread_table(), slot_kinds(key))[:, None, None]
    return (coarse_noise(jax.random.fold_in(key, 61), (SLOT_COUNT, BLOCK_ROWS, MODEL_WIDTH)) * scale_value).astype(jnp.float32)


def draw_first_slots(key, part):
    scale_value = jnp.take(grad_table(), slot_kinds(key))[:, None, None]
    return (coarse_noise(jax.random.fold_in(key, 62), (SLOT_COUNT, BLOCK_ROWS, MODEL_WIDTH)) * scale_value).astype(jnp.float32)


def draw_second_slots(key, part):
    scale_value = jnp.take(grad_table(), slot_kinds(key))[:, None, None]
    scale_factor = jnp.exp(jax.random.uniform(jax.random.fold_in(key, 63), (SLOT_COUNT, BLOCK_ROWS, MODEL_WIDTH), jnp.float32, math.log(0.5), math.log(8.0)))
    return (scale_value * scale_value * scale_factor).astype(jnp.float32)


def draw_vector_first(key, part):
    root_count = math.sqrt(PAGES * MASKM * 3.0 / 4.0)
    return (0.5 * root_count * coarse_noise(jax.random.fold_in(key, 71), (VEC, MODEL_WIDTH))).astype(jnp.float32)


def draw_vector_second(key, part):
    root_count = math.sqrt(PAGES * MASKM * 3.0 / 4.0)
    scale_factor = jnp.exp(jax.random.uniform(jax.random.fold_in(key, 72), (VEC, MODEL_WIDTH), jnp.float32, math.log(0.5), math.log(8.0)))
    return (0.25 * root_count * root_count * scale_factor).astype(jnp.float32)


def level_of(stream_key, extent, cuts, smallest, high):
    level, own = 1.0, jax.random.fold_in(stream_key, 6)
    for dim, parts in cuts:
        draws = jnp.exp(jax.random.uniform(jax.random.fold_in(own, dim), (parts,), jnp.float32, smallest / len(cuts), high / len(cuts)))
        level = level * jnp.repeat(draws, extent[dim] // parts).reshape([-1 if axis == dim else 1 for axis in range(len(extent))])
    return level


def bell_draw(key, dims, spread, bound, pieces=(), kind=jnp.bfloat16):
    drawn = spread * jax.random.normal(key, dims, jnp.float32)
    if pieces:
        drawn = drawn * level_of(key, dims, pieces, -0.22, 0.18)
    return jnp.clip(drawn, -bound, bound).astype(kind)


def setup_inputs(seed: int = 0) -> dict:
    keys = jax.random.split(jax.random.key(seed), 13)
    tokens = draw_tokens(jax.random.fold_in(keys[12], 71), 0)
    masked_pos = draw_masked_pos(jax.random.fold_in(keys[12], 71), 0)
    masked_count = draw_masked_count(jax.random.fold_in(keys[12], 71), 0)
    out_grad = bell_draw(keys[3], (PAGES, MASKM, MODEL_WIDTH), 1.0, 6.0, ((0, 32),))
    weights = draw_weights(jax.random.fold_in(keys[12], 71), 0)
    vectors = draw_vectors(jax.random.fold_in(keys[12], 71), 0)
    owner_list = draw_owner_list(jax.random.fold_in(keys[12], 71), 0)
    master_slots = draw_master_slots(jax.random.fold_in(keys[12], 71), 0)
    first_slots = draw_first_slots(jax.random.fold_in(keys[12], 71), 0)
    second_slots = draw_second_slots(jax.random.fold_in(keys[12], 71), 0)
    vector_first = draw_vector_first(jax.random.fold_in(keys[12], 71), 0)
    vector_second = draw_vector_second(jax.random.fold_in(keys[12], 71), 0)
    return dict(tokens=tokens, masked_pos=masked_pos, masked_count=masked_count, out_grad=out_grad, weights=weights, vectors=vectors, owner_list=owner_list, master_slots=master_slots, first_slots=first_slots, second_slots=second_slots, vector_first=vector_first, vector_second=vector_second)


HIGHEST_PRECISION = lax.Precision.HIGHEST
QUERY_SCALE = 0.125
NORM_EPSILON = 1e-06
INV_ROOT_TWO = 0.7071067811865476
FIRST_DECAY = 0.5
SECOND_DECAY = 0.5
LEARN_RATE = 0.05
VECTOR_RATE = 0.3
WEIGHT_DECAY = 0.01
ADAM_EPSILON = 1e-08

@jax.custom_vjp
def low(v):
    return lax.optimization_barrier(v.astype(jnp.bfloat16)).astype(jnp.float32)

@jax.custom_vjp
def low_back(v):
    return v

def low_keep(v):
    return (low(v), None)

def low_pass(kept, grad):
    return (grad,)

def back_keep(v):
    return (v, None)

def back_low(kept, grad):
    return (low(grad),)
low.defvjp(low_keep, low_pass)
low_back.defvjp(back_keep, back_low)

def product(left_side, right_side):
    return jnp.dot(left_side, right_side, precision=HIGHEST_PRECISION, preferred_element_type=jnp.float32)

def normalize(token_rows, gain_row, shift_row):
    center = token_rows - lax.optimization_barrier(jnp.mean(token_rows, axis=-1, keepdims=True))
    inverse = lax.rsqrt(lax.optimization_barrier(jnp.mean(center * center, axis=-1, keepdims=True)) + NORM_EPSILON)
    return center * inverse * gain_row + shift_row

def gelu_exact(preact):
    return 0.5 * preact * (1.0 + jax.scipy.special.erf(preact * INV_ROOT_TWO))

def attend_page(operands):
    queries, key_rows, values = operands
    scores = low_back(jnp.einsum('hqd,hkd->hqk', queries, key_rows, precision=HIGHEST_PRECISION))
    row_max = lax.optimization_barrier(jnp.max(scores, axis=2, keepdims=True))
    exponent = jnp.exp(scores - row_max)
    probability = low(exponent / lax.optimization_barrier(jnp.sum(exponent, axis=2, keepdims=True)))
    return jnp.einsum('hqk,hkd->hqd', probability, values, precision=HIGHEST_PRECISION)

def forward_pages(token_rows, weight_stack, vector_rows):
    page_count = token_rows.shape[0] // PAGE
    up_rows = FF // MODEL_WIDTH
    weight_query = weight_stack[0:MODEL_WIDTH]
    weight_key = weight_stack[MODEL_WIDTH:2 * MODEL_WIDTH]
    weight_value = weight_stack[2 * MODEL_WIDTH:3 * MODEL_WIDTH]
    weight_out = weight_stack[3 * MODEL_WIDTH:4 * MODEL_WIDTH]
    weight_up = weight_stack[4 * MODEL_WIDTH:4 * MODEL_WIDTH + FF]
    weight_down = weight_stack[4 * MODEL_WIDTH + FF:4 * MODEL_WIDTH + 2 * FF]
    bias_up = vector_rows[3:3 + up_rows].reshape(FF)
    queries = low_back(low((product(token_rows, weight_query) + vector_rows[0]) * QUERY_SCALE))
    key_rows = low_back(low(product(token_rows, weight_key)))
    values = low_back(low(product(token_rows, weight_value) + vector_rows[1]))

    def heads_first(tensor):
        return tensor.reshape(page_count, PAGE, HEADS, HD).transpose(0, 2, 1, 3)
    context = lax.map(jax.checkpoint(attend_page), (heads_first(queries), heads_first(key_rows), heads_first(values)))
    context = low_back(low(context.transpose(0, 2, 1, 3).reshape(page_count * PAGE, MODEL_WIDTH)))
    attn_out = low_back(product(context, weight_out) + vector_rows[2])
    hidden_one = normalize(token_rows + attn_out, vector_rows[4 + up_rows], vector_rows[5 + up_rows])
    up_pre = lax.dot_general(low(hidden_one), weight_up, (((1,), (1,)), ((), ())), precision=HIGHEST_PRECISION, preferred_element_type=jnp.float32)
    up_pre = low_back(up_pre + bias_up)
    activation = low(gelu_exact(up_pre))
    down_out = low_back(product(activation, weight_down) + vector_rows[3 + up_rows])
    return normalize(hidden_one + down_out, vector_rows[6 + up_rows], vector_rows[7 + up_rows])

def adam_step(parameter, moment_one, moment_two, gradient, rate):
    moment_one = FIRST_DECAY * moment_one + (1.0 - FIRST_DECAY) * gradient
    moment_two = SECOND_DECAY * moment_two + (1.0 - SECOND_DECAY) * gradient * gradient
    ascent = moment_one / (1.0 - FIRST_DECAY ** STEP) / (jnp.sqrt(moment_two / (1.0 - SECOND_DECAY ** STEP)) + ADAM_EPSILON)
    return (parameter - rate * (ascent + WEIGHT_DECAY * parameter), moment_one, moment_two)

def reference(tokens, masked_pos, masked_count, out_grad, weights, vectors, owner_list, master_slots, first_slots, second_slots, vector_first, vector_second):
    group_pages = PAGES_DEV
    group_count = PAGES // group_pages
    weight_float = weights.astype(jnp.float32)

    def one_group(carried, operands):
        token_rows, positions, counts, cot_rows = operands
        layer_rows, pullback = jax.vjp(forward_pages, token_rows.astype(jnp.float32), weight_float, vectors)
        live_slots = jnp.arange(MASKM, dtype=jnp.int32)[None, :] < counts[:, None]
        placed = (positions[:, :, None] == jnp.arange(PAGE, dtype=jnp.int32)[None, None, :]) & live_slots[:, :, None]
        cotangent = jnp.einsum('pms,pmd->psd', placed.astype(jnp.float32), cot_rows.astype(jnp.float32), precision=HIGHEST_PRECISION)
        grad_rows, grad_weights, grad_vectors = pullback(cotangent.reshape(group_pages * PAGE, MODEL_WIDTH))
        return ((carried[0] + grad_weights, carried[1] + grad_vectors), (layer_rows.astype(jnp.bfloat16), grad_rows))
    start_sums = (jnp.zeros((WROWS, MODEL_WIDTH), jnp.float32), jnp.zeros((VEC, MODEL_WIDTH), jnp.float32))
    operands = (tokens.reshape(group_count, group_pages * PAGE, MODEL_WIDTH), masked_pos.reshape(group_count, group_pages, MASKM), masked_count.reshape(group_count, group_pages), out_grad.reshape(group_count, group_pages, MASKM, MODEL_WIDTH))
    (grad_stack, grad_vectors), (layer_out, token_grad) = lax.scan(one_group, start_sums, operands)
    layer_out = layer_out.reshape(TOKENS, MODEL_WIDTH)
    token_grad = token_grad.reshape(TOKENS, MODEL_WIDTH)
    block_ids = jnp.arange(NBLK, dtype=jnp.int32)
    same_owner = owner_list[:, None] == owner_list[None, :]
    block_rank = lax.optimization_barrier(jnp.sum((same_owner & (block_ids[None, :] < block_ids[:, None])).astype(jnp.int32), axis=1))
    block_slot_map = owner_list * CAP + block_rank
    match_flags = block_slot_map[:, None] == jnp.arange(SLOT_COUNT, dtype=jnp.int32)[None, :]
    present = jnp.any(match_flags, axis=0)
    chosen = lax.optimization_barrier(jnp.sum(jnp.where(match_flags, block_ids[:, None], 0), axis=0)).astype(jnp.int32)
    grad_slots = jnp.where(present[:, None, None], grad_stack.reshape(NBLK, BLOCK_ROWS, MODEL_WIDTH)[chosen], 0.0)
    new_master, new_first, new_second = adam_step(master_slots, first_slots, second_slots, grad_slots, LEARN_RATE)
    new_vectors, new_vector_first, new_vector_second = adam_step(vectors, vector_first, vector_second, grad_vectors, VECTOR_RATE)
    new_weights = new_master[block_slot_map].reshape(WROWS, MODEL_WIDTH)
    return (layer_out, token_grad, new_weights, new_first, new_second, new_vectors, new_vector_first, new_vector_second)
```

```python
import functools

import jax
import jax.numpy as jnp
from jax import lax
from jax.experimental import pallas as pl
from jax.experimental.pallas import tpu as pltpu
from jax.sharding import PartitionSpec as P

WIDTH = 768
HEADS = 12
HD = 64
FF = 3072
PAGE = 512
MASKM = 104
ROWS = 48
STEP = 10
NBLK = 192
PAD = 128
UP_ROWS = FF // WIDTH

QUERY_SCALE = 0.125
NORM_EPSILON = 1e-06
INV_ROOT_TWO = 0.7071067811865476
INV_ROOT_TAU = 0.3989422804014327
FIRST_DECAY = 0.5
SECOND_DECAY = 0.5
LEARN_RATE = 0.05
VECTOR_RATE = 0.3
WEIGHT_DECAY = 0.01
ADAM_EPSILON = 1e-08

BF = jnp.bfloat16
F32 = jnp.float32
VMEM_LIMIT = 60 * 1024 * 1024
ANY = pl.BlockSpec(memory_space=pl.ANY)


def mm(a, b):
    return lax.dot_general(a, b, (((1,), (0,)), ((), ())), preferred_element_type=F32)


def mm_last(a, b):
    return lax.dot_general(a, b, (((1,), (1,)), ((), ())), preferred_element_type=F32)


def mm_first(a, b):
    return lax.dot_general(a, b, (((0,), (0,)), ((), ())), preferred_element_type=F32)


def row_sum(x):
    return jnp.sum(x, axis=0, keepdims=True)


def unit_of(x):
    center = x - jnp.mean(x, axis=1, keepdims=True)
    inverse = lax.rsqrt(jnp.mean(center * center, axis=1, keepdims=True) + NORM_EPSILON)
    return center * inverse, inverse


def unit_back(grad_out, gain, unit, inverse):
    grad_unit = grad_out * gain
    centered = grad_unit - jnp.mean(grad_unit, axis=1, keepdims=True)
    return inverse * (centered - unit * jnp.mean(grad_unit * unit, axis=1, keepdims=True))


def gelu_cdf(u):
    return 0.5 * (1.0 + lax.erf(u * INV_ROOT_TWO))


def half_masks():
    lane = lax.broadcasted_iota(jnp.int32, (1, 2 * HD), 1)
    low = jnp.where(lane < HD, 1.0, 0.0)
    return (low.astype(BF), (1.0 - low).astype(BF)), lane < HD


def softmax(scores):
    top = jnp.max(scores, axis=1, keepdims=True)
    exponent = jnp.exp(scores - top)
    total = jnp.sum(exponent, axis=1, keepdims=True)
    return exponent * (1.0 / total)


def one_hot_rows(pos):
    return jnp.where(
        pos == lax.broadcasted_iota(jnp.int32, (PAD, PAGE), 1), 1.0, 0.0
    ).astype(BF)


def project_kernel(
    pos_ref, tok_ref, vec_ref, w_any, q_ref, k_ref, v_ref, tm_ref, qm_ref, cm_ref, w_ref, sem
):
    @pl.when(pl.program_id(0) == 0)
    def _():
        copy = pltpu.make_async_copy(w_any.at[pl.ds(0, 3 * WIDTH)], w_ref, sem)
        copy.start()
        copy.wait()

    tok = tok_ref[...]
    q = ((mm(tok, w_ref[0:WIDTH]) + vec_ref[0:1]) * QUERY_SCALE).astype(BF)
    k = mm(tok, w_ref[WIDTH : 2 * WIDTH]).astype(BF)
    v = (mm(tok, w_ref[2 * WIDTH : 3 * WIDTH]) + vec_ref[1:2]).astype(BF)
    q_ref[...] = q
    k_ref[...] = k
    v_ref[...] = v
    pick = one_hot_rows(pos_ref[0])
    tm_ref[...] = mm(pick, tok).astype(BF)
    qm = mm(pick, q).astype(BF)
    qm_ref[...] = qm
    masks, low = half_masks()
    for pair in range(HEADS // 2):
        cols = slice(pair * 2 * HD, (pair + 1) * 2 * HD)
        kp, vp, qp = k[:, cols], v[:, cols], qm[:, cols]
        parts = []
        for mask in masks:
            prob = softmax(mm_last(qp * mask, kp)).astype(BF)
            parts.append(mm(prob, vp))
        cm_ref[:, cols] = jnp.where(low, parts[0], parts[1]).astype(BF)


def project(tokens, pos, vectors, stack):
    pages = tokens.shape[0] // PAGE
    tall = jax.ShapeDtypeStruct((pages * PAGE, WIDTH), BF)
    short = jax.ShapeDtypeStruct((pages * PAD, WIDTH), BF)
    page = pl.BlockSpec((PAGE, WIDTH), lambda i: (i, 0))
    few = pl.BlockSpec((PAD, WIDTH), lambda i: (i, 0))
    return pl.pallas_call(
        project_kernel,
        grid=(pages,),
        in_specs=[
            pl.BlockSpec((1, PAD, 1), lambda i: (i, 0, 0)),
            page,
            pl.BlockSpec((12, WIDTH), lambda i: (0, 0)),
            ANY,
        ],
        out_specs=[page, page, page, few, few, few],
        out_shape=[tall, tall, tall, short, short, short],
        scratch_shapes=[pltpu.VMEM((3 * WIDTH, WIDTH), BF), pltpu.SemaphoreType.DMA],
        compiler_params=pltpu.CompilerParams(vmem_limit_bytes=VMEM_LIMIT),
        name="project",
    )(pos, tokens, vectors, stack)


def masked_kernel(
    place_ref,
    tm_ref,
    cm_ref,
    cot_ref,
    vec_ref,
    w_any,
    gr_ref,
    gc_ref,
    gv_ref,
    dw_any,
    w_ref,
    up_ref,
    act_ref,
    hid_ref,
    stage_ref,
    in_sem,
    out_sem,
):
    parts = 1 + 2 * UP_ROWS
    loads = [
        pltpu.make_async_copy(
            w_any.at[pl.ds((3 + i) * WIDTH, WIDTH)], w_ref.at[i], in_sem.at[i]
        )
        for i in range(parts)
    ]
    for load in loads:
        load.start()
    per = WIDTH // ROWS

    def send(part, value):
        stage_ref[pl.ds(part * per, per)] = value.astype(BF).reshape(per, ROWS, WIDTH)

        @pl.loop(0, per)
        def _(i):
            block = part * per + i
            pltpu.make_async_copy(
                stage_ref.at[block], dw_any.at[place_ref[3 * per + block]], out_sem
            ).start()

    gain_one, shift_one = vec_ref[8:9], vec_ref[9:10]
    gain_two = vec_ref[10:11]
    cm = cm_ref[...]
    loads[0].wait()
    resid_one = tm_ref[...].astype(F32) + mm(cm, w_ref[0]) + vec_ref[2:3]
    unit_one, inv_one = unit_of(resid_one)
    hidden_one = unit_one * gain_one + shift_one
    hid_ref[...] = hidden_one.astype(BF)
    hid = hid_ref[...]
    for c in range(UP_ROWS):
        cols = slice(c * WIDTH, (c + 1) * WIDTH)
        loads[1 + c].wait()
        up = mm_last(hid, w_ref[1 + c]) + vec_ref[3 + c : 4 + c]
        up_ref[:, cols] = up
        act_ref[:, cols] = (up * gelu_cdf(up)).astype(BF)
    resid_two = hidden_one + vec_ref[7:8]
    for c in range(UP_ROWS):
        cols = slice(c * WIDTH, (c + 1) * WIDTH)
        loads[1 + UP_ROWS + c].wait()
        resid_two = resid_two + mm(act_ref[:, cols], w_ref[1 + UP_ROWS + c])
    unit_two, inv_two = unit_of(resid_two)
    cot = cot_ref[...].astype(F32)
    grad_two = unit_back(cot, gain_two, unit_two, inv_two)
    gv_ref[...] = jnp.zeros_like(gv_ref)
    gv_ref[10:11] = row_sum(cot * unit_two)
    gv_ref[11:12] = row_sum(cot)
    down = grad_two.astype(BF)
    gv_ref[7:8] = row_sum(down.astype(F32))
    grad_hidden = grad_two
    for c in range(UP_ROWS):
        cols = slice(c * WIDTH, (c + 1) * WIDTH)
        send(1 + UP_ROWS + c, mm_first(act_ref[:, cols], down))
        up = up_ref[:, cols]
        slope = gelu_cdf(up) + up * jnp.exp(-0.5 * up * up) * INV_ROOT_TAU
        grad_up = (mm_last(down, w_ref[1 + UP_ROWS + c]) * slope).astype(BF)
        gv_ref[3 + c : 4 + c] = row_sum(grad_up.astype(F32))
        send(1 + c, mm_first(grad_up, hid))
        grad_hidden = grad_hidden + mm(grad_up, w_ref[1 + c])
    gv_ref[8:9] = row_sum(grad_hidden * unit_one)
    gv_ref[9:10] = row_sum(grad_hidden)
    grad_one = unit_back(grad_hidden, gain_one, unit_one, inv_one)
    gr_ref[...] = grad_one
    attn = grad_one.astype(BF)
    gv_ref[2:3] = row_sum(attn.astype(F32))
    send(0, mm_first(cm, attn))
    gc_ref[...] = mm_last(attn, w_ref[0]).astype(BF)
    total = parts * per
    pltpu.make_async_copy(stage_ref, dw_any.at[pl.ds(0, total)], out_sem).wait()


def masked_part(place, tm, cm, cot, vectors, stack):
    rows = tm.shape[0]
    parts = 1 + 2 * UP_ROWS
    vm = pl.BlockSpec(memory_space=pltpu.VMEM)
    return pl.pallas_call(
        masked_kernel,
        grid_spec=pltpu.PrefetchScalarGridSpec(
            num_scalar_prefetch=1,
            grid=(),
            in_specs=[vm, vm, vm, vm, ANY],
            out_specs=[vm, vm, vm, ANY],
            scratch_shapes=[
                pltpu.VMEM((parts, WIDTH, WIDTH), BF),
                pltpu.VMEM((rows, FF), F32),
                pltpu.VMEM((rows, FF), BF),
                pltpu.VMEM((rows, WIDTH), BF),
                pltpu.VMEM((parts * WIDTH // ROWS, ROWS, WIDTH), BF),
                pltpu.SemaphoreType.DMA((parts,)),
                pltpu.SemaphoreType.DMA,
            ],
        ),
        out_shape=[
            jax.ShapeDtypeStruct((rows, WIDTH), F32),
            jax.ShapeDtypeStruct((rows, WIDTH), BF),
            jax.ShapeDtypeStruct((16, WIDTH), F32),
            jax.ShapeDtypeStruct((NBLK, ROWS, WIDTH), BF),
        ],
        compiler_params=pltpu.CompilerParams(vmem_limit_bytes=VMEM_LIMIT),
        name="masked",
    )(place, tm, cm, cot, vectors, stack)


def attention_back_kernel(
    place_ref,
    tok_ref,
    k_ref,
    v_ref,
    tm_ref,
    qm_ref,
    gc_ref,
    dw_in,
    dq_ref,
    dk_ref,
    dv_ref,
    gv_ref,
    dw_any,
    sum_ref,
    stage_ref,
    out_sem,
):
    page, last = pl.program_id(0), pl.num_programs(0) - 1
    per = WIDTH // ROWS
    masks, low = half_masks()

    @pl.when(page == 0)
    def _():
        sum_ref[...] = jnp.zeros_like(sum_ref)
        gv_ref[...] = jnp.zeros_like(gv_ref)

    for pair in range(HEADS // 2):
        cols = slice(pair * 2 * HD, (pair + 1) * 2 * HD)
        kp, vp, qp, gp = k_ref[:, cols], v_ref[:, cols], qm_ref[:, cols], gc_ref[:, cols]
        grad_v, grad_k, grad_q = None, None, []
        for mask in masks:
            qh, gh = qp * mask, gp * mask
            prob = softmax(mm_last(qh, kp))
            grad_prob = mm_last(gh, vp)
            spread = jnp.sum(prob * grad_prob, axis=1, keepdims=True)
            grad_s = (prob * (grad_prob - spread)).astype(BF)
            one_v = mm_first(prob.astype(BF), gh)
            one_k = mm_first(grad_s, qh)
            grad_v = one_v if grad_v is None else grad_v + one_v
            grad_k = one_k if grad_k is None else grad_k + one_k
            grad_q.append(mm(grad_s, kp))
        dv_ref[:, cols] = grad_v.astype(BF)
        dk_ref[:, cols] = grad_k.astype(BF)
        dq_ref[:, cols] = jnp.where(low, grad_q[0], grad_q[1]).astype(BF) * QUERY_SCALE
    dq, dk, dv = dq_ref[...], dk_ref[...], dv_ref[...]
    gv_ref[0:1] += row_sum(dq.astype(F32))
    gv_ref[1:2] += row_sum(dv.astype(F32))
    tok = tok_ref[...]
    sum_ref[0] += mm_first(tm_ref[...], dq)
    sum_ref[1] += mm_first(tok, dk)
    sum_ref[2] += mm_first(tok, dv)

    @pl.when(page == last)
    def _():
        for i in range(3):
            stage_ref[pl.ds(i * per, per)] = (
                sum_ref[i].astype(BF).reshape(per, ROWS, WIDTH)
            )

        @pl.loop(0, 3 * per)
        def _(i):
            pltpu.make_async_copy(
                stage_ref.at[i], dw_any.at[place_ref[i]], out_sem
            ).start()

        pltpu.make_async_copy(stage_ref, dw_any.at[pl.ds(0, 3 * per)], out_sem).wait()


def attention_back(place, tokens, k, v, tm, qm, gc, dw):
    pages = tokens.shape[0] // PAGE
    page = pl.BlockSpec((PAGE, WIDTH), lambda i, s: (i, 0))
    few = pl.BlockSpec((PAD, WIDTH), lambda i, s: (i, 0))
    tall = jax.ShapeDtypeStruct((pages * PAGE, WIDTH), BF)
    return pl.pallas_call(
        attention_back_kernel,
        grid_spec=pltpu.PrefetchScalarGridSpec(
            num_scalar_prefetch=1,
            grid=(pages,),
            in_specs=[page, page, page, few, few, few, ANY],
            out_specs=[few, page, page, pl.BlockSpec((8, WIDTH), lambda i, s: (0, 0)), ANY],
            scratch_shapes=[
                pltpu.VMEM((3, WIDTH, WIDTH), F32),
                pltpu.VMEM((3 * WIDTH // ROWS, ROWS, WIDTH), BF),
                pltpu.SemaphoreType.DMA,
            ],
        ),
        out_shape=[
            jax.ShapeDtypeStruct((pages * PAD, WIDTH), BF),
            tall,
            tall,
            jax.ShapeDtypeStruct((8, WIDTH), F32),
            jax.ShapeDtypeStruct(dw.shape, BF),
        ],
        input_output_aliases={7: 4},
        compiler_params=pltpu.CompilerParams(vmem_limit_bytes=VMEM_LIMIT),
        name="attention_back",
    )(place, tokens, k, v, tm, qm, gc, dw)


def forward_kernel(tok_ref, q_ref, k_ref, v_ref, vec_ref, w_any, out_ref, w_ref, ctx_ref, sem):
    parts = 1 + 2 * UP_ROWS

    @pl.when(pl.program_id(0) == 0)
    def _():
        pltpu.make_async_copy(w_any.at[pl.ds(3 * WIDTH, parts * WIDTH)], w_ref, sem).start()

    masks, low = half_masks()
    for pair in range(HEADS // 2):
        cols = slice(pair * 2 * HD, (pair + 1) * 2 * HD)
        kp, vp, qp = k_ref[:, cols], v_ref[:, cols], q_ref[:, cols]
        halves = []
        for mask in masks:
            prob = softmax(mm_last(qp * mask, kp)).astype(BF)
            halves.append(mm(prob, vp))
        ctx_ref[:, cols] = jnp.where(low, halves[0], halves[1]).astype(BF)

    @pl.when(pl.program_id(0) == 0)
    def _():
        pltpu.make_async_copy(w_any.at[pl.ds(3 * WIDTH, parts * WIDTH)], w_ref, sem).wait()

    resid_one = tok_ref[...].astype(F32) + mm(ctx_ref[...], w_ref[0:WIDTH]) + vec_ref[2:3]
    unit_one, _ = unit_of(resid_one)
    hidden_one = unit_one * vec_ref[8:9] + vec_ref[9:10]
    hid = hidden_one.astype(BF)
    resid_two = hidden_one + vec_ref[7:8]
    for c in range(UP_ROWS):
        at, to = (1 + c) * WIDTH, (1 + UP_ROWS + c) * WIDTH
        up = mm_last(hid, w_ref[at : at + WIDTH]) + vec_ref[3 + c : 4 + c]
        act = (up * gelu_cdf(up)).astype(BF)
        resid_two = resid_two + mm(act, w_ref[to : to + WIDTH])
    unit_two, _ = unit_of(resid_two)
    out_ref[...] = (unit_two * vec_ref[10:11] + vec_ref[11:12]).astype(BF)


def forward_rest(tokens, q, k, v, vectors, stack):
    pages = tokens.shape[0] // PAGE
    page = pl.BlockSpec((PAGE, WIDTH), lambda i: (i, 0))
    return pl.pallas_call(
        forward_kernel,
        grid=(pages,),
        in_specs=[page, page, page, page, pl.BlockSpec((12, WIDTH), lambda i: (0, 0)), ANY],
        out_specs=page,
        out_shape=jax.ShapeDtypeStruct(tokens.shape, BF),
        scratch_shapes=[
            pltpu.VMEM(((1 + 2 * UP_ROWS) * WIDTH, WIDTH), BF),
            pltpu.VMEM((PAGE, WIDTH), BF),
            pltpu.SemaphoreType.DMA,
        ],
        compiler_params=pltpu.CompilerParams(vmem_limit_bytes=VMEM_LIMIT),
        name="forward_rest",
    )(tokens, q, k, v, vectors, stack)


def input_grad_kernel(pos_ref, dq_ref, dk_ref, dv_ref, gr_ref, w_any, out_ref, w_ref, sem):
    @pl.when(pl.program_id(0) == 0)
    def _():
        copy = pltpu.make_async_copy(w_any.at[pl.ds(0, 3 * WIDTH)], w_ref, sem)
        copy.start()
        copy.wait()

    few = gr_ref[...] + mm_last(dq_ref[...], w_ref[0:WIDTH])
    high = few.astype(BF)
    rest = (few - high.astype(F32)).astype(BF)
    pick = one_hot_rows(pos_ref[0])
    out_ref[...] = (
        mm_last(dk_ref[...], w_ref[WIDTH : 2 * WIDTH])
        + mm_last(dv_ref[...], w_ref[2 * WIDTH : 3 * WIDTH])
        + (mm_first(pick, high) + mm_first(pick, rest))
    )


def input_grad(pos, dq, dk, dv, gr, stack):
    pages = dk.shape[0] // PAGE
    page = pl.BlockSpec((PAGE, WIDTH), lambda i: (i, 0))
    few = pl.BlockSpec((PAD, WIDTH), lambda i: (i, 0))
    return pl.pallas_call(
        input_grad_kernel,
        grid=(pages,),
        in_specs=[pl.BlockSpec((1, PAD, 1), lambda i: (i, 0, 0)), few, page, page, few, ANY],
        out_specs=page,
        out_shape=jax.ShapeDtypeStruct(dk.shape, F32),
        scratch_shapes=[pltpu.VMEM((3 * WIDTH, WIDTH), BF), pltpu.SemaphoreType.DMA],
        compiler_params=pltpu.CompilerParams(vmem_limit_bytes=VMEM_LIMIT),
        name="input_grad",
    )(pos, dq, dk, dv, gr, stack)


def adam_step(parameter, moment_one, moment_two, gradient, rate):
    moment_one = FIRST_DECAY * moment_one + (1.0 - FIRST_DECAY) * gradient
    moment_two = SECOND_DECAY * moment_two + (1.0 - SECOND_DECAY) * gradient * gradient
    ascent = (
        moment_one
        / (1.0 - FIRST_DECAY**STEP)
        / (jnp.sqrt(moment_two / (1.0 - SECOND_DECAY**STEP)) + ADAM_EPSILON)
    )
    return (parameter - rate * (ascent + WEIGHT_DECAY * parameter), moment_one, moment_two)


def weight_step_kernel(from_ref, grad_ref, state_ref, out_ref):
    new, _, _ = adam_step(
        state_ref[0, 0].astype(F32),
        state_ref[0, 1].astype(F32),
        state_ref[0, 2].astype(F32),
        grad_ref[0].astype(F32),
        LEARN_RATE,
    )
    out_ref[0] = new.astype(BF)


def weight_step(source, grads, states):
    return pl.pallas_call(
        weight_step_kernel,
        grid_spec=pltpu.PrefetchScalarGridSpec(
            num_scalar_prefetch=1,
            grid=(grads.shape[0],),
            in_specs=[
                pl.BlockSpec((1, ROWS, WIDTH), lambda i, s: (i, 0, 0)),
                pl.BlockSpec((1, 3, ROWS, WIDTH), lambda i, s: (s[i], 0, 0, 0)),
            ],
            out_specs=pl.BlockSpec((1, ROWS, WIDTH), lambda i, s: (i, 0, 0)),
        ),
        out_shape=jax.ShapeDtypeStruct(grads.shape, BF),
        name="weight_step",
    )(source, grads, states)


def moment_step_kernel(from_ref, live_ref, grad_ref, first_ref, second_ref, one_ref, two_ref):
    live = live_ref[pl.program_id(0)] > 0
    grad = jnp.where(live, grad_ref[0].astype(F32), 0.0)
    one_ref[0] = FIRST_DECAY * first_ref[0] + (1.0 - FIRST_DECAY) * grad
    two_ref[0] = SECOND_DECAY * second_ref[0] + (1.0 - SECOND_DECAY) * grad * grad


def moment_step(source, live, grads, first, second):
    slot = pl.BlockSpec((1, ROWS, WIDTH), lambda i, s, n: (i, 0, 0))
    shape = jax.ShapeDtypeStruct(first.shape, F32)
    return pl.pallas_call(
        moment_step_kernel,
        grid_spec=pltpu.PrefetchScalarGridSpec(
            num_scalar_prefetch=2,
            grid=(first.shape[0],),
            in_specs=[
                pl.BlockSpec((1, ROWS, WIDTH), lambda i, s, n: (s[i], 0, 0)),
                slot,
                slot,
            ],
            out_specs=[slot, slot],
        ),
        out_shape=[shape, shape],
        name="moment_step",
    )(source, live, grads, first, second)


def take_kernel(from_ref, in_ref, out_ref):
    out_ref[0] = in_ref[0].astype(F32)


def take_blocks(source, blocks):
    count = source.shape[0]
    return pl.pallas_call(
        take_kernel,
        grid_spec=pltpu.PrefetchScalarGridSpec(
            num_scalar_prefetch=1,
            grid=(count,),
            in_specs=[pl.BlockSpec((1, ROWS, WIDTH), lambda i, s: (s[i], 0, 0))],
            out_specs=pl.BlockSpec((1, ROWS, WIDTH), lambda i, s: (i, 0, 0)),
        ),
        out_shape=jax.ShapeDtypeStruct((count, ROWS, WIDTH), F32),
        name="take_blocks",
    )(source, blocks)


def local(
    groups,
    tokens,
    masked_pos,
    masked_count,
    out_grad,
    weights,
    vectors,
    owner_list,
    master_slots,
    first_slots,
    second_slots,
    vector_first,
    vector_second,
):
    pages = masked_pos.shape[0]
    capacity = master_slots.shape[0]
    held = weights.shape[0] // ROWS
    spread = lax.axis_size("fsdp")
    me_f = lax.axis_index("fsdp")
    ids = groups * spread
    each = NBLK // ids
    lanes = -(-capacity // ids)
    base = lax.axis_index("dp") * spread if groups > 1 else 0
    me = base + me_f

    blocks = jnp.arange(NBLK, dtype=jnp.int32)
    lower = owner_list[None, :] < owner_list[:, None]
    tied = (owner_list[None, :] == owner_list[:, None]) & (blocks[None, :] < blocks[:, None])
    rank = jnp.sum((lower | tied).astype(jnp.int32), axis=1)
    place = (rank % ids) * each + rank // ids
    owners = jnp.arange(spread, dtype=jnp.int32)
    start = jnp.sum((owner_list[None, :] < owners[:, None]).astype(jnp.int32), axis=1)
    count = jnp.sum((owner_list[None, :] == owners[:, None]).astype(jnp.int32), axis=1)
    turn = jnp.arange(lanes, dtype=jnp.int32) * ids

    my_start, my_count = start[me_f], count[me_f]
    slot_to = ((base + owners - my_start) % ids)[:, None] + turn[None, :]
    slot_to = jnp.minimum(slot_to, capacity - 1).reshape(-1)
    slot_at = ((me - start) % ids)[:, None] + turn[None, :]
    send_to = jnp.clip((start[:, None] + slot_at) // ids, 0, each - 1).reshape(-1)
    my_rank = me + ids * jnp.arange(each, dtype=jnp.int32)
    my_owner = jnp.sum((start + count)[None, :] <= my_rank[:, None], axis=1).astype(jnp.int32)
    my_lane = (my_rank - start[my_owner]) // ids
    state_at = my_owner * lanes + my_lane
    slots = jnp.arange(capacity, dtype=jnp.int32)
    grad_at = ((my_start + slots) % ids) * lanes + slots // ids
    grad_live = (slots < my_count).astype(jnp.int32)
    held_at = lax.dynamic_slice(place, (me_f * held,), (held,))

    states = jnp.stack(
        [
            jnp.take(master_slots, slot_to, axis=0).astype(BF),
            jnp.take(first_slots, slot_to, axis=0).astype(BF),
            jnp.take(second_slots, slot_to, axis=0).astype(BF),
        ],
        axis=1,
    )
    states = lax.all_to_all(states, "fsdp", 0, 0, tiled=True)

    live = jnp.arange(MASKM, dtype=jnp.int32)[None, :] < masked_count[:, None]
    pos = jnp.pad(
        jnp.where(live, masked_pos, -1), ((0, 0), (0, PAD - MASKM)), constant_values=-1
    )[:, :, None]
    cot = jnp.pad(
        jnp.where(live[:, :, None], out_grad, jnp.zeros((), BF)), ((0, 0), (0, PAD - MASKM), (0, 0))
    ).reshape(pages * PAD, WIDTH)

    stack = lax.all_gather(weights, "fsdp", axis=0, tiled=True)
    q, k, v, tm, qm, cm = project(tokens, pos, vectors, stack)
    gr, gc, gv, dw = masked_part(place, tm, cm, cot, vectors, stack)
    dq, dk, dv, gv_attn, dw = attention_back(place, tokens, k, v, tm, qm, gc, dw)
    grad_vectors = jnp.concatenate([gv_attn[0:2], gv[2:12]], axis=0)
    if groups > 1:
        mine = lax.psum_scatter(dw, ("dp", "fsdp"), scatter_dimension=0, tiled=True)
    else:
        mine = lax.psum(lax.psum_scatter(dw, "fsdp", scatter_dimension=0, tiled=True), "dp")
    layer_out = forward_rest(tokens, q, k, v, vectors, stack)
    token_grad = input_grad(pos, dq, dk, dv, gr, stack)
    grad_vectors = jnp.sum(lax.all_gather(grad_vectors, ("dp", "fsdp")), axis=0)

    new_mine = weight_step(state_at, mine, states)
    if groups > 1:
        new_all = lax.all_gather(new_mine, ("dp", "fsdp"), axis=0, tiled=True)
    else:
        new_all = lax.all_gather(new_mine, "fsdp", axis=0, tiled=True)
    owned = lax.all_to_all(jnp.take(mine, send_to, axis=0), "fsdp", 0, 0, tiled=True)
    if groups > 1:
        owned = lax.all_gather(owned, "dp", axis=0, tiled=True)
    new_first, new_second = moment_step(grad_at, grad_live, owned, first_slots, second_slots)
    new_weights = take_blocks(held_at, new_all).reshape(held * ROWS, WIDTH)
    new_vectors, new_vector_first, new_vector_second = adam_step(
        vectors, vector_first, vector_second, grad_vectors, VECTOR_RATE
    )
    return (
        layer_out,
        token_grad,
        new_weights,
        new_first,
        new_second,
        new_vectors,
        new_vector_first,
        new_vector_second,
    )


def solution(mesh):
    dp, fsdp = mesh.shape["dp"], mesh.shape["fsdp"]
    groups = 2 if dp == 2 and NBLK % (2 * fsdp) == 0 else 1
    both = ("dp", "fsdp")
    return jax.shard_map(
        functools.partial(local, groups),
        mesh=mesh,
        in_specs=(
            P(both, None),
            P(both, None),
            P(both),
            P(both, None, None),
            P("fsdp", None),
            P(),
            P(),
            P("fsdp", None, None),
            P("fsdp", None, None),
            P("fsdp", None, None),
            P(),
            P(),
        ),
        out_specs=(
            P(both, None),
            P(both, None),
            P("fsdp", None),
            P("fsdp", None, None),
            P("fsdp", None, None),
            P(),
            P(),
            P(),
        ),
        check_vma=False,
    )
```

```python
import functools

import jax
import jax.numpy as jnp
from jax import lax
from jax.experimental import pallas as pl
from jax.experimental.pallas import tpu as pltpu
from jax.sharding import PartitionSpec as P

WIDTH = 768
HEADS = 12
HD = 64
FF = 3072
PAGE = 512
MASKM = 104
ROWS = 48
STEP = 10
NBLK = 192
PAD = 128
UP_ROWS = FF // WIDTH

QUERY_SCALE = 0.125
NORM_EPSILON = 1e-06
INV_ROOT_TWO = 0.7071067811865476
INV_ROOT_TAU = 0.3989422804014327
FIRST_DECAY = 0.5
SECOND_DECAY = 0.5
LEARN_RATE = 0.05
VECTOR_RATE = 0.3
WEIGHT_DECAY = 0.01
ADAM_EPSILON = 1e-08

BF = jnp.bfloat16
F32 = jnp.float32
VMEM_LIMIT = 60 * 1024 * 1024
ANY = pl.BlockSpec(memory_space=pl.ANY)


def cost(tflop, mbytes):
    return pl.CostEstimate(
        flops=int(tflop * 1e12), bytes_accessed=int(mbytes * 1e6), transcendentals=0
    )


def mm(a, b):
    return lax.dot_general(a, b, (((1,), (0,)), ((), ())), preferred_element_type=F32)


def mm_last(a, b):
    return lax.dot_general(a, b, (((1,), (1,)), ((), ())), preferred_element_type=F32)


def mm_first(a, b):
    return lax.dot_general(a, b, (((0,), (0,)), ((), ())), preferred_element_type=F32)


def row_sum(x):
    return jnp.sum(x, axis=0, keepdims=True)


def unit_of(x):
    center = x - jnp.mean(x, axis=1, keepdims=True)
    inverse = lax.rsqrt(jnp.mean(center * center, axis=1, keepdims=True) + NORM_EPSILON)
    return center * inverse, inverse


def unit_back(grad_out, gain, unit, inverse):
    grad_unit = grad_out * gain
    centered = grad_unit - jnp.mean(grad_unit, axis=1, keepdims=True)
    return inverse * (centered - unit * jnp.mean(grad_unit * unit, axis=1, keepdims=True))


def gelu_cdf(u):
    return 0.5 * (1.0 + lax.erf(u * INV_ROOT_TWO))


def half_masks():
    lane = lax.broadcasted_iota(jnp.int32, (1, 2 * HD), 1)
    low = jnp.where(lane < HD, 1.0, 0.0)
    return (low.astype(BF), (1.0 - low).astype(BF)), lane < HD


def softmax(scores):
    top = jnp.max(scores, axis=1, keepdims=True)
    exponent = jnp.exp(scores - top)
    total = jnp.sum(exponent, axis=1, keepdims=True)
    return exponent * (1.0 / total)


def one_hot_rows(pos):
    return jnp.where(
        pos == lax.broadcasted_iota(jnp.int32, (PAD, PAGE), 1), 1.0, 0.0
    ).astype(BF)


def project_kernel(
    pos_ref, tok_ref, vec_ref, w_any, q_ref, k_ref, v_ref, tm_ref, qm_ref, cm_ref, w_ref, sem
):
    @pl.when(pl.program_id(0) == 0)
    def _():
        copy = pltpu.make_async_copy(w_any.at[pl.ds(0, 3 * WIDTH)], w_ref, sem)
        copy.start()
        copy.wait()

    tok = tok_ref[...]
    q = ((mm(tok, w_ref[0:WIDTH]) + vec_ref[0:1]) * QUERY_SCALE).astype(BF)
    k = mm(tok, w_ref[WIDTH : 2 * WIDTH]).astype(BF)
    v = (mm(tok, w_ref[2 * WIDTH : 3 * WIDTH]) + vec_ref[1:2]).astype(BF)
    q_ref[...] = q
    k_ref[...] = k
    v_ref[...] = v
    pick = one_hot_rows(pos_ref[0])
    tm_ref[...] = mm(pick, tok).astype(BF)
    qm = mm(pick, q).astype(BF)
    qm_ref[...] = qm
    masks, low = half_masks()
    for pair in range(HEADS // 2):
        cols = slice(pair * 2 * HD, (pair + 1) * 2 * HD)
        kp, vp, qp = k[:, cols], v[:, cols], qm[:, cols]
        parts = []
        for mask in masks:
            prob = softmax(mm_last(qp * mask, kp)).astype(BF)
            parts.append(mm(prob, vp))
        cm_ref[:, cols] = jnp.where(low, parts[0], parts[1]).astype(BF)


def project(tokens, pos, vectors, stack):
    pages = tokens.shape[0] // PAGE
    tall = jax.ShapeDtypeStruct((pages * PAGE, WIDTH), BF)
    short = jax.ShapeDtypeStruct((pages * PAD, WIDTH), BF)
    page = pl.BlockSpec((PAGE, WIDTH), lambda i: (i, 0))
    few = pl.BlockSpec((PAD, WIDTH), lambda i: (i, 0))
    return pl.pallas_call(
        project_kernel,
        grid=(pages,),
        in_specs=[
            pl.BlockSpec((1, PAD, 1), lambda i: (i, 0, 0)),
            page,
            pl.BlockSpec((12, WIDTH), lambda i: (0, 0)),
            ANY,
        ],
        out_specs=[page, page, page, few, few, few],
        out_shape=[tall, tall, tall, short, short, short],
        scratch_shapes=[pltpu.VMEM((3 * WIDTH, WIDTH), BF), pltpu.SemaphoreType.DMA],
        compiler_params=pltpu.CompilerParams(vmem_limit_bytes=VMEM_LIMIT),
        cost_estimate=cost(0.018, 20),
        name="project",
    )(pos, tokens, vectors, stack)


def masked_kernel(
    place_ref,
    tm_ref,
    cm_ref,
    cot_ref,
    vec_ref,
    w_any,
    gr_ref,
    gc_ref,
    gv_ref,
    dw_any,
    w_ref,
    up_ref,
    act_ref,
    hid_ref,
    stage_ref,
    in_sem,
    out_sem,
):
    parts = 1 + 2 * UP_ROWS
    loads = [
        pltpu.make_async_copy(
            w_any.at[pl.ds((3 + i) * WIDTH, WIDTH)], w_ref.at[i], in_sem.at[i]
        )
        for i in range(parts)
    ]
    for load in loads:
        load.start()
    per = WIDTH // ROWS

    def send(part, value):
        stage_ref[pl.ds(part * per, per)] = value.astype(BF).reshape(per, ROWS, WIDTH)

        @pl.loop(0, per)
        def _(i):
            block = part * per + i
            pltpu.make_async_copy(
                stage_ref.at[block], dw_any.at[place_ref[3 * per + block]], out_sem
            ).start()

    gain_one, shift_one = vec_ref[8:9], vec_ref[9:10]
    gain_two = vec_ref[10:11]
    cm = cm_ref[...]
    loads[0].wait()
    resid_one = tm_ref[...].astype(F32) + mm(cm, w_ref[0]) + vec_ref[2:3]
    unit_one, inv_one = unit_of(resid_one)
    hidden_one = unit_one * gain_one + shift_one
    hid_ref[...] = hidden_one.astype(BF)
    hid = hid_ref[...]
    for c in range(UP_ROWS):
        cols = slice(c * WIDTH, (c + 1) * WIDTH)
        loads[1 + c].wait()
        up = mm_last(hid, w_ref[1 + c]) + vec_ref[3 + c : 4 + c]
        up_ref[:, cols] = up
        act_ref[:, cols] = (up * gelu_cdf(up)).astype(BF)
    resid_two = hidden_one + vec_ref[7:8]
    for c in range(UP_ROWS):
        cols = slice(c * WIDTH, (c + 1) * WIDTH)
        loads[1 + UP_ROWS + c].wait()
        resid_two = resid_two + mm(act_ref[:, cols], w_ref[1 + UP_ROWS + c])
    unit_two, inv_two = unit_of(resid_two)
    cot = cot_ref[...].astype(F32)
    grad_two = unit_back(cot, gain_two, unit_two, inv_two)
    gv_ref[...] = jnp.zeros_like(gv_ref)
    gv_ref[10:11] = row_sum(cot * unit_two)
    gv_ref[11:12] = row_sum(cot)
    down = grad_two.astype(BF)
    gv_ref[7:8] = row_sum(down.astype(F32))
    grad_hidden = grad_two
    for c in range(UP_ROWS):
        cols = slice(c * WIDTH, (c + 1) * WIDTH)
        send(1 + UP_ROWS + c, mm_first(act_ref[:, cols], down))
        up = up_ref[:, cols]
        slope = gelu_cdf(up) + up * jnp.exp(-0.5 * up * up) * INV_ROOT_TAU
        grad_up = (mm_last(down, w_ref[1 + UP_ROWS + c]) * slope).astype(BF)
        gv_ref[3 + c : 4 + c] = row_sum(grad_up.astype(F32))
        send(1 + c, mm_first(grad_up, hid))
        grad_hidden = grad_hidden + mm(grad_up, w_ref[1 + c])
    gv_ref[8:9] = row_sum(grad_hidden * unit_one)
    gv_ref[9:10] = row_sum(grad_hidden)
    grad_one = unit_back(grad_hidden, gain_one, unit_one, inv_one)
    gr_ref[...] = grad_one
    attn = grad_one.astype(BF)
    gv_ref[2:3] = row_sum(attn.astype(F32))
    send(0, mm_first(cm, attn))
    gc_ref[...] = mm_last(attn, w_ref[0]).astype(BF)
    total = parts * per
    pltpu.make_async_copy(stage_ref, dw_any.at[pl.ds(0, total)], out_sem).wait()


def masked_part(place, tm, cm, cot, vectors, stack):
    rows = tm.shape[0]
    parts = 1 + 2 * UP_ROWS
    vm = pl.BlockSpec(memory_space=pltpu.VMEM)
    return pl.pallas_call(
        masked_kernel,
        grid_spec=pltpu.PrefetchScalarGridSpec(
            num_scalar_prefetch=1,
            grid=(),
            in_specs=[vm, vm, vm, vm, ANY],
            out_specs=[vm, vm, vm, ANY],
            scratch_shapes=[
                pltpu.VMEM((parts, WIDTH, WIDTH), BF),
                pltpu.VMEM((rows, FF), F32),
                pltpu.VMEM((rows, FF), BF),
                pltpu.VMEM((rows, WIDTH), BF),
                pltpu.VMEM((parts * WIDTH // ROWS, ROWS, WIDTH), BF),
                pltpu.SemaphoreType.DMA((parts,)),
                pltpu.SemaphoreType.DMA,
            ],
        ),
        out_shape=[
            jax.ShapeDtypeStruct((rows, WIDTH), F32),
            jax.ShapeDtypeStruct((rows, WIDTH), BF),
            jax.ShapeDtypeStruct((16, WIDTH), F32),
            jax.ShapeDtypeStruct((NBLK, ROWS, WIDTH), BF),
        ],
        compiler_params=pltpu.CompilerParams(vmem_limit_bytes=VMEM_LIMIT),
        cost_estimate=cost(0.024, 30),
        name="masked",
    )(place, tm, cm, cot, vectors, stack)


def attention_back_kernel(
    place_ref,
    tok_ref,
    k_ref,
    v_ref,
    tm_ref,
    qm_ref,
    gc_ref,
    dw_in,
    dq_ref,
    dk_ref,
    dv_ref,
    gv_ref,
    dw_any,
    sum_ref,
    stage_ref,
    out_sem,
):
    page, last = pl.program_id(0), pl.num_programs(0) - 1
    per = WIDTH // ROWS
    masks, low = half_masks()

    @pl.when(page == 0)
    def _():
        sum_ref[...] = jnp.zeros_like(sum_ref)
        gv_ref[...] = jnp.zeros_like(gv_ref)

    for pair in range(HEADS // 2):
        cols = slice(pair * 2 * HD, (pair + 1) * 2 * HD)
        kp, vp, qp, gp = k_ref[:, cols], v_ref[:, cols], qm_ref[:, cols], gc_ref[:, cols]
        grad_v, grad_k, grad_q = None, None, []
        for mask in masks:
            qh, gh = qp * mask, gp * mask
            prob = softmax(mm_last(qh, kp))
            grad_prob = mm_last(gh, vp)
            spread = jnp.sum(prob * grad_prob, axis=1, keepdims=True)
            grad_s = (prob * (grad_prob - spread)).astype(BF)
            one_v = mm_first(prob.astype(BF), gh)
            one_k = mm_first(grad_s, qh)
            grad_v = one_v if grad_v is None else grad_v + one_v
            grad_k = one_k if grad_k is None else grad_k + one_k
            grad_q.append(mm(grad_s, kp))
        dv_ref[:, cols] = grad_v.astype(BF)
        dk_ref[:, cols] = grad_k.astype(BF)
        dq_ref[:, cols] = jnp.where(low, grad_q[0], grad_q[1]).astype(BF) * QUERY_SCALE
    dq, dk, dv = dq_ref[...], dk_ref[...], dv_ref[...]
    gv_ref[0:1] += row_sum(dq.astype(F32))
    gv_ref[1:2] += row_sum(dv.astype(F32))
    tok = tok_ref[...]
    sum_ref[0] += mm_first(tm_ref[...], dq)
    sum_ref[1] += mm_first(tok, dk)
    sum_ref[2] += mm_first(tok, dv)

    @pl.when(page == last)
    def _():
        for i in range(3):
            stage_ref[pl.ds(i * per, per)] = (
                sum_ref[i].astype(BF).reshape(per, ROWS, WIDTH)
            )

        @pl.loop(0, 3 * per)
        def _(i):
            pltpu.make_async_copy(
                stage_ref.at[i], dw_any.at[place_ref[i]], out_sem
            ).start()

        pltpu.make_async_copy(stage_ref, dw_any.at[pl.ds(0, 3 * per)], out_sem).wait()


def attention_back(place, tokens, k, v, tm, qm, gc, dw):
    pages = tokens.shape[0] // PAGE
    page = pl.BlockSpec((PAGE, WIDTH), lambda i, s: (i, 0))
    few = pl.BlockSpec((PAD, WIDTH), lambda i, s: (i, 0))
    tall = jax.ShapeDtypeStruct((pages * PAGE, WIDTH), BF)
    return pl.pallas_call(
        attention_back_kernel,
        grid_spec=pltpu.PrefetchScalarGridSpec(
            num_scalar_prefetch=1,
            grid=(pages,),
            in_specs=[page, page, page, few, few, few, ANY],
            out_specs=[few, page, page, pl.BlockSpec((8, WIDTH), lambda i, s: (0, 0)), ANY],
            scratch_shapes=[
                pltpu.VMEM((3, WIDTH, WIDTH), F32),
                pltpu.VMEM((3 * WIDTH // ROWS, ROWS, WIDTH), BF),
                pltpu.SemaphoreType.DMA,
            ],
        ),
        out_shape=[
            jax.ShapeDtypeStruct((pages * PAD, WIDTH), BF),
            tall,
            tall,
            jax.ShapeDtypeStruct((8, WIDTH), F32),
            jax.ShapeDtypeStruct(dw.shape, BF),
        ],
        input_output_aliases={7: 4},
        compiler_params=pltpu.CompilerParams(vmem_limit_bytes=VMEM_LIMIT),
        cost_estimate=cost(0.025, 30),
        name="attention_back",
    )(place, tokens, k, v, tm, qm, gc, dw)


def forward_kernel(tok_ref, q_ref, k_ref, v_ref, vec_ref, w_any, out_ref, w_ref, ctx_ref, sem):
    parts = 1 + 2 * UP_ROWS

    @pl.when(pl.program_id(0) == 0)
    def _():
        pltpu.make_async_copy(w_any.at[pl.ds(3 * WIDTH, parts * WIDTH)], w_ref, sem).start()

    masks, low = half_masks()
    for pair in range(HEADS // 2):
        cols = slice(pair * 2 * HD, (pair + 1) * 2 * HD)
        kp, vp, qp = k_ref[:, cols], v_ref[:, cols], q_ref[:, cols]
        halves = []
        for mask in masks:
            prob = softmax(mm_last(qp * mask, kp)).astype(BF)
            halves.append(mm(prob, vp))
        ctx_ref[:, cols] = jnp.where(low, halves[0], halves[1]).astype(BF)

    @pl.when(pl.program_id(0) == 0)
    def _():
        pltpu.make_async_copy(w_any.at[pl.ds(3 * WIDTH, parts * WIDTH)], w_ref, sem).wait()

    resid_one = tok_ref[...].astype(F32) + mm(ctx_ref[...], w_ref[0:WIDTH]) + vec_ref[2:3]
    unit_one, _ = unit_of(resid_one)
    hidden_one = unit_one * vec_ref[8:9] + vec_ref[9:10]
    hid = hidden_one.astype(BF)
    resid_two = hidden_one + vec_ref[7:8]
    for c in range(UP_ROWS):
        at, to = (1 + c) * WIDTH, (1 + UP_ROWS + c) * WIDTH
        up = mm_last(hid, w_ref[at : at + WIDTH]) + vec_ref[3 + c : 4 + c]
        act = (up * gelu_cdf(up)).astype(BF)
        resid_two = resid_two + mm(act, w_ref[to : to + WIDTH])
    unit_two, _ = unit_of(resid_two)
    out_ref[...] = (unit_two * vec_ref[10:11] + vec_ref[11:12]).astype(BF)


def forward_rest(tokens, q, k, v, vectors, stack):
    pages = tokens.shape[0] // PAGE
    page = pl.BlockSpec((PAGE, WIDTH), lambda i: (i, 0))
    return pl.pallas_call(
        forward_kernel,
        grid=(pages,),
        in_specs=[page, page, page, page, pl.BlockSpec((12, WIDTH), lambda i: (0, 0)), ANY],
        out_specs=page,
        out_shape=jax.ShapeDtypeStruct(tokens.shape, BF),
        scratch_shapes=[
            pltpu.VMEM(((1 + 2 * UP_ROWS) * WIDTH, WIDTH), BF),
            pltpu.VMEM((PAGE, WIDTH), BF),
            pltpu.SemaphoreType.DMA,
        ],
        compiler_params=pltpu.CompilerParams(vmem_limit_bytes=VMEM_LIMIT),
        cost_estimate=cost(0.036, 30),
        name="forward_rest",
    )(tokens, q, k, v, vectors, stack)


def input_grad_kernel(pos_ref, dq_ref, dk_ref, dv_ref, gr_ref, w_any, out_ref, w_ref, sem):
    @pl.when(pl.program_id(0) == 0)
    def _():
        copy = pltpu.make_async_copy(w_any.at[pl.ds(0, 3 * WIDTH)], w_ref, sem)
        copy.start()
        copy.wait()

    few = gr_ref[...] + mm_last(dq_ref[...], w_ref[0:WIDTH])
    high = few.astype(BF)
    rest = (few - high.astype(F32)).astype(BF)
    pick = one_hot_rows(pos_ref[0])
    out_ref[...] = (
        mm_last(dk_ref[...], w_ref[WIDTH : 2 * WIDTH])
        + mm_last(dv_ref[...], w_ref[2 * WIDTH : 3 * WIDTH])
        + (mm_first(pick, high) + mm_first(pick, rest))
    )


def input_grad(pos, dq, dk, dv, gr, stack):
    pages = dk.shape[0] // PAGE
    page = pl.BlockSpec((PAGE, WIDTH), lambda i: (i, 0))
    few = pl.BlockSpec((PAD, WIDTH), lambda i: (i, 0))
    return pl.pallas_call(
        input_grad_kernel,
        grid=(pages,),
        in_specs=[pl.BlockSpec((1, PAD, 1), lambda i: (i, 0, 0)), few, page, page, few, ANY],
        out_specs=page,
        out_shape=jax.ShapeDtypeStruct(dk.shape, F32),
        scratch_shapes=[pltpu.VMEM((3 * WIDTH, WIDTH), BF), pltpu.SemaphoreType.DMA],
        compiler_params=pltpu.CompilerParams(vmem_limit_bytes=VMEM_LIMIT),
        cost_estimate=cost(0.010, 20),
        name="input_grad",
    )(pos, dq, dk, dv, gr, stack)


def adam_step(parameter, moment_one, moment_two, gradient, rate):
    moment_one = FIRST_DECAY * moment_one + (1.0 - FIRST_DECAY) * gradient
    moment_two = SECOND_DECAY * moment_two + (1.0 - SECOND_DECAY) * gradient * gradient
    ascent = (
        moment_one
        / (1.0 - FIRST_DECAY**STEP)
        / (jnp.sqrt(moment_two / (1.0 - SECOND_DECAY**STEP)) + ADAM_EPSILON)
    )
    return (parameter - rate * (ascent + WEIGHT_DECAY * parameter), moment_one, moment_two)


def all_sum(x):
    for axis in ("fsdp", "dp"):
        size, step = lax.axis_size(axis), 1
        while step < size:
            x = x + lax.ppermute(x, axis, [(i, i ^ step) for i in range(size)])
            step *= 2
    return x


def weight_step_kernel(from_ref, grad_ref, state_ref, out_ref):
    new, _, _ = adam_step(
        state_ref[0, 0].astype(F32),
        state_ref[0, 1].astype(F32),
        state_ref[0, 2].astype(F32),
        grad_ref[0].astype(F32),
        LEARN_RATE,
    )
    out_ref[0] = new.astype(BF)


def weight_step(source, grads, states):
    return pl.pallas_call(
        weight_step_kernel,
        grid_spec=pltpu.PrefetchScalarGridSpec(
            num_scalar_prefetch=1,
            grid=(grads.shape[0],),
            in_specs=[
                pl.BlockSpec((1, ROWS, WIDTH), lambda i, s: (i, 0, 0)),
                pl.BlockSpec((1, 3, ROWS, WIDTH), lambda i, s: (s[i], 0, 0, 0)),
            ],
            out_specs=pl.BlockSpec((1, ROWS, WIDTH), lambda i, s: (i, 0, 0)),
        ),
        out_shape=jax.ShapeDtypeStruct(grads.shape, BF),
        cost_estimate=cost(0.0, 2),
        name="weight_step",
    )(source, grads, states)


def moment_step_kernel(
    from_ref, live_ref, grad_ref, other_ref, first_ref, second_ref, one_ref, two_ref
):
    live = live_ref[pl.program_id(0)]
    grad = jnp.where(
        live == 1,
        grad_ref[0].astype(F32),
        jnp.where(live == 2, other_ref[0].astype(F32), 0.0),
    )
    one_ref[0] = FIRST_DECAY * first_ref[0] + (1.0 - FIRST_DECAY) * grad
    two_ref[0] = SECOND_DECAY * second_ref[0] + (1.0 - SECOND_DECAY) * grad * grad


def moment_step(source, live, grads, other, first, second):
    slot = pl.BlockSpec((1, ROWS, WIDTH), lambda i, s, n: (i, 0, 0))
    near = pl.BlockSpec((1, ROWS, WIDTH), lambda i, s, n: (s[i], 0, 0))
    shape = jax.ShapeDtypeStruct(first.shape, F32)
    return pl.pallas_call(
        moment_step_kernel,
        grid_spec=pltpu.PrefetchScalarGridSpec(
            num_scalar_prefetch=2,
            grid=(first.shape[0],),
            in_specs=[near, near, slot, slot],
            out_specs=[slot, slot],
        ),
        out_shape=[shape, shape],
        cost_estimate=cost(0.0, 18),
        name="moment_step",
    )(source, live, grads, other, first, second)


def take_kernel(from_ref, in_ref, out_ref):
    out_ref[0] = in_ref[0].astype(F32)


def take_blocks(source, blocks):
    count = source.shape[0]
    return pl.pallas_call(
        take_kernel,
        grid_spec=pltpu.PrefetchScalarGridSpec(
            num_scalar_prefetch=1,
            grid=(count,),
            in_specs=[pl.BlockSpec((1, ROWS, WIDTH), lambda i, s: (s[i], 0, 0))],
            out_specs=pl.BlockSpec((1, ROWS, WIDTH), lambda i, s: (i, 0, 0)),
        ),
        out_shape=jax.ShapeDtypeStruct((count, ROWS, WIDTH), F32),
        cost_estimate=cost(0.0, 3),
        name="take_blocks",
    )(source, blocks)


def local(
    groups,
    tokens,
    masked_pos,
    masked_count,
    out_grad,
    weights,
    vectors,
    owner_list,
    master_slots,
    first_slots,
    second_slots,
    vector_first,
    vector_second,
):
    pages = masked_pos.shape[0]
    capacity = master_slots.shape[0]
    held = weights.shape[0] // ROWS
    spread = lax.axis_size("fsdp")
    me_f = lax.axis_index("fsdp")
    ids = groups * spread
    each = NBLK // ids
    lanes = -(-capacity // ids)
    base = lax.axis_index("dp") * spread if groups > 1 else 0
    me = base + me_f

    blocks = jnp.arange(NBLK, dtype=jnp.int32)
    lower = owner_list[None, :] < owner_list[:, None]
    tied = (owner_list[None, :] == owner_list[:, None]) & (blocks[None, :] < blocks[:, None])
    rank = jnp.sum((lower | tied).astype(jnp.int32), axis=1)
    place = (rank % ids) * each + rank // ids
    owners = jnp.arange(spread, dtype=jnp.int32)
    start = jnp.sum((owner_list[None, :] < owners[:, None]).astype(jnp.int32), axis=1)
    count = jnp.sum((owner_list[None, :] == owners[:, None]).astype(jnp.int32), axis=1)
    turn = jnp.arange(lanes, dtype=jnp.int32) * ids

    my_start, my_count = start[me_f], count[me_f]
    slot_to = ((base + owners - my_start) % ids)[:, None] + turn[None, :]
    slot_to = jnp.minimum(slot_to, capacity - 1).reshape(-1)
    slot_at = ((me - start) % ids)[:, None] + turn[None, :]
    send_to = jnp.clip((start[:, None] + slot_at) // ids, 0, each - 1).reshape(-1)
    my_rank = me + ids * jnp.arange(each, dtype=jnp.int32)
    my_owner = jnp.sum((start + count)[None, :] <= my_rank[:, None], axis=1).astype(jnp.int32)
    my_lane = (my_rank - start[my_owner]) // ids
    state_at = my_owner * lanes + my_lane
    slots = jnp.arange(capacity, dtype=jnp.int32)
    slot_id = (my_start + slots) % ids
    grad_at = (slot_id % spread) * lanes + slots // ids
    grad_live = (slots < my_count).astype(jnp.int32) * (1 + (slot_id // spread != base // spread))
    held_at = lax.dynamic_slice(place, (me_f * held,), (held,))

    states = jnp.stack(
        [
            jnp.take(master_slots, slot_to, axis=0, mode="clip").astype(BF),
            jnp.take(first_slots, slot_to, axis=0, mode="clip").astype(BF),
            jnp.take(second_slots, slot_to, axis=0, mode="clip").astype(BF),
        ],
        axis=1,
    )
    states = lax.all_to_all(states, "fsdp", 0, 0, tiled=True)
    states, tokens = lax.optimization_barrier((states, tokens))

    live = jnp.arange(MASKM, dtype=jnp.int32)[None, :] < masked_count[:, None]
    pos = jnp.pad(
        jnp.where(live, masked_pos, -1), ((0, 0), (0, PAD - MASKM)), constant_values=-1
    )[:, :, None]
    cot = jnp.pad(
        jnp.where(live[:, :, None], out_grad, jnp.zeros((), BF)), ((0, 0), (0, PAD - MASKM), (0, 0))
    ).reshape(pages * PAD, WIDTH)

    stack = lax.all_gather(weights, "fsdp", axis=0, tiled=True)
    q, k, v, tm, qm, cm = project(tokens, pos, vectors, stack)
    gr, gc, gv, dw = masked_part(place, tm, cm, cot, vectors, stack)
    dq, dk, dv, gv_attn, dw = attention_back(place, tokens, k, v, tm, qm, gc, dw)
    grad_vectors = jnp.concatenate([gv_attn[0:2], gv[2:12]], axis=0)
    if groups > 1:
        mine = lax.psum_scatter(dw, ("dp", "fsdp"), scatter_dimension=0, tiled=True)
    else:
        mine = lax.psum(lax.psum_scatter(dw, "fsdp", scatter_dimension=0, tiled=True), "dp")
    layer_out = forward_rest(tokens, q, k, v, vectors, stack)
    token_grad = input_grad(pos, dq, dk, dv, gr, stack)
    grad_vectors = all_sum(grad_vectors)
    mine, layer_out, token_grad, grad_vectors = lax.optimization_barrier(
        (mine, layer_out, token_grad, grad_vectors)
    )

    new_mine = weight_step(state_at, mine, states)
    if groups > 1:
        new_all = lax.all_gather(new_mine, ("dp", "fsdp"), axis=0, tiled=True)
    else:
        new_all = lax.all_gather(new_mine, "fsdp", axis=0, tiled=True)
    owned = lax.all_to_all(jnp.take(mine, send_to, axis=0, mode="clip"), "fsdp", 0, 0, tiled=True)
    other = lax.ppermute(owned, "dp", [(0, 1), (1, 0)]) if groups > 1 else owned
    new_first, new_second = moment_step(
        grad_at, grad_live, owned, other, first_slots, second_slots
    )
    new_weights = take_blocks(held_at, new_all).reshape(held * ROWS, WIDTH)
    new_vectors, new_vector_first, new_vector_second = adam_step(
        vectors, vector_first, vector_second, grad_vectors, VECTOR_RATE
    )
    return (
        layer_out,
        token_grad,
        new_weights,
        new_first,
        new_second,
        new_vectors,
        new_vector_first,
        new_vector_second,
    )


def solution(mesh):
    dp, fsdp = mesh.shape["dp"], mesh.shape["fsdp"]
    groups = 2 if dp == 2 and NBLK % (2 * fsdp) == 0 else 1
    both = ("dp", "fsdp")
    return jax.shard_map(
        functools.partial(local, groups),
        mesh=mesh,
        in_specs=(
            P(both, None),
            P(both, None),
            P(both),
            P(both, None, None),
            P("fsdp", None),
            P(),
            P(),
            P("fsdp", None, None),
            P("fsdp", None, None),
            P("fsdp", None, None),
            P(),
            P(),
        ),
        out_specs=(
            P(both, None),
            P(both, None),
            P("fsdp", None),
            P("fsdp", None, None),
            P("fsdp", None, None),
            P(),
            P(),
            P(),
        ),
        check_vma=False,
    )
```

```python
import functools

import jax
import jax.numpy as jnp
from jax import lax
from jax.experimental import pallas as pl
from jax.experimental.pallas import tpu as pltpu
from jax.sharding import PartitionSpec as P

WIDTH = 768
HEADS = 12
HD = 64
FF = 3072
PAGE = 512
MASKM = 104
ROWS = 48
STEP = 10
NBLK = 192
PAD = 128
STACK = NBLK * ROWS
UP_ROWS = FF // WIDTH

QUERY_SCALE = 0.125
NORM_EPSILON = 1e-06
INV_ROOT_TWO = 0.7071067811865476
INV_ROOT_TAU = 0.3989422804014327
FIRST_DECAY = 0.5
SECOND_DECAY = 0.5
LEARN_RATE = 0.05
VECTOR_RATE = 0.3
WEIGHT_DECAY = 0.01
ADAM_EPSILON = 1e-08

BF = jnp.bfloat16
F32 = jnp.float32
VMEM_LIMIT = 60 * 1024 * 1024
ANY = pl.BlockSpec(memory_space=pl.ANY)
VM = pl.BlockSpec(memory_space=pltpu.VMEM)


def cost(tflop, mbytes):
    return pl.CostEstimate(
        flops=int(tflop * 1e12), bytes_accessed=int(mbytes * 1e6), transcendentals=0
    )


def mm(a, b):
    return lax.dot_general(a, b, (((1,), (0,)), ((), ())), preferred_element_type=F32)


def mm_last(a, b):
    return lax.dot_general(a, b, (((1,), (1,)), ((), ())), preferred_element_type=F32)


def mm_first(a, b):
    return lax.dot_general(a, b, (((0,), (0,)), ((), ())), preferred_element_type=F32)


def send_blocks(stage_ref, first, count, place_ref, shift, arrays, sem):
    @pl.loop(first, first + count)
    def _(i):
        place, low = place_ref[shift + i], 0
        for array in arrays:
            high = low + array.shape[0]

            @pl.when((place >= low) & (place < high))
            def _(array=array, low=low):
                pltpu.make_async_copy(stage_ref.at[i], array.at[place - low], sem).start()

            low = high


def wait_blocks(stage_ref, first, count, arrays, sem):
    pltpu.make_async_copy(
        stage_ref.at[pl.ds(first, count)], arrays[0].at[pl.ds(0, count)], sem
    ).wait()


def row_sum(x):
    return jnp.sum(x, axis=0, keepdims=True)


def unit_of(x):
    center = x - jnp.mean(x, axis=1, keepdims=True)
    inverse = lax.rsqrt(jnp.mean(center * center, axis=1, keepdims=True) + NORM_EPSILON)
    return center * inverse, inverse


def unit_back(grad_out, gain, unit, inverse):
    grad_unit = grad_out * gain
    centered = grad_unit - jnp.mean(grad_unit, axis=1, keepdims=True)
    return inverse * (centered - unit * jnp.mean(grad_unit * unit, axis=1, keepdims=True))


def gelu_cdf(u):
    return 0.5 * (1.0 + lax.erf(u * INV_ROOT_TWO))


def half_masks():
    lane = lax.broadcasted_iota(jnp.int32, (1, 2 * HD), 1)
    low = jnp.where(lane < HD, 1.0, 0.0)
    return (low.astype(BF), (1.0 - low).astype(BF)), lane < HD


def softmax(scores):
    top = jnp.max(scores, axis=1, keepdims=True)
    exponent = jnp.exp(scores - top)
    total = jnp.sum(exponent, axis=1, keepdims=True)
    return exponent * (1.0 / total)


def one_hot_rows(pos):
    return jnp.where(
        pos == lax.broadcasted_iota(jnp.int32, (PAD, PAGE), 1), 1.0, 0.0
    ).astype(BF)


def project_kernel(counts, rows_ref, pos_ref, tok_ref, vec_ref, *rest):
    pieces, rest = rest[: max(1, len(counts))], rest[max(1, len(counts)) :]
    q_ref, k_ref, v_ref, tm_ref, qm_ref, cm_ref, *stacks, w_ref, sem = rest
    step, last = pl.program_id(0), pl.num_programs(0) - 1

    def cut(first, act):
        at = 0
        for piece, (number, size) in zip(pieces, counts):

            @pl.loop(0, number)
            def _(i, piece=piece, size=size, at=at):
                row = pl.multiple_of(rows_ref[at + i], 16)

                @pl.when((row < 3 * WIDTH) == first)
                def _():
                    source = piece.at[pl.ds(pl.multiple_of(i * size, 16), size)]
                    target = w_ref.at[pl.ds(row, size)]
                    act(pltpu.make_async_copy(source, target, sem.at[1 + at + i]))

            at += number

    @pl.when(step == 0)
    def _():
        if counts:
            cut(True, lambda copy: copy.start())
            cut(False, lambda copy: copy.start())
            cut(True, lambda copy: copy.wait())
        else:
            copy = pltpu.make_async_copy(pieces[0].at[pl.ds(0, 3 * WIDTH)], w_ref, sem.at[0])
            copy.start()
            copy.wait()

    if counts:

        @pl.when(step == 1)
        def _():
            cut(False, lambda copy: copy.wait())
            pltpu.make_async_copy(w_ref, stacks[0], sem.at[0]).start()

    tok = tok_ref[...]
    q = ((mm(tok, w_ref[0:WIDTH]) + vec_ref[0:1]) * QUERY_SCALE).astype(BF)
    k = mm(tok, w_ref[WIDTH : 2 * WIDTH]).astype(BF)
    v = (mm(tok, w_ref[2 * WIDTH : 3 * WIDTH]) + vec_ref[1:2]).astype(BF)
    q_ref[...] = q
    k_ref[...] = k
    v_ref[...] = v
    pick = one_hot_rows(pos_ref[0])
    tm_ref[...] = mm(pick, tok).astype(BF)
    qm = mm(pick, q).astype(BF)
    qm_ref[...] = qm
    masks, low = half_masks()
    for pair in range(HEADS // 2):
        cols = slice(pair * 2 * HD, (pair + 1) * 2 * HD)
        kp, vp, qp = k[:, cols], v[:, cols], qm[:, cols]
        parts = []
        for mask in masks:
            prob = softmax(mm_last(qp * mask, kp)).astype(BF)
            parts.append(mm(prob, vp))
        cm_ref[:, cols] = jnp.where(low, parts[0], parts[1]).astype(BF)

    if counts:

        @pl.when(step == last)
        def _():
            pltpu.make_async_copy(w_ref, stacks[0], sem.at[0]).wait()


def project(tokens, pos, vectors, pieces, rows, counts):
    pages = tokens.shape[0] // PAGE
    tall = jax.ShapeDtypeStruct((pages * PAGE, WIDTH), BF)
    short = jax.ShapeDtypeStruct((pages * PAD, WIDTH), BF)
    page = pl.BlockSpec((PAGE, WIDTH), lambda i, s: (i, 0))
    few = pl.BlockSpec((PAD, WIDTH), lambda i, s: (i, 0))
    stack = [jax.ShapeDtypeStruct((STACK, WIDTH), BF)] if counts else []
    total = sum(number for number, _ in counts)
    return pl.pallas_call(
        functools.partial(project_kernel, counts),
        grid_spec=pltpu.PrefetchScalarGridSpec(
            num_scalar_prefetch=1,
            grid=(pages,),
            in_specs=[
                pl.BlockSpec((1, PAD, 1), lambda i, s: (i, 0, 0)),
                page,
                pl.BlockSpec((12, WIDTH), lambda i, s: (0, 0)),
            ]
            + [ANY] * len(pieces),
            out_specs=[page, page, page, few, few, few] + [ANY] * len(stack),
            scratch_shapes=[
                pltpu.VMEM((STACK if counts else 3 * WIDTH, WIDTH), BF),
                pltpu.SemaphoreType.DMA((1 + total,)),
            ],
        ),
        out_shape=[tall, tall, tall, short, short, short] + stack,
        compiler_params=pltpu.CompilerParams(vmem_limit_bytes=VMEM_LIMIT),
        cost_estimate=cost(0.018, 20),
        name="project",
    )(rows, pos, tokens, vectors, *pieces)


def masked_kernel(
    place_ref,
    tm_ref,
    cm_ref,
    cot_ref,
    vec_ref,
    w_any,
    gr_ref,
    gc_ref,
    gv_ref,
    *rest,
):
    *dws, w_ref, up_ref, act_ref, hid_ref, stage_ref, in_sem, out_sem = rest
    parts = 1 + 2 * UP_ROWS
    loads = [
        pltpu.make_async_copy(
            w_any.at[pl.ds((3 + i) * WIDTH, WIDTH)], w_ref.at[i], in_sem.at[i]
        )
        for i in range(parts)
    ]
    for load in loads:
        load.start()
    per = WIDTH // ROWS

    def send(part, value):
        stage_ref[pl.ds(part * per, per)] = value.astype(BF).reshape(per, ROWS, WIDTH)
        send_blocks(stage_ref, part * per, per, place_ref, 3 * per, dws, out_sem.at[part])

    gain_one, shift_one = vec_ref[8:9], vec_ref[9:10]
    gain_two = vec_ref[10:11]
    cm = cm_ref[...]
    loads[0].wait()
    resid_one = tm_ref[...].astype(F32) + mm(cm, w_ref[0]) + vec_ref[2:3]
    unit_one, inv_one = unit_of(resid_one)
    hidden_one = unit_one * gain_one + shift_one
    hid_ref[...] = hidden_one.astype(BF)
    hid = hid_ref[...]
    for c in range(UP_ROWS):
        cols = slice(c * WIDTH, (c + 1) * WIDTH)
        loads[1 + c].wait()
        up = mm_last(hid, w_ref[1 + c]) + vec_ref[3 + c : 4 + c]
        up_ref[:, cols] = up
        act_ref[:, cols] = (up * gelu_cdf(up)).astype(BF)
    resid_two = hidden_one + vec_ref[7:8]
    for c in range(UP_ROWS):
        cols = slice(c * WIDTH, (c + 1) * WIDTH)
        loads[1 + UP_ROWS + c].wait()
        resid_two = resid_two + mm(act_ref[:, cols], w_ref[1 + UP_ROWS + c])
    unit_two, inv_two = unit_of(resid_two)
    cot = cot_ref[...].astype(F32)
    grad_two = unit_back(cot, gain_two, unit_two, inv_two)
    gv_ref[...] = jnp.zeros_like(gv_ref)
    gv_ref[10:11] = row_sum(cot * unit_two)
    gv_ref[11:12] = row_sum(cot)
    down = grad_two.astype(BF)
    gv_ref[7:8] = row_sum(down.astype(F32))
    grad_hidden = grad_two
    for c in range(UP_ROWS):
        cols = slice(c * WIDTH, (c + 1) * WIDTH)
        send(1 + UP_ROWS + c, mm_first(act_ref[:, cols], down))
        up = up_ref[:, cols]
        slope = gelu_cdf(up) + up * jnp.exp(-0.5 * up * up) * INV_ROOT_TAU
        grad_up = (mm_last(down, w_ref[1 + UP_ROWS + c]) * slope).astype(BF)
        gv_ref[3 + c : 4 + c] = row_sum(grad_up.astype(F32))
        send(1 + c, mm_first(grad_up, hid))
        grad_hidden = grad_hidden + mm(grad_up, w_ref[1 + c])
    gv_ref[8:9] = row_sum(grad_hidden * unit_one)
    gv_ref[9:10] = row_sum(grad_hidden)
    grad_one = unit_back(grad_hidden, gain_one, unit_one, inv_one)
    gr_ref[...] = grad_one
    attn = grad_one.astype(BF)
    gv_ref[2:3] = row_sum(attn.astype(F32))
    send(0, mm_first(cm, attn))
    gc_ref[...] = mm_last(attn, w_ref[0]).astype(BF)
    for part in range(parts):
        wait_blocks(stage_ref, part * per, per, dws, out_sem.at[part])


def masked_part(place, sizes, tm, cm, cot, vectors, stack):
    rows = tm.shape[0]
    parts = 1 + 2 * UP_ROWS
    vm = pl.BlockSpec(memory_space=pltpu.VMEM)
    return pl.pallas_call(
        masked_kernel,
        grid_spec=pltpu.PrefetchScalarGridSpec(
            num_scalar_prefetch=1,
            grid=(),
            in_specs=[vm, vm, vm, vm, ANY],
            out_specs=[vm, vm, vm] + [ANY] * len(sizes),
            scratch_shapes=[
                pltpu.VMEM((parts, WIDTH, WIDTH), BF),
                pltpu.VMEM((rows, FF), F32),
                pltpu.VMEM((rows, FF), BF),
                pltpu.VMEM((rows, WIDTH), BF),
                pltpu.VMEM((parts * WIDTH // ROWS, ROWS, WIDTH), BF),
                pltpu.SemaphoreType.DMA((parts,)),
                pltpu.SemaphoreType.DMA((parts,)),
            ],
        ),
        out_shape=[
            jax.ShapeDtypeStruct((rows, WIDTH), F32),
            jax.ShapeDtypeStruct((rows, WIDTH), BF),
            jax.ShapeDtypeStruct((16, WIDTH), F32),
        ]
        + [jax.ShapeDtypeStruct((size, ROWS, WIDTH), BF) for size in sizes],
        compiler_params=pltpu.CompilerParams(vmem_limit_bytes=VMEM_LIMIT),
        cost_estimate=cost(0.024, 30),
        name="masked",
    )(place, tm, cm, cot, vectors, stack)


def attention_back_kernel(
    place_ref,
    tok_ref,
    k_ref,
    v_ref,
    tm_ref,
    qm_ref,
    gc_ref,
    *rest,
):
    arrays = (len(rest) - 7) // 2
    dq_ref, dk_ref, dv_ref, gv_ref, *dws, sum_ref, stage_ref, out_sem = rest[arrays:]
    page, last = pl.program_id(0), pl.num_programs(0) - 1
    per = WIDTH // ROWS
    masks, low = half_masks()

    @pl.when(page == 0)
    def _():
        sum_ref[...] = jnp.zeros_like(sum_ref)
        gv_ref[...] = jnp.zeros_like(gv_ref)

    for pair in range(HEADS // 2):
        cols = slice(pair * 2 * HD, (pair + 1) * 2 * HD)
        kp, vp, qp, gp = k_ref[:, cols], v_ref[:, cols], qm_ref[:, cols], gc_ref[:, cols]
        grad_v, grad_k, grad_q = None, None, []
        for mask in masks:
            qh, gh = qp * mask, gp * mask
            prob = softmax(mm_last(qh, kp))
            grad_prob = mm_last(gh, vp)
            spread = jnp.sum(prob * grad_prob, axis=1, keepdims=True)
            grad_s = (prob * (grad_prob - spread)).astype(BF)
            one_v = mm_first(prob.astype(BF), gh)
            one_k = mm_first(grad_s, qh)
            grad_v = one_v if grad_v is None else grad_v + one_v
            grad_k = one_k if grad_k is None else grad_k + one_k
            grad_q.append(mm(grad_s, kp))
        dv_ref[:, cols] = grad_v.astype(BF)
        dk_ref[:, cols] = grad_k.astype(BF)
        dq_ref[:, cols] = jnp.where(low, grad_q[0], grad_q[1]).astype(BF) * QUERY_SCALE
    dq, dk, dv = dq_ref[...], dk_ref[...], dv_ref[...]
    gv_ref[0:1] += row_sum(dq.astype(F32))
    gv_ref[1:2] += row_sum(dv.astype(F32))
    tok = tok_ref[...]
    sum_ref[0] += mm_first(tm_ref[...], dq)
    sum_ref[1] += mm_first(tok, dk)
    sum_ref[2] += mm_first(tok, dv)

    @pl.when(page == last)
    def _():
        for i in range(3):
            stage_ref[pl.ds(i * per, per)] = (
                sum_ref[i].astype(BF).reshape(per, ROWS, WIDTH)
            )

            send_blocks(stage_ref, i * per, per, place_ref, 0, dws, out_sem.at[i])
        for i in range(3):
            wait_blocks(stage_ref, i * per, per, dws, out_sem.at[i])


def attention_back(place, tokens, k, v, tm, qm, gc, dws):
    pages = tokens.shape[0] // PAGE
    page = pl.BlockSpec((PAGE, WIDTH), lambda i, s: (i, 0))
    few = pl.BlockSpec((PAD, WIDTH), lambda i, s: (i, 0))
    tall = jax.ShapeDtypeStruct((pages * PAGE, WIDTH), BF)
    return pl.pallas_call(
        attention_back_kernel,
        grid_spec=pltpu.PrefetchScalarGridSpec(
            num_scalar_prefetch=1,
            grid=(pages,),
            in_specs=[page, page, page, few, few, few] + [ANY] * len(dws),
            out_specs=[few, page, page, pl.BlockSpec((8, WIDTH), lambda i, s: (0, 0))]
            + [ANY] * len(dws),
            scratch_shapes=[
                pltpu.VMEM((3, WIDTH, WIDTH), F32),
                pltpu.VMEM((3 * WIDTH // ROWS, ROWS, WIDTH), BF),
                pltpu.SemaphoreType.DMA((3,)),
            ],
        ),
        out_shape=[
            jax.ShapeDtypeStruct((pages * PAD, WIDTH), BF),
            tall,
            tall,
            jax.ShapeDtypeStruct((8, WIDTH), F32),
        ]
        + [jax.ShapeDtypeStruct(dw.shape, BF) for dw in dws],
        input_output_aliases={7 + i: 4 + i for i in range(len(dws))},
        compiler_params=pltpu.CompilerParams(vmem_limit_bytes=VMEM_LIMIT),
        cost_estimate=cost(0.025, 30),
        name="attention_back",
    )(place, tokens, k, v, tm, qm, gc, *dws)


def forward_kernel(tok_ref, q_ref, k_ref, v_ref, vec_ref, w_any, *rest):
    out_ref, w_ref, ctx_ref, sem = rest[-4:]
    parts = 1 + 2 * UP_ROWS
    load = pltpu.make_async_copy(w_any.at[pl.ds(3 * WIDTH, parts * WIDTH)], w_ref, sem)
    load.start()

    masks, low = half_masks()
    for pair in range(HEADS // 2):
        cols = slice(pair * 2 * HD, (pair + 1) * 2 * HD)
        kp, vp, qp = k_ref[:, cols], v_ref[:, cols], q_ref[:, cols]
        halves = []
        for mask in masks:
            prob = softmax(mm_last(qp * mask, kp)).astype(BF)
            halves.append(mm(prob, vp))
        ctx_ref[:, cols] = jnp.where(low, halves[0], halves[1]).astype(BF)

    load.wait()
    resid_one = tok_ref[...].astype(F32) + mm(ctx_ref[...], w_ref[0:WIDTH]) + vec_ref[2:3]
    unit_one, _ = unit_of(resid_one)
    hidden_one = unit_one * vec_ref[8:9] + vec_ref[9:10]
    hid = hidden_one.astype(BF)
    resid_two = hidden_one + vec_ref[7:8]
    for c in range(UP_ROWS):
        at, to = (1 + c) * WIDTH, (1 + UP_ROWS + c) * WIDTH
        up = mm_last(hid, w_ref[at : at + WIDTH]) + vec_ref[3 + c : 4 + c]
        act = (up * gelu_cdf(up)).astype(BF)
        resid_two = resid_two + mm(act, w_ref[to : to + WIDTH])
    unit_two, _ = unit_of(resid_two)
    out_ref[...] = (unit_two * vec_ref[10:11] + vec_ref[11:12]).astype(BF)


def forward_page(index, tokens, q, k, v, vectors, stack, before, *after):
    extra = before + after
    page = pl.BlockSpec((PAGE, WIDTH), lambda i: (index, 0))
    whole = pl.BlockSpec((12, WIDTH), lambda i: (0, 0))
    return pl.pallas_call(
        forward_kernel,
        grid=(1,),
        in_specs=[page, page, page, page, whole, ANY] + [ANY] * len(extra),
        out_specs=page,
        out_shape=jax.ShapeDtypeStruct(tokens.shape, BF),
        scratch_shapes=[
            pltpu.VMEM(((1 + 2 * UP_ROWS) * WIDTH, WIDTH), BF),
            pltpu.VMEM((PAGE, WIDTH), BF),
            pltpu.SemaphoreType.DMA,
        ],
        input_output_aliases={6: 0} if before else {},
        compiler_params=pltpu.CompilerParams(vmem_limit_bytes=VMEM_LIMIT),
        cost_estimate=cost(0.0, 0.001),
        name="forward_page",
    )(tokens, q, k, v, vectors, stack, *extra)


def input_grad_kernel(pos_ref, dq_ref, dk_ref, dv_ref, gr_ref, w_any, *rest):
    out_ref, w_ref, sem = rest[-3:]

    @pl.when(pl.program_id(0) == 0)
    def _():
        copy = pltpu.make_async_copy(w_any.at[pl.ds(0, 3 * WIDTH)], w_ref, sem)
        copy.start()
        copy.wait()

    few = gr_ref[...] + mm_last(dq_ref[...], w_ref[0:WIDTH])
    high = few.astype(BF)
    rest = (few - high.astype(F32)).astype(BF)
    pick = one_hot_rows(pos_ref[0])
    out_ref[...] = (
        mm_last(dk_ref[...], w_ref[WIDTH : 2 * WIDTH])
        + mm_last(dv_ref[...], w_ref[2 * WIDTH : 3 * WIDTH])
        + (mm_first(pick, high) + mm_first(pick, rest))
    )


def input_grad(pos, dq, dk, dv, gr, stack, *after):
    pages = dk.shape[0] // PAGE
    page = pl.BlockSpec((PAGE, WIDTH), lambda i: (i, 0))
    few = pl.BlockSpec((PAD, WIDTH), lambda i: (i, 0))
    return pl.pallas_call(
        input_grad_kernel,
        grid=(pages,),
        in_specs=[pl.BlockSpec((1, PAD, 1), lambda i: (i, 0, 0)), few, page, page, few, ANY]
        + [ANY] * len(after),
        out_specs=page,
        out_shape=jax.ShapeDtypeStruct(dk.shape, F32),
        scratch_shapes=[pltpu.VMEM((3 * WIDTH, WIDTH), BF), pltpu.SemaphoreType.DMA],
        compiler_params=pltpu.CompilerParams(vmem_limit_bytes=VMEM_LIMIT),
        cost_estimate=cost(0.0, 0.001),
        name="input_grad",
    )(pos, dq, dk, dv, gr, stack, *after)


def adam_step(parameter, moment_one, moment_two, gradient, rate):
    moment_one = FIRST_DECAY * moment_one + (1.0 - FIRST_DECAY) * gradient
    moment_two = SECOND_DECAY * moment_two + (1.0 - SECOND_DECAY) * gradient * gradient
    ascent = (
        moment_one
        / (1.0 - FIRST_DECAY**STEP)
        / (jnp.sqrt(moment_two / (1.0 - SECOND_DECAY**STEP)) + ADAM_EPSILON)
    )
    return (parameter - rate * (ascent + WEIGHT_DECAY * parameter), moment_one, moment_two)


ORDER = (2, 1, 3, 0)
SIZES = (96, 24, 48, 24)


def swap_dp(x):
    return lax.ppermute(x, "dp", [(0, 1), (1, 0)])


def swap_y(x):
    return lax.ppermute(x, "fsdp", [(f, f ^ 2) for f in range(16)])


def swap_core(x):
    return lax.ppermute(x, "fsdp", [(f, f ^ 1) for f in range(16)])


def up_z(x, steps):
    return lax.ppermute(x, "fsdp", [(f, (f + 4 * steps) % 16) for f in range(16)])


def apart(group, spot):
    me_d, me_f = lax.axis_index("dp"), lax.axis_index("fsdp")
    steps = (spot // 4 - me_f // 4) % 4
    dy = (spot // 2 % 2 + me_f // 2) % 2
    return steps, (group + me_d) % 2, dy, (spot + me_f) % 2


def relative_place(group, spot, turn):
    steps, dx, dy, core = apart(group, spot)
    half, third = turn // 3, turn % 3
    first = jnp.where(dx == 1, 0, 12) + dy * 3
    second = jnp.where(dy == 1, 6, 18) + dx * 3
    inner = jnp.where(half == 0, first, second) + third
    rank = jnp.where(steps == 2, 0, jnp.where(steps == 0, 3, jnp.where(steps == 1, 1, 2)))
    return core * 96 + rank * 24 + inner


def blocks_spec(shape, first=0):
    return pl.BlockSpec(shape, lambda i: (i + first,) + (0,) * (len(shape) - 1))


def core_sum_kernel(keep_ref, from_ref, *rest):
    for part, out in enumerate(rest[-4:]):
        out[0] = keep_ref[0, part] + from_ref[0, part]


def core_sum(keep, got, first, *after):
    count = got.shape[0] // 24
    whole, six = (1, 4, 6, ROWS, WIDTH), (1, 6, ROWS, WIDTH)
    return pl.pallas_call(
        core_sum_kernel,
        grid=(count,),
        in_specs=[blocks_spec(whole, first), blocks_spec(whole)] + [ANY] * len(after),
        out_specs=[blocks_spec(six)] * 4,
        out_shape=[jax.ShapeDtypeStruct((count,) + six[1:], BF)] * 4,
        compiler_params=pltpu.CompilerParams(vmem_limit_bytes=VMEM_LIMIT),
        cost_estimate=cost(0.0, 0.001),
        name="core_sum",
    )(keep.reshape((4,) + whole[1:]), got.reshape((count,) + whole[1:]), *after)


def first_sum_kernel(a_ref, b_ref, to_a_ref, to_b_ref, *rest):
    keep_a, keep_b, send_a, send_b = rest[-4:]
    half_a, half_b = a_ref[0] + to_a_ref[0], b_ref[0] + to_b_ref[0]
    keep_a[0], keep_b[0], send_a[0], send_b[0] = half_a[:3], half_b[:3], half_a[3:], half_b[3:]


def first_sum(a, b, to_a, to_b, *after, weight=0.001):
    count, six, three = a.shape[0], (1, 6, ROWS, WIDTH), (1, 3, ROWS, WIDTH)
    return pl.pallas_call(
        first_sum_kernel,
        grid=(count,),
        in_specs=[blocks_spec(six)] * 4 + [ANY] * len(after),
        out_specs=[blocks_spec(three)] * 4,
        out_shape=[jax.ShapeDtypeStruct((count,) + three[1:], BF)] * 4,
        compiler_params=pltpu.CompilerParams(vmem_limit_bytes=VMEM_LIMIT),
        cost_estimate=cost(0.0, weight),
        name="first_sum",
    )(a, b, to_a, to_b, *after)


def last_sum_kernel(count, a_ref, b_ref, to_a_ref, to_b_ref, *rest):
    for i, out in enumerate(rest[-count:]):
        out[0:3] = a_ref[i] + to_a_ref[i]
        out[3:6] = b_ref[i] + to_b_ref[i]


def last_sum(a, b, to_a, to_b, *after):
    count = a.shape[0]
    return pl.pallas_call(
        functools.partial(last_sum_kernel, count),
        in_specs=[VM] * 4 + [ANY] * len(after),
        out_specs=[VM] * count,
        out_shape=[jax.ShapeDtypeStruct((6, ROWS, WIDTH), BF)] * count,
        compiler_params=pltpu.CompilerParams(vmem_limit_bytes=VMEM_LIMIT),
        cost_estimate=cost(0.0, 0.001),
        name="last_sum",
    )(a, b, to_a, to_b, *after)


def reduce_blocks(dws, tasks):
    keep = dws[0]
    got = [swap_core(send) for send in dws[1:]]
    xs_far, ys_far, a_far, b_far = core_sum(keep, got[0], 0)
    to_far = swap_dp(xs_far), swap_y(ys_far)
    a_far, b_far, ys_far, xs_far = first_sum(a_far, b_far, *to_far)
    to_far = swap_y(ys_far), swap_dp(xs_far)
    xs_near, ys_near, a_near, b_near = core_sum(keep, got[1], 1, ys_far)
    to_near = swap_dp(xs_near), swap_y(ys_near)
    done = tasks[0](xs_near)
    a_near, b_near, ys_near, xs_near = first_sum(a_near, b_near, *to_near, done)
    to_near = swap_y(ys_near), swap_dp(xs_near)
    (far,) = last_sum(a_far, b_far, *to_far, ys_near)
    xs_own, ys_own, a_own, b_own = core_sum(keep, got[2], 3, far)
    far = up_z(far, 2)
    to_own = swap_dp(xs_own), swap_y(ys_own)
    done = tasks[1](xs_own)
    up, down = last_sum(a_near, b_near, *to_near, done, far)
    near = up_z(up, 1), up_z(down, 3)
    a_own, b_own, ys_own, xs_own = first_sum(a_own, b_own, *to_own, up)
    to_own = swap_y(ys_own), swap_dp(xs_own)
    done = tasks[2](ys_own)
    return (a_own, to_own[0], b_own, to_own[1]), (far,) + near, done


def weight_step_kernel(halves, wholes, *refs):
    half_refs, refs = refs[:halves], refs[halves:]
    whole_refs, refs = refs[:wholes], refs[wholes:]
    state_ref, grad_out, new_out = refs[0], refs[-2], refs[-1]
    for i in range(grad_out.shape[0]):
        parts = [ref[i] for ref in whole_refs]
        if halves:
            first = 2 * (i // 3)
            parts += [ref[0, i % 3] for ref in half_refs[first : first + 2]]
        total = parts[0].astype(F32)
        for part in parts[1:]:
            total = total + part.astype(F32)
        grad = total.astype(BF)
        grad_out[i] = grad
        new, _, _ = adam_step(
            state_ref[i, 0].astype(F32),
            state_ref[i, 1].astype(F32),
            state_ref[i, 2].astype(F32),
            grad.astype(F32),
            LEARN_RATE,
        )
        new_out[i] = new.astype(BF)


def weight_step(halves, wholes, states, *after):
    count = states.shape[0]
    shape = jax.ShapeDtypeStruct((count, ROWS, WIDTH), BF)
    return pl.pallas_call(
        functools.partial(weight_step_kernel, len(halves), len(wholes)),
        in_specs=[VM] * (len(halves) + len(wholes) + 1) + [ANY] * len(after),
        out_specs=[VM] * 2,
        out_shape=[shape, shape],
        compiler_params=pltpu.CompilerParams(vmem_limit_bytes=VMEM_LIMIT),
        cost_estimate=cost(0.0, 0.001),
        name="weight_step",
    )(*halves, *wholes, states, *after)


def moment_step_kernel(info_ref, a_ref, b_ref, first_ref, second_ref, *rest):
    one_ref, two_ref = rest[-2:]
    count = first_ref.shape[0]
    lead, live = info_ref[0] == 0, info_ref[1]
    for i in range(count):
        one, two = a_ref[i // 2].astype(F32), b_ref[i // 2].astype(F32)
        grad = jnp.where(lead if i % 2 == 0 else jnp.logical_not(lead), one, two)
        grad = jnp.where(pl.program_id(0) * count + i < live, grad, 0.0)
        one_ref[i] = FIRST_DECAY * first_ref[i] + (1.0 - FIRST_DECAY) * grad
        two_ref[i] = SECOND_DECAY * second_ref[i] + (1.0 - SECOND_DECAY) * grad * grad


def moment_step(info, a, b, first, second, *after):
    each = 4 if first.shape[0] % 4 == 0 else 2
    grads = pl.BlockSpec((each // 2, ROWS, WIDTH), lambda i, s: (i, 0, 0))
    slots = pl.BlockSpec((each, ROWS, WIDTH), lambda i, s: (i, 0, 0))
    shape = jax.ShapeDtypeStruct(first.shape, F32)
    return pl.pallas_call(
        moment_step_kernel,
        grid_spec=pltpu.PrefetchScalarGridSpec(
            num_scalar_prefetch=1,
            grid=(first.shape[0] // each,),
            in_specs=[grads, grads, slots, slots] + [ANY] * len(after),
            out_specs=[slots, slots],
        ),
        out_shape=[shape, shape],
        compiler_params=pltpu.CompilerParams(vmem_limit_bytes=VMEM_LIMIT),
        cost_estimate=cost(0.0, 0.001),
        name="moment_step",
    )(info, a, b, first, second, *after)


def pick_kernel(sizes, arrays, from_ref, *refs):
    outs, sem = refs[-1 - len(sizes) : -1], refs[-1]
    slot = 0
    for out, size in zip(outs, sizes):

        @pl.loop(0, size)
        def _(i, out=out, slot=slot):
            number, low = from_ref[slot + i], 0
            for array in refs[:arrays]:
                high = low + array.shape[0]

                @pl.when((number >= low) & (number < high))
                def _(array=array, low=low):
                    pltpu.make_async_copy(
                        array.at[number - low], out.at[i], sem.at[slot + i]
                    ).start()

                low = high

        slot += size
    slot = 0
    for out, size in zip(outs, sizes):

        @pl.loop(0, size)
        def _(i, out=out, slot=slot):
            pltpu.make_async_copy(refs[0].at[0], out.at[i], sem.at[slot + i]).wait()

        slot += size


def pick_blocks(source, arrays, sizes, *after):
    arrays = [array.reshape(-1, ROWS, WIDTH) for array in arrays]
    return pl.pallas_call(
        functools.partial(pick_kernel, sizes, len(arrays)),
        grid_spec=pltpu.PrefetchScalarGridSpec(
            num_scalar_prefetch=1,
            grid=(),
            in_specs=[ANY] * (len(arrays) + len(after)),
            out_specs=[VM] * len(sizes),
            scratch_shapes=[pltpu.SemaphoreType.DMA((sum(sizes),))],
        ),
        out_shape=[jax.ShapeDtypeStruct((size, ROWS, WIDTH), BF) for size in sizes],
        compiler_params=pltpu.CompilerParams(vmem_limit_bytes=VMEM_LIMIT),
        cost_estimate=cost(0.0, 0.001),
        name="pick_blocks",
    )(source, *arrays, *after)


def move_kernel(plan, *refs):
    for out, pieces in zip(refs[-len(plan) :], plan):
        at = 0
        for source, low, high in pieces:
            out[at : at + high - low] = refs[source][low:high]
            at += high - low


def move(plan, arrays, *after):
    return pl.pallas_call(
        functools.partial(move_kernel, plan),
        in_specs=[VM] * len(arrays) + [ANY] * len(after),
        out_specs=[VM] * len(plan),
        out_shape=[
            jax.ShapeDtypeStruct((sum(high - low for _, low, high in pieces), ROWS, WIDTH), BF)
            for pieces in plan
        ],
        compiler_params=pltpu.CompilerParams(vmem_limit_bytes=VMEM_LIMIT),
        cost_estimate=cost(0.0, 0.001),
        name="move",
    )(*arrays, *after)


ENDS = (((0, 0, 3),), ((1, 3, 6),))
TWO_ENDS = (((0, 0, 3), (0, 6, 9)), ((1, 3, 6), (1, 9, 12)))


def gather_blocks(mine, tasks):
    up, down = up_z(mine, 1), up_z(mine, 3)
    far = up_z(up, 1)
    own_x, own_y = swap_dp(mine), swap_y(mine)
    done = tasks[0](mine)
    end_x, end_y = move(ENDS, [own_x, own_y], *done)
    own = [mine, own_x, own_y, swap_y(end_x), swap_dp(end_y)]
    (near,) = move((((0, 0, 6), (1, 0, 6)),), [up, down], end_x)
    near_x, near_y = swap_dp(near), swap_y(near)
    done = tasks[1](near)
    done = tasks[2](*done, far)
    far_x, far_y = swap_dp(far), swap_y(far)
    end_x, end_y = move(TWO_ENDS, [near_x, near_y], *done)
    near = [near, near_x, near_y, swap_y(end_x), swap_dp(end_y)]
    end_x, end_y = move(ENDS, [far_x, far_y], end_x)
    far = [far, far_x, far_y, swap_y(end_x), swap_dp(end_y)]
    return own + far + near, end_x


PIECES = ((1, 288), (1, 288), (1, 288), (1, 144), (1, 144))
PIECES += PIECES + tuple((2 * number, rows) for number, rows in PIECES)
PIECES += PIECES


def piece_rows():
    me_d, me_f = lax.axis_index("dp"), lax.axis_index("fsdp")
    rows = []
    for core in (0, 1):
        for steps in ((0,), (2,), (1, 3)):
            for dx, dy, low in ((0, 0, 0), (1, 0, 0), (0, 1, 0), (1, 1, 0), (1, 1, 144)):
                for step in steps:
                    z = (me_f // 4 - step) % 4
                    y, c = (me_f // 2 + dy) % 2, (me_f + core) % 2
                    rows.append((((z * 2 + y) * 2 + c) * 2 + (me_d + dx) % 2) * 288 + low)
    return jnp.stack(rows).astype(jnp.int32)


def gather_stack(weights, early):
    half = weights.shape[0] // 2
    mine = lax.dynamic_slice(weights, (lax.axis_index("dp") * half, 0), (half, WIDTH))
    tasks = [lambda *after: early, lambda *after: after, lambda *after: after]
    arrays, _ = gather_blocks(mine.reshape(-1, ROWS, WIDTH), tasks)
    arrays += [swap_core(array) for array in arrays]
    return [array.reshape(-1, WIDTH) for array in arrays]


def gathered_place(group, spot, turn):
    ahead, dx, dy, core = apart(group, spot)
    steps = (4 - ahead) % 4
    side, pair = dx + 2 * dy, steps // 2
    plain = jnp.where(steps == 2, 24, 0) + side * 6 + turn
    corner = jnp.where(turn < 3, 84 + pair * 3 + turn, 90 + pair * 3 + turn - 3)
    near = jnp.where(side == 3, corner, 48 + side * 12 + pair * 6 + turn)
    steps_odd = steps % 2 == 1
    return jnp.where(steps_odd, near, plain), core == 0


def local(
    groups,
    tokens,
    masked_pos,
    masked_count,
    out_grad,
    weights,
    vectors,
    owner_list,
    master_slots,
    first_slots,
    second_slots,
    vector_first,
    vector_second,
):
    pages = masked_pos.shape[0]
    capacity = master_slots.shape[0]
    held = weights.shape[0] // ROWS
    spread = lax.axis_size("fsdp")
    me_f = lax.axis_index("fsdp")
    ids = groups * spread
    each = NBLK // ids
    lanes = -(-capacity // ids)
    my_group = lax.axis_index("dp") if groups > 1 else 0
    me = me_f * groups + my_group

    blocks = jnp.arange(NBLK, dtype=jnp.int32)
    lower = owner_list[None, :] < owner_list[:, None]
    tied = (owner_list[None, :] == owner_list[:, None]) & (blocks[None, :] < blocks[:, None])
    rank = jnp.sum((lower | tied).astype(jnp.int32), axis=1)
    group, spot, turn = rank % groups, rank % ids // groups, rank // ids
    place = (group * spread + spot) * each + turn
    direct = groups == 2 and spread == 16 and each == 6 and pages == 3
    if direct:
        sizes = SIZES
        put = relative_place(group, spot, turn)
    else:
        sizes, put = (NBLK,), place
    owners = jnp.arange(spread, dtype=jnp.int32)
    start = jnp.sum((owner_list[None, :] < owners[:, None]).astype(jnp.int32), axis=1)
    count = jnp.sum((owner_list[None, :] == owners[:, None]).astype(jnp.int32), axis=1)
    lane = jnp.arange(lanes, dtype=jnp.int32) * ids

    my_start, my_count = start[me_f], count[me_f]
    slot_to = ((owners * groups + my_group - my_start) % ids)[:, None] + lane[None, :]
    slot_to = jnp.minimum(slot_to, capacity - 1).reshape(-1)
    slot_at = ((me - start) % ids)[:, None] + lane[None, :]
    send_to = jnp.clip((start[:, None] + slot_at) // ids, 0, each - 1).reshape(-1)
    my_rank = me + ids * jnp.arange(each, dtype=jnp.int32)
    my_owner = jnp.sum((start + count)[None, :] <= my_rank[:, None], axis=1).astype(jnp.int32)
    my_lane = (my_rank - start[my_owner]) // ids
    state_at = my_owner * lanes + my_lane
    lead = (my_group - my_start) % 2 if groups > 1 else 0
    slots = jnp.arange(capacity // 2, dtype=jnp.int32) * 2

    def grad_at(first):
        which = slots + first
        return ((my_start + which) % ids // groups) * lanes + which // ids

    info = jnp.stack([jnp.asarray(lead, jnp.int32), my_count])

    states = jnp.stack(
        [
            jnp.take(master_slots, slot_to, axis=0, mode="clip").astype(BF),
            jnp.take(first_slots, slot_to, axis=0, mode="clip").astype(BF),
            jnp.take(second_slots, slot_to, axis=0, mode="clip").astype(BF),
        ],
        axis=1,
    )

    live = jnp.arange(MASKM, dtype=jnp.int32)[None, :] < masked_count[:, None]
    pos = jnp.pad(
        jnp.where(live, masked_pos, -1), ((0, 0), (0, PAD - MASKM)), constant_values=-1
    )[:, :, None]
    cot = jnp.pad(
        jnp.where(live[:, :, None], out_grad, jnp.zeros((), BF)), ((0, 0), (0, PAD - MASKM), (0, 0))
    ).reshape(pages * PAD, WIDTH)

    if direct:
        pieces, rows, counts = gather_stack(weights, (states, cot)), piece_rows(), PIECES
        last, states = lax.optimization_barrier((pieces[-1], states))
        pieces = pieces[:-1] + [last]
    else:
        pieces, rows, counts = [lax.all_gather(weights, "fsdp", axis=0, tiled=True)], jnp.zeros((1,), jnp.int32), ()
    states = lax.all_to_all(states, "fsdp", 0, 0, tiled=True)
    q, k, v, tm, qm, cm, *stack = project(tokens, pos, vectors, pieces, rows, counts)
    stack = stack[0] if direct else pieces[0]
    gr, gc, gv, *dws = masked_part(put, sizes, tm, cm, cot, vectors, stack)
    dq, dk, dv, gv_attn, *dws = attention_back(put, tokens, k, v, tm, qm, gc, dws)
    grad_vectors = jnp.concatenate([gv_attn[0:2], gv[2:12]], axis=0)
    dws, states = lax.optimization_barrier((dws, states))
    grad_vectors = jnp.sum(lax.all_gather(grad_vectors, ("dp", "fsdp")), axis=0)
    outs = []

    def page_task(*after):
        outs[:] = [
            forward_page(page_task.next, tokens, q, k, v, vectors, stack, tuple(outs), *after)
        ]
        page_task.next += 1
        return outs[0]

    def grad_task(*after):
        outs.append(input_grad(pos, dq, dk, dv, gr, stack, *after))
        return outs[-1]

    page_task.next = 0
    tasks = [page_task] * pages + [grad_task]
    states = jnp.take(states, state_at, axis=0, mode="clip")
    if direct:
        halves, wholes, done = reduce_blocks(dws, tasks)
    else:
        if groups > 1:
            mine = lax.psum_scatter(dws[0], ("dp", "fsdp"), scatter_dimension=0, tiled=True)
        else:
            mine = lax.psum_scatter(dws[0], "fsdp", scatter_dimension=0, tiled=True)
            mine = lax.psum(mine, "dp")
        for task in tasks:
            done = task()
        halves, wholes = (), (mine,)
    mine, new_mine = weight_step(halves, wholes, states, done, grad_vectors)

    held_first = me_f * held

    def held_table(table, first):
        return lax.dynamic_slice(table, (first,), (held,))

    def exchange(*after):
        (send,) = pick_blocks(send_to, [mine], (spread * lanes,), *after)
        return send, lax.all_to_all(send, "fsdp", 0, 0, tiled=True)

    if direct:
        kept = []

        def send_task(*after):
            send, owned = exchange(*after)
            kept.append(owned)
            return (send,)

        def swap_task(*after):
            (even,) = pick_blocks(grad_at(lead), kept, (capacity // 2,), *after)
            kept[:] = even, swap_dp(even)
            return (even,)

        def last_task(*after):
            return (tasks[pages](*after),)

        arrays, _ = gather_blocks(new_mine, (last_task, send_task, swap_task))
        at, near = gathered_place(group, spot, turn)
        at = jnp.where(near, at, 0)
        sibling = (me_f + 1 - 2 * (me_f % 2)) * held
        table = jnp.concatenate([held_table(at, held_first), held_table(at, sibling)])
        mine, handed = pick_blocks(table, arrays, (held, held))
        new_first, new_second = moment_step(info, *kept, first_slots, second_slots, mine)
        handed = swap_core(handed)
        ours = held_table(near, held_first)
        new_weights = jnp.where(ours[:, None, None], mine, handed).astype(F32)
    else:
        _, owned = exchange()
        axes = ("dp", "fsdp") if groups > 1 else "fsdp"
        new_all = lax.all_gather(new_mine, axes, axis=0, tiled=True)
        (kept,) = pick_blocks(held_table(place, held_first), [new_all], (held,))
        new_weights = kept.astype(F32)
        if groups > 1:
            (even,) = pick_blocks(grad_at(lead), [owned], (capacity // 2,))
            odd = swap_dp(even)
        else:
            even, odd = pick_blocks(
                jnp.concatenate([grad_at(0), grad_at(1)]), [owned], (capacity // 2, capacity // 2)
            )
        new_first, new_second = moment_step(info, even, odd, first_slots, second_slots)
    layer_out, token_grad = outs
    new_weights = new_weights.reshape(held * ROWS, WIDTH)
    new_vectors, new_vector_first, new_vector_second = adam_step(
        vectors, vector_first, vector_second, grad_vectors, VECTOR_RATE
    )
    return (
        layer_out,
        token_grad,
        new_weights,
        new_first,
        new_second,
        new_vectors,
        new_vector_first,
        new_vector_second,
    )


def solution(mesh):
    dp, fsdp = mesh.shape["dp"], mesh.shape["fsdp"]
    groups = 2 if dp == 2 and NBLK % (2 * fsdp) == 0 else 1
    both = ("dp", "fsdp")
    return jax.shard_map(
        functools.partial(local, groups),
        mesh=mesh,
        in_specs=(
            P(both, None),
            P(both, None),
            P(both),
            P(both, None, None),
            P("fsdp", None),
            P(),
            P(),
            P("fsdp", None, None),
            P("fsdp", None, None),
            P("fsdp", None, None),
            P(),
            P(),
        ),
        out_specs=(
            P(both, None),
            P(both, None),
            P("fsdp", None),
            P("fsdp", None, None),
            P("fsdp", None, None),
            P(),
            P(),
            P(),
        ),
        check_vma=False,
    )
```

```python
import functools

import jax
import jax.numpy as jnp
from jax import lax
from jax.experimental import pallas as pl
from jax.experimental.pallas import tpu as pltpu
from jax.sharding import PartitionSpec as P

WIDTH = 768
HEADS = 12
HD = 64
FF = 3072
PAGE = 512
MASKM = 104
ROWS = 48
STEP = 10
NBLK = 192
PAD = 112
STACK = NBLK * ROWS
UP_ROWS = FF // WIDTH

QUERY_SCALE = 0.125
NORM_EPSILON = 1e-06
INV_ROOT_TWO = 0.7071067811865476
INV_ROOT_TAU = 0.3989422804014327
FIRST_DECAY = 0.5
SECOND_DECAY = 0.5
LEARN_RATE = 0.05
VECTOR_RATE = 0.3
WEIGHT_DECAY = 0.01
ADAM_EPSILON = 1e-08

BF = jnp.bfloat16
F32 = jnp.float32
VMEM_LIMIT = 60 * 1024 * 1024
ANY = pl.BlockSpec(memory_space=pl.ANY)
VM = pl.BlockSpec(memory_space=pltpu.VMEM)


def cost(tflop, mbytes):
    return pl.CostEstimate(
        flops=int(tflop * 1e12), bytes_accessed=int(mbytes * 1e6), transcendentals=0
    )


def mm(a, b):
    return lax.dot_general(a, b, (((1,), (0,)), ((), ())), preferred_element_type=F32)


def mm_last(a, b):
    return lax.dot_general(a, b, (((1,), (1,)), ((), ())), preferred_element_type=F32)


def mm_first(a, b):
    return lax.dot_general(a, b, (((0,), (0,)), ((), ())), preferred_element_type=F32)


def send_blocks(stage_ref, first, count, place_ref, shift, arrays, sem):
    @pl.loop(first, first + count)
    def _(i):
        place, low = place_ref[shift + i], 0
        for array in arrays:
            high = low + array.shape[0]

            @pl.when((place >= low) & (place < high))
            def _(array=array, low=low):
                pltpu.make_async_copy(stage_ref.at[i], array.at[place - low], sem).start()

            low = high


def wait_blocks(stage_ref, first, count, sem):
    blocks = stage_ref.at[pl.ds(first, count)]
    pltpu.make_async_copy(blocks, blocks, sem).wait()


def row_sum(x):
    return jnp.sum(x, axis=0, keepdims=True)


def unit_of(x):
    center = x - jnp.mean(x, axis=1, keepdims=True)
    inverse = lax.rsqrt(jnp.mean(center * center, axis=1, keepdims=True) + NORM_EPSILON)
    return center * inverse, inverse


def unit_back(grad_out, gain, unit, inverse):
    grad_unit = grad_out * gain
    centered = grad_unit - jnp.mean(grad_unit, axis=1, keepdims=True)
    return inverse * (centered - unit * jnp.mean(grad_unit * unit, axis=1, keepdims=True))


def gelu_cdf(u):
    return 0.5 * (1.0 + lax.erf(u * INV_ROOT_TWO))


def half_masks():
    lane = lax.broadcasted_iota(jnp.int32, (1, 2 * HD), 1)
    low = jnp.where(lane < HD, 1.0, 0.0)
    return (low.astype(BF), (1.0 - low).astype(BF)), lane < HD


def both_heads(x, masks):
    return jnp.concatenate([x * masks[0], x * masks[1]], axis=0)


def own_lanes(x, low):
    rows = x.shape[0] // 2
    return jnp.where(low, x[:rows], x[rows:])


def softmax(scores):
    top = jnp.max(scores, axis=1, keepdims=True)
    exponent = jnp.exp(scores - top)
    total = jnp.sum(exponent, axis=1, keepdims=True)
    return exponent * (1.0 / total)


def one_hot_rows(pos):
    return jnp.where(
        pos == lax.broadcasted_iota(jnp.int32, (PAD, PAGE), 1), 1.0, 0.0
    ).astype(BF)


def project_kernel(counts, rows_ref, pos_ref, tok_ref, vec_ref, *rest):
    pieces, rest = rest[: max(1, len(counts))], rest[max(1, len(counts)) :]
    q_ref, k_ref, v_ref, tm_ref, qm_ref, cm_ref, *stacks, w_ref, sem = rest
    step, last = pl.program_id(0), pl.num_programs(0) - 1

    def cut(first, act):
        at = 0
        for piece, (number, size) in zip(pieces, counts):

            @pl.loop(0, number)
            def _(i, piece=piece, size=size, at=at):
                row = pl.multiple_of(rows_ref[at + i], 16)

                @pl.when((row < 3 * WIDTH) == first)
                def _():
                    source = piece.at[pl.ds(pl.multiple_of(i * size, 16), size)]
                    target = w_ref.at[pl.ds(row, size)]
                    act(pltpu.make_async_copy(source, target, sem.at[1 + at + i]))

            at += number

    @pl.when(step == 0)
    def _():
        if counts:
            cut(True, lambda copy: copy.start())
            cut(False, lambda copy: copy.start())
            cut(True, lambda copy: copy.wait())
        else:
            copy = pltpu.make_async_copy(pieces[0].at[pl.ds(0, 3 * WIDTH)], w_ref, sem.at[0])
            copy.start()
            copy.wait()

    if counts:

        @pl.when(step == 1)
        def _():
            cut(False, lambda copy: copy.wait())
            pltpu.make_async_copy(w_ref, stacks[0], sem.at[0]).start()

    tok = tok_ref[...]
    q = ((mm(tok, w_ref[0:WIDTH]) + vec_ref[0:1]) * QUERY_SCALE).astype(BF)
    k = mm(tok, w_ref[WIDTH : 2 * WIDTH]).astype(BF)
    v = (mm(tok, w_ref[2 * WIDTH : 3 * WIDTH]) + vec_ref[1:2]).astype(BF)
    q_ref[...] = q
    k_ref[...] = k
    v_ref[...] = v
    pick = one_hot_rows(pos_ref[0])
    tm_ref[...] = mm(pick, tok).astype(BF)
    qm = mm(pick, q).astype(BF)
    qm_ref[...] = qm
    masks, low = half_masks()
    for pair in range(HEADS // 2):
        cols = slice(pair * 2 * HD, (pair + 1) * 2 * HD)
        prob = softmax(mm_last(both_heads(qm[:, cols], masks), k[:, cols])).astype(BF)
        cm_ref[:, cols] = own_lanes(mm(prob, v[:, cols]), low).astype(BF)

    if counts:

        @pl.when(step == last)
        def _():
            pltpu.make_async_copy(w_ref, stacks[0], sem.at[0]).wait()


def project(tokens, pos, vectors, pieces, rows, counts):
    pages = tokens.shape[0] // PAGE
    tall = jax.ShapeDtypeStruct((pages * PAGE, WIDTH), BF)
    short = jax.ShapeDtypeStruct((pages * PAD, WIDTH), BF)
    page = pl.BlockSpec((PAGE, WIDTH), lambda i, s: (i, 0))
    few = pl.BlockSpec((PAD, WIDTH), lambda i, s: (i, 0))
    stack = [jax.ShapeDtypeStruct((STACK, WIDTH), BF)] if counts else []
    total = sum(number for number, _ in counts)
    return pl.pallas_call(
        functools.partial(project_kernel, counts),
        grid_spec=pltpu.PrefetchScalarGridSpec(
            num_scalar_prefetch=1,
            grid=(pages,),
            in_specs=[
                pl.BlockSpec((1, PAD, 1), lambda i, s: (i, 0, 0)),
                page,
                pl.BlockSpec((12, WIDTH), lambda i, s: (0, 0)),
            ]
            + [ANY] * len(pieces),
            out_specs=[page, page, page, few, few, few] + [ANY] * len(stack),
            scratch_shapes=[
                pltpu.VMEM((STACK if counts else 3 * WIDTH, WIDTH), BF),
                pltpu.SemaphoreType.DMA((1 + total,)),
            ],
        ),
        out_shape=[tall, tall, tall, short, short, short] + stack,
        compiler_params=pltpu.CompilerParams(vmem_limit_bytes=VMEM_LIMIT),
        cost_estimate=cost(0.018, 20),
        name="project",
    )(rows, pos, tokens, vectors, *pieces)


def masked_kernel(
    place_ref,
    tm_ref,
    cm_ref,
    cot_ref,
    vec_ref,
    w_any,
    gr_ref,
    gc_ref,
    gv_ref,
    *rest,
):
    *dws, w_ref, up_ref, act_ref, hid_ref, stage_ref, in_sem, out_sem = rest
    parts = 1 + 2 * UP_ROWS
    loads = [
        pltpu.make_async_copy(
            w_any.at[pl.ds((3 + i) * WIDTH, WIDTH)], w_ref.at[i], in_sem.at[i]
        )
        for i in range(parts)
    ]
    for load in loads:
        load.start()
    per = WIDTH // ROWS

    def keep(part, value):
        stage_ref[pl.ds(part * per, per)] = value.astype(BF).reshape(per, ROWS, WIDTH)

    gain_one, shift_one = vec_ref[8:9], vec_ref[9:10]
    gain_two = vec_ref[10:11]
    cm = cm_ref[...]
    loads[0].wait()
    resid_one = tm_ref[...].astype(F32) + mm(cm, w_ref[0]) + vec_ref[2:3]
    unit_one, inv_one = unit_of(resid_one)
    hidden_one = unit_one * gain_one + shift_one
    hid_ref[...] = hidden_one.astype(BF)
    hid = hid_ref[...]
    for c in range(UP_ROWS):
        cols = slice(c * WIDTH, (c + 1) * WIDTH)
        loads[1 + c].wait()
        up = mm_last(hid, w_ref[1 + c]) + vec_ref[3 + c : 4 + c]
        cdf = gelu_cdf(up)
        up_ref[:, cols] = cdf + up * jnp.exp(-0.5 * up * up) * INV_ROOT_TAU
        act_ref[:, cols] = (up * cdf).astype(BF)
    resid_two = hidden_one + vec_ref[7:8]
    for c in range(UP_ROWS):
        cols = slice(c * WIDTH, (c + 1) * WIDTH)
        loads[1 + UP_ROWS + c].wait()
        resid_two = resid_two + mm(act_ref[:, cols], w_ref[1 + UP_ROWS + c])
    unit_two, inv_two = unit_of(resid_two)
    cot = cot_ref[...].astype(F32)
    grad_two = unit_back(cot, gain_two, unit_two, inv_two)
    gv_ref[...] = jnp.zeros_like(gv_ref)
    gv_ref[10:11] = row_sum(cot * unit_two)
    gv_ref[11:12] = row_sum(cot)
    down = grad_two.astype(BF)
    gv_ref[7:8] = row_sum(down.astype(F32))
    grad_hidden = grad_two
    for c in range(UP_ROWS):
        cols = slice(c * WIDTH, (c + 1) * WIDTH)
        keep(1 + UP_ROWS + c, mm_first(act_ref[:, cols], down))
        grad_up = (mm_last(down, w_ref[1 + UP_ROWS + c]) * up_ref[:, cols]).astype(BF)
        gv_ref[3 + c : 4 + c] = row_sum(grad_up.astype(F32))
        keep(1 + c, mm_first(grad_up, hid))
        grad_hidden = grad_hidden + mm(grad_up, w_ref[1 + c])
    send_blocks(stage_ref, per, 2 * UP_ROWS * per, place_ref, 3 * per, dws, out_sem.at[1])
    gv_ref[8:9] = row_sum(grad_hidden * unit_one)
    gv_ref[9:10] = row_sum(grad_hidden)
    grad_one = unit_back(grad_hidden, gain_one, unit_one, inv_one)
    gr_ref[...] = grad_one
    attn = grad_one.astype(BF)
    gv_ref[2:3] = row_sum(attn.astype(F32))
    keep(0, mm_first(cm, attn))
    send_blocks(stage_ref, 0, per, place_ref, 3 * per, dws, out_sem.at[0])
    gc_ref[...] = mm_last(attn, w_ref[0]).astype(BF)
    wait_blocks(stage_ref, 0, per, out_sem.at[0])
    wait_blocks(stage_ref, per, 2 * UP_ROWS * per, out_sem.at[1])


def masked_part(place, sizes, tm, cm, cot, vectors, stack):
    rows = tm.shape[0]
    parts = 1 + 2 * UP_ROWS
    vm = pl.BlockSpec(memory_space=pltpu.VMEM)
    return pl.pallas_call(
        masked_kernel,
        grid_spec=pltpu.PrefetchScalarGridSpec(
            num_scalar_prefetch=1,
            grid=(),
            in_specs=[vm, vm, vm, vm, ANY],
            out_specs=[vm, vm, vm] + [ANY] * len(sizes),
            scratch_shapes=[
                pltpu.VMEM((parts, WIDTH, WIDTH), BF),
                pltpu.VMEM((rows, FF), F32),
                pltpu.VMEM((rows, FF), BF),
                pltpu.VMEM((rows, WIDTH), BF),
                pltpu.VMEM((parts * WIDTH // ROWS, ROWS, WIDTH), BF),
                pltpu.SemaphoreType.DMA((parts,)),
                pltpu.SemaphoreType.DMA((2,)),
            ],
        ),
        out_shape=[
            jax.ShapeDtypeStruct((rows, WIDTH), F32),
            jax.ShapeDtypeStruct((rows, WIDTH), BF),
            jax.ShapeDtypeStruct((16, WIDTH), F32),
        ]
        + [jax.ShapeDtypeStruct((size, ROWS, WIDTH), BF) for size in sizes],
        compiler_params=pltpu.CompilerParams(vmem_limit_bytes=VMEM_LIMIT),
        cost_estimate=cost(0.024, 30),
        name="masked",
    )(place, tm, cm, cot, vectors, stack)


def attention_back_kernel(
    place_ref,
    tok_ref,
    k_ref,
    v_ref,
    tm_ref,
    qm_ref,
    gc_ref,
    *rest,
):
    arrays = (len(rest) - 7) // 2
    dq_ref, dk_ref, dv_ref, gv_ref, *dws, sum_ref, stage_ref, out_sem = rest[arrays:]
    page, last = pl.program_id(0), pl.num_programs(0) - 1
    per = WIDTH // ROWS
    masks, low = half_masks()

    @pl.when(page == 0)
    def _():
        sum_ref[...] = jnp.zeros_like(sum_ref)
        gv_ref[...] = jnp.zeros_like(gv_ref)

    for pair in range(HEADS // 2):
        cols = slice(pair * 2 * HD, (pair + 1) * 2 * HD)
        kp, vp = k_ref[:, cols], v_ref[:, cols]
        qh, gh = both_heads(qm_ref[:, cols], masks), both_heads(gc_ref[:, cols], masks)
        prob = softmax(mm_last(qh, kp))
        grad_prob = mm_last(gh, vp)
        spread = jnp.sum(prob * grad_prob, axis=1, keepdims=True)
        grad_s = (prob * (grad_prob - spread)).astype(BF)
        dv_ref[:, cols] = mm_first(prob.astype(BF), gh).astype(BF)
        dk_ref[:, cols] = mm_first(grad_s, qh).astype(BF)
        dq_ref[:, cols] = own_lanes(mm(grad_s, kp), low).astype(BF) * QUERY_SCALE
    dq, dk, dv = dq_ref[...], dk_ref[...], dv_ref[...]
    gv_ref[0:1] += row_sum(dq.astype(F32))
    gv_ref[1:2] += row_sum(dv.astype(F32))
    tok = tok_ref[...]
    sum_ref[0] += mm_first(tm_ref[...], dq)
    sum_ref[1] += mm_first(tok, dk)
    sum_ref[2] += mm_first(tok, dv)

    @pl.when(page == last)
    def _():
        for i in range(3):
            stage_ref[pl.ds(i * per, per)] = (
                sum_ref[i].astype(BF).reshape(per, ROWS, WIDTH)
            )

            send_blocks(stage_ref, i * per, per, place_ref, 0, dws, out_sem.at[i])
        for i in range(3):
            wait_blocks(stage_ref, i * per, per, out_sem.at[i])


def attention_back(place, tokens, k, v, tm, qm, gc, dws):
    pages = tokens.shape[0] // PAGE
    page = pl.BlockSpec((PAGE, WIDTH), lambda i, s: (i, 0))
    few = pl.BlockSpec((PAD, WIDTH), lambda i, s: (i, 0))
    tall = jax.ShapeDtypeStruct((pages * PAGE, WIDTH), BF)
    return pl.pallas_call(
        attention_back_kernel,
        grid_spec=pltpu.PrefetchScalarGridSpec(
            num_scalar_prefetch=1,
            grid=(pages,),
            in_specs=[page, page, page, few, few, few] + [ANY] * len(dws),
            out_specs=[few, page, page, pl.BlockSpec((8, WIDTH), lambda i, s: (0, 0))]
            + [ANY] * len(dws),
            scratch_shapes=[
                pltpu.VMEM((3, WIDTH, WIDTH), F32),
                pltpu.VMEM((3 * WIDTH // ROWS, ROWS, WIDTH), BF),
                pltpu.SemaphoreType.DMA((3,)),
            ],
        ),
        out_shape=[
            jax.ShapeDtypeStruct((pages * PAD, WIDTH), BF),
            tall,
            tall,
            jax.ShapeDtypeStruct((8, WIDTH), F32),
        ]
        + [jax.ShapeDtypeStruct(dw.shape, BF) for dw in dws],
        input_output_aliases={7 + i: 4 + i for i in range(len(dws))},
        compiler_params=pltpu.CompilerParams(vmem_limit_bytes=VMEM_LIMIT),
        cost_estimate=cost(0.025, 30),
        name="attention_back",
    )(place, tokens, k, v, tm, qm, gc, *dws)


def forward_kernel(tok_ref, q_ref, k_ref, v_ref, vec_ref, w_any, *rest):
    out_ref, w_ref, ctx_ref, sem = rest[-4:]
    parts = 1 + 2 * UP_ROWS
    load = pltpu.make_async_copy(w_any.at[pl.ds(3 * WIDTH, parts * WIDTH)], w_ref, sem)
    load.start()

    masks, low = half_masks()
    for pair in range(HEADS // 2):
        cols = slice(pair * 2 * HD, (pair + 1) * 2 * HD)
        prob = softmax(mm_last(both_heads(q_ref[:, cols], masks), k_ref[:, cols])).astype(BF)
        ctx_ref[:, cols] = own_lanes(mm(prob, v_ref[:, cols]), low).astype(BF)
    load.wait()
    resid_one = tok_ref[...].astype(F32) + mm(ctx_ref[...], w_ref[0:WIDTH]) + vec_ref[2:3]
    unit_one, _ = unit_of(resid_one)
    hidden_one = unit_one * vec_ref[8:9] + vec_ref[9:10]
    hid = hidden_one.astype(BF)
    resid_two = hidden_one + vec_ref[7:8]
    for c in range(UP_ROWS):
        at, to = (1 + c) * WIDTH, (1 + UP_ROWS + c) * WIDTH
        up = mm_last(hid, w_ref[at : at + WIDTH]) + vec_ref[3 + c : 4 + c]
        act = (up * gelu_cdf(up)).astype(BF)
        resid_two = resid_two + mm(act, w_ref[to : to + WIDTH])
    unit_two, _ = unit_of(resid_two)
    out_ref[...] = (unit_two * vec_ref[10:11] + vec_ref[11:12]).astype(BF)


def forward_page(index, tokens, q, k, v, vectors, stack, before, *after):
    extra = before + after
    page = pl.BlockSpec((PAGE, WIDTH), lambda i: (index, 0))
    whole = pl.BlockSpec((12, WIDTH), lambda i: (0, 0))
    return pl.pallas_call(
        forward_kernel,
        grid=(1,),
        in_specs=[page, page, page, page, whole, ANY] + [ANY] * len(extra),
        out_specs=page,
        out_shape=jax.ShapeDtypeStruct(tokens.shape, BF),
        scratch_shapes=[
            pltpu.VMEM(((1 + 2 * UP_ROWS) * WIDTH, WIDTH), BF),
            pltpu.VMEM((PAGE, WIDTH), BF),
            pltpu.SemaphoreType.DMA,
        ],
        input_output_aliases={6: 0} if before else {},
        compiler_params=pltpu.CompilerParams(vmem_limit_bytes=VMEM_LIMIT),
        cost_estimate=cost(0.0, 0.001),
        name="forward_page",
    )(tokens, q, k, v, vectors, stack, *extra)


def input_grad_kernel(pos_ref, dq_ref, dk_ref, dv_ref, gr_ref, w_any, *rest):
    out_ref, w_ref, sem = rest[-3:]

    @pl.when(pl.program_id(0) == 0)
    def _():
        copy = pltpu.make_async_copy(w_any.at[pl.ds(0, 3 * WIDTH)], w_ref, sem)
        copy.start()
        copy.wait()

    few = gr_ref[...] + mm_last(dq_ref[...], w_ref[0:WIDTH])
    high = few.astype(BF)
    rest = (few - high.astype(F32)).astype(BF)
    pick = one_hot_rows(pos_ref[0])
    out_ref[...] = (
        mm_last(dk_ref[...], w_ref[WIDTH : 2 * WIDTH])
        + mm_last(dv_ref[...], w_ref[2 * WIDTH : 3 * WIDTH])
        + (mm_first(pick, high) + mm_first(pick, rest))
    )


def input_grad(pos, dq, dk, dv, gr, stack, *after):
    pages = dk.shape[0] // PAGE
    page = pl.BlockSpec((PAGE, WIDTH), lambda i: (i, 0))
    few = pl.BlockSpec((PAD, WIDTH), lambda i: (i, 0))
    return pl.pallas_call(
        input_grad_kernel,
        grid=(pages,),
        in_specs=[pl.BlockSpec((1, PAD, 1), lambda i: (i, 0, 0)), few, page, page, few, ANY]
        + [ANY] * len(after),
        out_specs=page,
        out_shape=jax.ShapeDtypeStruct(dk.shape, F32),
        scratch_shapes=[pltpu.VMEM((3 * WIDTH, WIDTH), BF), pltpu.SemaphoreType.DMA],
        compiler_params=pltpu.CompilerParams(vmem_limit_bytes=VMEM_LIMIT),
        cost_estimate=cost(0.0, 0.001),
        name="input_grad",
    )(pos, dq, dk, dv, gr, stack, *after)


def adam_step(parameter, moment_one, moment_two, gradient, rate):
    moment_one = FIRST_DECAY * moment_one + (1.0 - FIRST_DECAY) * gradient
    moment_two = SECOND_DECAY * moment_two + (1.0 - SECOND_DECAY) * gradient * gradient
    ascent = (
        moment_one
        / (1.0 - FIRST_DECAY**STEP)
        / (jnp.sqrt(moment_two / (1.0 - SECOND_DECAY**STEP)) + ADAM_EPSILON)
    )
    return (parameter - rate * (ascent + WEIGHT_DECAY * parameter), moment_one, moment_two)


ORDER = (2, 1, 3, 0)
SIZES = (96, 24, 48, 24)


def swap_dp(x):
    return lax.ppermute(x, "dp", [(0, 1), (1, 0)])


def swap_y(x):
    return lax.ppermute(x, "fsdp", [(f, f ^ 2) for f in range(16)])


def swap_core(x):
    return lax.ppermute(x, "fsdp", [(f, f ^ 1) for f in range(16)])


def up_z(x, steps):
    return lax.ppermute(x, "fsdp", [(f, (f + 4 * steps) % 16) for f in range(16)])


def apart(group, spot):
    me_d, me_f = lax.axis_index("dp"), lax.axis_index("fsdp")
    steps = (spot // 4 - me_f // 4) % 4
    dy = (spot // 2 % 2 + me_f // 2) % 2
    return steps, (group + me_d) % 2, dy, (spot + me_f) % 2


def relative_place(group, spot, turn):
    steps, dx, dy, core = apart(group, spot)
    half, third = turn // 3, turn % 3
    first = jnp.where(dx == 1, 0, 12) + dy * 3
    second = jnp.where(dy == 1, 6, 18) + dx * 3
    inner = jnp.where(half == 0, first, second) + third
    rank = jnp.where(steps == 2, 0, jnp.where(steps == 0, 3, jnp.where(steps == 1, 1, 2)))
    return core * 96 + rank * 24 + inner


def blocks_spec(shape, first=0):
    return pl.BlockSpec(shape, lambda i: (i + first,) + (0,) * (len(shape) - 1))


def core_sum_kernel(keep_ref, from_ref, *rest):
    for part, out in enumerate(rest[-4:]):
        out[0] = keep_ref[0, part] + from_ref[0, part]


def core_sum(keep, got, first, *after):
    count = got.shape[0] // 24
    whole, six = (1, 4, 6, ROWS, WIDTH), (1, 6, ROWS, WIDTH)
    return pl.pallas_call(
        core_sum_kernel,
        grid=(count,),
        in_specs=[blocks_spec(whole, first), blocks_spec(whole)] + [ANY] * len(after),
        out_specs=[blocks_spec(six)] * 4,
        out_shape=[jax.ShapeDtypeStruct((count,) + six[1:], BF)] * 4,
        compiler_params=pltpu.CompilerParams(vmem_limit_bytes=VMEM_LIMIT),
        cost_estimate=cost(0.0, 0.001),
        name="core_sum",
    )(keep.reshape((4,) + whole[1:]), got.reshape((count,) + whole[1:]), *after)


def first_sum_kernel(a_ref, b_ref, to_a_ref, to_b_ref, *rest):
    keep_a, keep_b, send_a, send_b = rest[-4:]
    half_a, half_b = a_ref[0] + to_a_ref[0], b_ref[0] + to_b_ref[0]
    keep_a[0], keep_b[0], send_a[0], send_b[0] = half_a[:3], half_b[:3], half_a[3:], half_b[3:]


def first_sum(a, b, to_a, to_b, *after, weight=0.001):
    count, six, three = a.shape[0], (1, 6, ROWS, WIDTH), (1, 3, ROWS, WIDTH)
    return pl.pallas_call(
        first_sum_kernel,
        grid=(count,),
        in_specs=[blocks_spec(six)] * 4 + [ANY] * len(after),
        out_specs=[blocks_spec(three)] * 4,
        out_shape=[jax.ShapeDtypeStruct((count,) + three[1:], BF)] * 4,
        compiler_params=pltpu.CompilerParams(vmem_limit_bytes=VMEM_LIMIT),
        cost_estimate=cost(0.0, weight),
        name="first_sum",
    )(a, b, to_a, to_b, *after)


def last_sum_kernel(count, passing, a_ref, b_ref, to_a_ref, to_b_ref, *rest):
    for i, out in enumerate(rest[-count:]):
        for low, one, two in ((0, a_ref, to_a_ref), (3, b_ref, to_b_ref)):
            total = one[i].astype(F32) + two[i].astype(F32)
            if i == 0 and passing:
                total = total + rest[0][low : low + 3].astype(F32)
            out[low : low + 3] = total.astype(BF)


def last_sum(a, b, to_a, to_b, passing, *after):
    count = a.shape[0]
    return pl.pallas_call(
        functools.partial(last_sum_kernel, count, len(passing)),
        in_specs=[VM] * (4 + len(passing)) + [ANY] * len(after),
        out_specs=[VM] * count,
        out_shape=[jax.ShapeDtypeStruct((6, ROWS, WIDTH), BF)] * count,
        compiler_params=pltpu.CompilerParams(vmem_limit_bytes=VMEM_LIMIT),
        cost_estimate=cost(0.0, 0.001),
        name="last_sum",
    )(a, b, to_a, to_b, *passing, *after)


def reduce_blocks(dws, tasks):
    keep = dws[0]
    got = [swap_core(send) for send in dws[1:]]
    xs_far, ys_far, a_far, b_far = core_sum(keep, got[0], 0)
    to_far = swap_dp(xs_far), swap_y(ys_far)
    a_far, b_far, ys_far, xs_far = first_sum(a_far, b_far, *to_far)
    to_far = swap_y(ys_far), swap_dp(xs_far)
    xs_near, ys_near, a_near, b_near = core_sum(keep, got[1], 1, ys_far)
    to_near = swap_dp(xs_near), swap_y(ys_near)
    done = tasks[0](xs_near)
    a_near, b_near, ys_near, xs_near = first_sum(a_near, b_near, *to_near, done)
    to_near = swap_y(ys_near), swap_dp(xs_near)
    (far,) = last_sum(a_far, b_far, *to_far, (), ys_near)
    xs_own, ys_own, a_own, b_own = core_sum(keep, got[2], 3, far)
    far = up_z(far, 1)
    to_own = swap_dp(xs_own), swap_y(ys_own)
    up, down = last_sum(a_near, b_near, *to_near, (far,), xs_own)
    near = up_z(up, 1), up_z(down, 3)
    a_own, b_own, ys_own, xs_own = first_sum(a_own, b_own, *to_own, up)
    to_own = swap_y(ys_own), swap_dp(xs_own)
    done = tasks[1](ys_own)
    return (a_own, to_own[0], b_own, to_own[1]), near, done


def weight_step_kernel(halves, wholes, *refs):
    half_refs, refs = refs[:halves], refs[halves:]
    whole_refs, refs = refs[:wholes], refs[wholes:]
    state_ref, grad_out, new_out = refs[0], refs[-2], refs[-1]
    for i in range(grad_out.shape[0]):
        parts = [ref[i] for ref in whole_refs]
        if halves:
            first = 2 * (i // 3)
            parts += [ref[0, i % 3] for ref in half_refs[first : first + 2]]
        total = parts[0].astype(F32)
        for part in parts[1:]:
            total = total + part.astype(F32)
        grad = total.astype(BF)
        grad_out[i] = grad
        new, _, _ = adam_step(
            state_ref[i, 0].astype(F32),
            state_ref[i, 1].astype(F32),
            state_ref[i, 2].astype(F32),
            grad.astype(F32),
            LEARN_RATE,
        )
        new_out[i] = new.astype(BF)


def weight_step(halves, wholes, states, *after):
    count = states.shape[0]
    shape = jax.ShapeDtypeStruct((count, ROWS, WIDTH), BF)
    return pl.pallas_call(
        functools.partial(weight_step_kernel, len(halves), len(wholes)),
        in_specs=[VM] * (len(halves) + len(wholes) + 1) + [ANY] * len(after),
        out_specs=[VM] * 2,
        out_shape=[shape, shape],
        compiler_params=pltpu.CompilerParams(vmem_limit_bytes=VMEM_LIMIT),
        cost_estimate=cost(0.0, 0.001),
        name="weight_step",
    )(*halves, *wholes, states, *after)


def moment_step_kernel(info_ref, grad_ref, first_ref, second_ref, *rest):
    one_ref, two_ref = rest[-2:]
    count = first_ref.shape[0]
    for i in range(count):
        slot = 2 * (pl.program_id(0) * count + i) + info_ref[0]
        grad = jnp.where(slot < info_ref[1], grad_ref[i].astype(F32), 0.0)
        one_ref[i, 0] = FIRST_DECAY * first_ref[i, 0] + (1.0 - FIRST_DECAY) * grad
        two_ref[i, 0] = SECOND_DECAY * second_ref[i, 0] + (1.0 - SECOND_DECAY) * grad * grad


def moment_step(info, grads, first, second, before, *after):
    half = grads.shape[0]
    each = 4 if half % 4 == 0 else 2
    pairs = (half, 2, ROWS, WIDTH)
    slots = pl.BlockSpec((each, 1, ROWS, WIDTH), lambda i, s: (i, s[0], 0, 0))
    shape = jax.ShapeDtypeStruct(pairs, F32)
    extra = before + after
    return tuple(
        pl.pallas_call(
            moment_step_kernel,
            grid_spec=pltpu.PrefetchScalarGridSpec(
                num_scalar_prefetch=1,
                grid=(half // each,),
                in_specs=[pl.BlockSpec((each, ROWS, WIDTH), lambda i, s: (i, 0, 0)), slots, slots]
                + [ANY] * len(extra),
                out_specs=[slots, slots],
            ),
            out_shape=[shape, shape],
            input_output_aliases={4: 0, 5: 1} if before else {},
            compiler_params=pltpu.CompilerParams(vmem_limit_bytes=VMEM_LIMIT),
            cost_estimate=cost(0.0, 0.001),
            name="moment_step",
        )(info, grads, first.reshape(pairs), second.reshape(pairs), *extra)
    )


def pick_kernel(sizes, arrays, from_ref, *refs):
    outs, sem = refs[-1 - len(sizes) : -1], refs[-1]
    slot = 0
    for out, size in zip(outs, sizes):

        @pl.loop(0, size)
        def _(i, out=out, slot=slot):
            number, low = from_ref[slot + i], 0
            for array in refs[:arrays]:
                high = low + array.shape[0]

                @pl.when((number >= low) & (number < high))
                def _(array=array, low=low):
                    pltpu.make_async_copy(
                        array.at[number - low], out.at[i], sem.at[slot + i]
                    ).start()

                low = high

        slot += size
    slot = 0
    for out, size in zip(outs, sizes):

        @pl.loop(0, size)
        def _(i, out=out, slot=slot):
            pltpu.make_async_copy(refs[0].at[0], out.at[i], sem.at[slot + i]).wait()

        slot += size


def pick_blocks(source, arrays, sizes, *after):
    arrays = [array.reshape(-1, ROWS, WIDTH) for array in arrays]
    return pl.pallas_call(
        functools.partial(pick_kernel, sizes, len(arrays)),
        grid_spec=pltpu.PrefetchScalarGridSpec(
            num_scalar_prefetch=1,
            grid=(),
            in_specs=[ANY] * (len(arrays) + len(after)),
            out_specs=[VM] * len(sizes),
            scratch_shapes=[pltpu.SemaphoreType.DMA((sum(sizes),))],
        ),
        out_shape=[jax.ShapeDtypeStruct((size, ROWS, WIDTH), BF) for size in sizes],
        compiler_params=pltpu.CompilerParams(vmem_limit_bytes=VMEM_LIMIT),
        cost_estimate=cost(0.0, 0.001),
        name="pick_blocks",
    )(source, *arrays, *after)


def move_kernel(plan, *refs):
    for out, pieces in zip(refs[-len(plan) :], plan):
        at = 0
        for source, low, high in pieces:
            out[at : at + high - low] = refs[source][low:high]
            at += high - low


def move(plan, arrays, *after):
    return pl.pallas_call(
        functools.partial(move_kernel, plan),
        in_specs=[VM] * len(arrays) + [ANY] * len(after),
        out_specs=[VM] * len(plan),
        out_shape=[
            jax.ShapeDtypeStruct((sum(high - low for _, low, high in pieces), ROWS, WIDTH), BF)
            for pieces in plan
        ],
        compiler_params=pltpu.CompilerParams(vmem_limit_bytes=VMEM_LIMIT),
        cost_estimate=cost(0.0, 0.001),
        name="move",
    )(*arrays, *after)


ENDS = (((0, 0, 3),), ((1, 3, 6),))
TWO_ENDS = (((0, 0, 3), (0, 6, 9)), ((1, 3, 6), (1, 9, 12)))


def gather_blocks(mine, tasks):
    up, down = up_z(mine, 1), up_z(mine, 3)
    far = up_z(up, 1)
    own_x, own_y = swap_dp(mine), swap_y(mine)
    done = tasks[0](mine)
    end_x, end_y = move(ENDS, [own_x, own_y], *done)
    own = [mine, own_x, own_y, swap_y(end_x), swap_dp(end_y)]
    (near,) = move((((0, 0, 6), (1, 0, 6)),), [up, down], end_x)
    near_x, near_y = swap_dp(near), swap_y(near)
    done = tasks[1](near)
    if len(tasks) == 2:
        far_x, far_y = swap_dp(far), swap_y(far)
        end_x, end_y = move(TWO_ENDS, [near_x, near_y], *done, far)
        near = [near, near_x, near_y, swap_y(end_x), swap_dp(end_y)]
        end_x, end_y = move(ENDS, [far_x, far_y], end_x)
    else:
        (far,) = move((((0, 0, 6),),), [far], *done)
        far_x, far_y = swap_dp(far), swap_y(far)
        end_x, end_y = move(TWO_ENDS, [near_x, near_y], far, *own[3:])
        near = [near, near_x, near_y, swap_y(end_x), swap_dp(end_y)]
        done = tasks[2](end_x)
        end_x, end_y = move(ENDS, [far_x, far_y], *done)
    far = [far, far_x, far_y, swap_y(end_x), swap_dp(end_y)]
    return own + far + near, end_x


PIECES = ((1, 288), (1, 288), (1, 288), (1, 144), (1, 144))
PIECES += PIECES + tuple((2 * number, rows) for number, rows in PIECES)
PIECES += PIECES


def piece_rows():
    me_d, me_f = lax.axis_index("dp"), lax.axis_index("fsdp")
    rows = []
    for core in (0, 1):
        for steps in ((0,), (2,), (1, 3)):
            for dx, dy, low in ((0, 0, 0), (1, 0, 0), (0, 1, 0), (1, 1, 0), (1, 1, 144)):
                for step in steps:
                    z = (me_f // 4 - step) % 4
                    y, c = (me_f // 2 + dy) % 2, (me_f + core) % 2
                    rows.append((((z * 2 + y) * 2 + c) * 2 + (me_d + dx) % 2) * 288 + low)
    return jnp.stack(rows).astype(jnp.int32)


def gather_stack(weights, early):
    half = weights.shape[0] // 2
    mine = lax.dynamic_slice(weights, (lax.axis_index("dp") * half, 0), (half, WIDTH))
    tasks = [lambda *after: early, lambda *after: after]
    arrays, _ = gather_blocks(mine.reshape(-1, ROWS, WIDTH), tasks)
    arrays += [swap_core(array) for array in arrays]
    return [array.reshape(-1, WIDTH) for array in arrays]


def gathered_place(group, spot, turn):
    ahead, dx, dy, core = apart(group, spot)
    steps = (4 - ahead) % 4
    side, pair = dx + 2 * dy, steps // 2
    plain = jnp.where(steps == 2, 24, 0) + side * 6 + turn
    corner = jnp.where(turn < 3, 84 + pair * 3 + turn, 90 + pair * 3 + turn - 3)
    near = jnp.where(side == 3, corner, 48 + side * 12 + pair * 6 + turn)
    steps_odd = steps % 2 == 1
    return jnp.where(steps_odd, near, plain), core == 0


def local(
    groups,
    tokens,
    masked_pos,
    masked_count,
    out_grad,
    weights,
    vectors,
    owner_list,
    master_slots,
    first_slots,
    second_slots,
    vector_first,
    vector_second,
):
    pages = masked_pos.shape[0]
    capacity = master_slots.shape[0]
    held = weights.shape[0] // ROWS
    spread = lax.axis_size("fsdp")
    me_f = lax.axis_index("fsdp")
    ids = groups * spread
    each = NBLK // ids
    lanes = -(-capacity // ids)
    my_group = lax.axis_index("dp") if groups > 1 else 0
    me = me_f * groups + my_group

    blocks = jnp.arange(NBLK, dtype=jnp.int32)
    lower = owner_list[None, :] < owner_list[:, None]
    tied = (owner_list[None, :] == owner_list[:, None]) & (blocks[None, :] < blocks[:, None])
    rank = jnp.sum((lower | tied).astype(jnp.int32), axis=1)
    group, spot, turn = rank % groups, rank % ids // groups, rank // ids
    place = (group * spread + spot) * each + turn
    direct = groups == 2 and spread == 16 and each == 6 and pages == 3
    if direct:
        sizes = SIZES
        put = relative_place(group, spot, turn)
    else:
        sizes, put = (NBLK,), place
    owners = jnp.arange(spread, dtype=jnp.int32)
    start = jnp.sum((owner_list[None, :] < owners[:, None]).astype(jnp.int32), axis=1)
    count = jnp.sum((owner_list[None, :] == owners[:, None]).astype(jnp.int32), axis=1)
    lane = jnp.arange(lanes, dtype=jnp.int32) * ids

    my_start, my_count = start[me_f], count[me_f]
    slot_to = ((owners * groups + my_group - my_start) % ids)[:, None] + lane[None, :]
    slot_to = jnp.minimum(slot_to, capacity - 1).reshape(-1)
    slot_at = ((me - start) % ids)[:, None] + lane[None, :]
    send_to = jnp.clip((start[:, None] + slot_at) // ids, 0, each - 1).reshape(-1)
    my_rank = me + ids * jnp.arange(each, dtype=jnp.int32)
    my_owner = jnp.sum((start + count)[None, :] <= my_rank[:, None], axis=1).astype(jnp.int32)
    my_lane = (my_rank - start[my_owner]) // ids
    state_at = my_owner * lanes + my_lane
    lead = (my_group - my_start) % 2 if groups > 1 else 0
    slots = jnp.arange(capacity // 2, dtype=jnp.int32) * 2

    def grad_at(first):
        which = slots + first
        return ((my_start + which) % ids // groups) * lanes + which // ids

    info = [jnp.stack([jnp.asarray(side, jnp.int32), my_count]) for side in (lead, 1 - lead)]

    states = jnp.stack(
        [
            jnp.take(master_slots, slot_to, axis=0, mode="clip").astype(BF),
            jnp.take(first_slots, slot_to, axis=0, mode="clip").astype(BF),
            jnp.take(second_slots, slot_to, axis=0, mode="clip").astype(BF),
        ],
        axis=1,
    )

    live = jnp.arange(MASKM, dtype=jnp.int32)[None, :] < masked_count[:, None]
    pos = jnp.pad(
        jnp.where(live, masked_pos, -1), ((0, 0), (0, PAD - MASKM)), constant_values=-1
    )[:, :, None]
    cot = jnp.pad(
        jnp.where(live[:, :, None], out_grad, jnp.zeros((), BF)), ((0, 0), (0, PAD - MASKM), (0, 0))
    ).reshape(pages * PAD, WIDTH)

    if direct:
        pieces, rows, counts = gather_stack(weights, (states, cot)), piece_rows(), PIECES
        last, states = lax.optimization_barrier((pieces[-1], states))
        pieces = pieces[:-1] + [last]
    else:
        pieces, rows, counts = [lax.all_gather(weights, "fsdp", axis=0, tiled=True)], jnp.zeros((1,), jnp.int32), ()
    states = lax.all_to_all(states, "fsdp", 0, 0, tiled=True)
    q, k, v, tm, qm, cm, *stack = project(tokens, pos, vectors, pieces, rows, counts)
    stack = stack[0] if direct else pieces[0]
    gr, gc, gv, *dws = masked_part(put, sizes, tm, cm, cot, vectors, stack)
    dq, dk, dv, gv_attn, *dws = attention_back(put, tokens, k, v, tm, qm, gc, dws)
    grad_vectors = jnp.concatenate([gv_attn[0:2], gv[2:12]], axis=0)
    dws, states = lax.optimization_barrier((dws, states))
    grad_vectors = jnp.sum(lax.all_gather(grad_vectors, ("dp", "fsdp")), axis=0)
    layer_out, token_grad = [], []

    def page_task(page, *after):
        layer_out[:] = [
            forward_page(page, tokens, q, k, v, vectors, stack, tuple(layer_out), *after)
        ]
        return layer_out[0]

    def grad_task(*after):
        token_grad.append(input_grad(pos, dq, dk, dv, gr, stack, *after))
        return token_grad[0]

    tasks = [functools.partial(page_task, page) for page in range(pages)] + [grad_task]
    states = jnp.take(states, state_at, axis=0, mode="clip")
    if direct:
        halves, wholes, done = reduce_blocks(dws, tasks)
    else:
        if groups > 1:
            mine = lax.psum_scatter(dws[0], ("dp", "fsdp"), scatter_dimension=0, tiled=True)
        else:
            mine = lax.psum_scatter(dws[0], "fsdp", scatter_dimension=0, tiled=True)
            mine = lax.psum(mine, "dp")
        for task in tasks:
            done = task()
        halves, wholes = (), (mine,)
    mine, new_mine = weight_step(halves, wholes, states, done)

    held_first = me_f * held

    def held_table(table, first):
        return lax.dynamic_slice(table, (first,), (held,))

    def exchange(*after):
        (send,) = pick_blocks(send_to, [mine], (spread * lanes,), grad_vectors, *after)
        return send, lax.all_to_all(send, "fsdp", 0, 0, tiled=True)

    if direct:
        kept, moments = [], []

        def send_task(*after):
            send, owned = exchange(*after)
            kept.append(owned)
            return (tasks[2](send),)

        def swap_task(*after):
            (even,) = pick_blocks(grad_at(lead), kept, (capacity // 2,), *after)
            kept[:] = [swap_dp(even)]
            moments.append(moment_step(info[0], even, first_slots, second_slots, ()))
            return even, moments[0][0]

        def last_task(*after):
            return (tasks[pages](*after),)

        arrays, _ = gather_blocks(new_mine, (last_task, send_task, swap_task))
        at, near = gathered_place(group, spot, turn)
        at = jnp.where(near, at, 0)
        sibling = (me_f + 1 - 2 * (me_f % 2)) * held
        table = jnp.concatenate([held_table(at, held_first), held_table(at, sibling)])
        mine, handed = pick_blocks(table, arrays, (held, held))
        new_first, new_second = moment_step(
            info[1], kept[0], first_slots, second_slots, moments[0], mine
        )
        handed = swap_core(handed)
        ours = held_table(near, held_first)
        new_weights = jnp.where(ours[:, None, None], mine, handed).astype(F32)
    else:
        _, owned = exchange()
        axes = ("dp", "fsdp") if groups > 1 else "fsdp"
        new_all = lax.all_gather(new_mine, axes, axis=0, tiled=True)
        (kept,) = pick_blocks(held_table(place, held_first), [new_all], (held,))
        new_weights = kept.astype(F32)
        if groups > 1:
            (even,) = pick_blocks(grad_at(lead), [owned], (capacity // 2,))
            odd = swap_dp(even)
        else:
            even, odd = pick_blocks(
                jnp.concatenate([grad_at(0), grad_at(1)]), [owned], (capacity // 2, capacity // 2)
            )
        moments = moment_step(info[0], even, first_slots, second_slots, ())
        new_first, new_second = moment_step(info[1], odd, first_slots, second_slots, moments)
    (layer_out,), (token_grad,) = layer_out, token_grad
    new_weights = new_weights.reshape(held * ROWS, WIDTH)
    new_first, new_second = (x.reshape(first_slots.shape) for x in (new_first, new_second))
    new_vectors, new_vector_first, new_vector_second = adam_step(
        vectors, vector_first, vector_second, grad_vectors, VECTOR_RATE
    )
    return (
        layer_out,
        token_grad,
        new_weights,
        new_first,
        new_second,
        new_vectors,
        new_vector_first,
        new_vector_second,
    )


def solution(mesh):
    dp, fsdp = mesh.shape["dp"], mesh.shape["fsdp"]
    groups = 2 if dp == 2 and NBLK % (2 * fsdp) == 0 else 1
    both = ("dp", "fsdp")
    return jax.shard_map(
        functools.partial(local, groups),
        mesh=mesh,
        in_specs=(
            P(both, None),
            P(both, None),
            P(both),
            P(both, None, None),
            P("fsdp", None),
            P(),
            P(),
            P("fsdp", None, None),
            P("fsdp", None, None),
            P("fsdp", None, None),
            P(),
            P(),
        ),
        out_specs=(
            P(both, None),
            P(both, None),
            P("fsdp", None),
            P("fsdp", None, None),
            P("fsdp", None, None),
            P(),
            P(),
            P(),
        ),
        check_vma=False,
    )
```

```python
import functools

import jax
import jax.numpy as jnp
from jax import lax
from jax.experimental import pallas as pl
from jax.experimental.pallas import tpu as pltpu
from jax.sharding import PartitionSpec as P

WIDTH = 768
HEADS = 12
HD = 64
FF = 3072
PAGE = 512
MASKM = 104
ROWS = 48
STEP = 10
NBLK = 192
PAD = 112
STACK = NBLK * ROWS
UP_ROWS = FF // WIDTH

QUERY_SCALE = 0.125
NORM_EPSILON = 1e-06
INV_ROOT_TWO = 0.7071067811865476
INV_ROOT_TAU = 0.3989422804014327
FIRST_DECAY = 0.5
SECOND_DECAY = 0.5
LEARN_RATE = 0.05
VECTOR_RATE = 0.3
WEIGHT_DECAY = 0.01
ADAM_EPSILON = 1e-08

BF = jnp.bfloat16
F32 = jnp.float32
VMEM_LIMIT = 60 * 1024 * 1024
ANY = pl.BlockSpec(memory_space=pl.ANY)
VM = pl.BlockSpec(memory_space=pltpu.VMEM)


def cost(tflop, mbytes):
    return pl.CostEstimate(
        flops=int(tflop * 1e12), bytes_accessed=int(mbytes * 1e6), transcendentals=0
    )


def mm(a, b):
    return lax.dot_general(a, b, (((1,), (0,)), ((), ())), preferred_element_type=F32)


def mm_last(a, b):
    return lax.dot_general(a, b, (((1,), (1,)), ((), ())), preferred_element_type=F32)


def mm_first(a, b):
    return lax.dot_general(a, b, (((0,), (0,)), ((), ())), preferred_element_type=F32)


def send_blocks(stage_ref, first, count, place_ref, shift, arrays, sem):
    @pl.loop(first, first + count)
    def _(i):
        place, low = place_ref[shift + i], 0
        for array in arrays:
            high = low + array.shape[0]

            @pl.when((place >= low) & (place < high))
            def _(array=array, low=low):
                pltpu.make_async_copy(stage_ref.at[i], array.at[place - low], sem).start()

            low = high


def wait_blocks(stage_ref, first, count, sem):
    blocks = stage_ref.at[pl.ds(first, count)]
    pltpu.make_async_copy(blocks, blocks, sem).wait()


def row_sum(x):
    return jnp.sum(x, axis=0, keepdims=True)


def unit_of(x):
    center = x - jnp.mean(x, axis=1, keepdims=True)
    inverse = lax.rsqrt(jnp.mean(center * center, axis=1, keepdims=True) + NORM_EPSILON)
    return center * inverse, inverse


def unit_back(grad_out, gain, unit, inverse):
    grad_unit = grad_out * gain
    centered = grad_unit - jnp.mean(grad_unit, axis=1, keepdims=True)
    return inverse * (centered - unit * jnp.mean(grad_unit * unit, axis=1, keepdims=True))


def gelu_cdf(u):
    return 0.5 * (1.0 + lax.erf(u * INV_ROOT_TWO))


def half_masks():
    lane = lax.broadcasted_iota(jnp.int32, (1, 2 * HD), 1)
    low = jnp.where(lane < HD, 1.0, 0.0)
    return (low.astype(BF), (1.0 - low).astype(BF)), lane < HD


def both_heads(x, masks):
    return jnp.concatenate([x * masks[0], x * masks[1]], axis=0)


def own_lanes(x, low):
    rows = x.shape[0] // 2
    return jnp.where(low, x[:rows], x[rows:])


def softmax(scores):
    top = jnp.max(scores, axis=1, keepdims=True)
    exponent = jnp.exp(scores - top)
    total = jnp.sum(exponent, axis=1, keepdims=True)
    return exponent * (1.0 / total)


def one_hot_rows(pos):
    return jnp.where(
        pos == lax.broadcasted_iota(jnp.int32, (PAD, PAGE), 1), 1.0, 0.0
    ).astype(BF)


def project_kernel(counts, rows_ref, pos_ref, tok_ref, vec_ref, *rest):
    pieces, rest = rest[: max(1, len(counts))], rest[max(1, len(counts)) :]
    q_ref, k_ref, v_ref, tm_ref, qm_ref, cm_ref, *stacks, w_ref, sem = rest
    step, last = pl.program_id(0), pl.num_programs(0) - 1

    def cut(first, act):
        at = 0
        for piece, (number, size) in zip(pieces, counts):

            @pl.loop(0, number)
            def _(i, piece=piece, size=size, at=at):
                row = pl.multiple_of(rows_ref[at + i], 16)

                @pl.when((row < 3 * WIDTH) == first)
                def _():
                    source = piece.at[pl.ds(pl.multiple_of(i * size, 16), size)]
                    target = w_ref.at[pl.ds(row, size)]
                    act(pltpu.make_async_copy(source, target, sem.at[1 + at + i]))

            at += number

    @pl.when(step == 0)
    def _():
        if counts:
            cut(True, lambda copy: copy.start())
            cut(False, lambda copy: copy.start())
            cut(True, lambda copy: copy.wait())
        else:
            copy = pltpu.make_async_copy(pieces[0].at[pl.ds(0, 3 * WIDTH)], w_ref, sem.at[0])
            copy.start()
            copy.wait()

    if counts:

        @pl.when(step == 1)
        def _():
            cut(False, lambda copy: copy.wait())
            pltpu.make_async_copy(w_ref, stacks[0], sem.at[0]).start()

    tok = tok_ref[...]
    q = ((mm(tok, w_ref[0:WIDTH]) + vec_ref[0:1]) * QUERY_SCALE).astype(BF)
    k = mm(tok, w_ref[WIDTH : 2 * WIDTH]).astype(BF)
    v = (mm(tok, w_ref[2 * WIDTH : 3 * WIDTH]) + vec_ref[1:2]).astype(BF)
    q_ref[...] = q
    k_ref[...] = k
    v_ref[...] = v
    pick = one_hot_rows(pos_ref[0])
    tm_ref[...] = mm(pick, tok).astype(BF)
    qm = mm(pick, q).astype(BF)
    qm_ref[...] = qm
    masks, low = half_masks()
    pairs = [slice(pair * 2 * HD, (pair + 1) * 2 * HD) for pair in range(HEADS // 2)]

    def scores_of(cols):
        return mm_last(both_heads(qm[:, cols], masks), k[:, cols])

    ahead = scores_of(pairs[0])
    for i, cols in enumerate(pairs):
        scores = ahead
        if i + 1 < len(pairs):
            ahead = scores_of(pairs[i + 1])
        prob = softmax(scores).astype(BF)
        cm_ref[:, cols] = own_lanes(mm(prob, v[:, cols]), low).astype(BF)

    if counts:

        @pl.when(step == last)
        def _():
            pltpu.make_async_copy(w_ref, stacks[0], sem.at[0]).wait()


def project(tokens, pos, vectors, pieces, rows, counts):
    pages = tokens.shape[0] // PAGE
    tall = jax.ShapeDtypeStruct((pages * PAGE, WIDTH), BF)
    short = jax.ShapeDtypeStruct((pages * PAD, WIDTH), BF)
    page = pl.BlockSpec((PAGE, WIDTH), lambda i, s: (i, 0))
    few = pl.BlockSpec((PAD, WIDTH), lambda i, s: (i, 0))
    stack = [jax.ShapeDtypeStruct((STACK, WIDTH), BF)] if counts else []
    total = sum(number for number, _ in counts)
    return pl.pallas_call(
        functools.partial(project_kernel, counts),
        grid_spec=pltpu.PrefetchScalarGridSpec(
            num_scalar_prefetch=1,
            grid=(pages,),
            in_specs=[
                pl.BlockSpec((1, PAD, 1), lambda i, s: (i, 0, 0)),
                page,
                pl.BlockSpec((12, WIDTH), lambda i, s: (0, 0)),
            ]
            + [ANY] * len(pieces),
            out_specs=[page, page, page, few, few, few] + [ANY] * len(stack),
            scratch_shapes=[
                pltpu.VMEM((STACK if counts else 3 * WIDTH, WIDTH), BF),
                pltpu.SemaphoreType.DMA((1 + total,)),
            ],
        ),
        out_shape=[tall, tall, tall, short, short, short] + stack,
        compiler_params=pltpu.CompilerParams(vmem_limit_bytes=VMEM_LIMIT),
        cost_estimate=cost(0.018, 20),
        name="project",
    )(rows, pos, tokens, vectors, *pieces)


def masked_kernel(
    place_ref,
    tm_ref,
    cm_ref,
    cot_ref,
    vec_ref,
    w_any,
    gr_ref,
    gc_ref,
    gv_ref,
    *rest,
):
    *dws, w_ref, up_ref, act_ref, hid_ref, stage_ref, in_sem, out_sem = rest
    parts = 1 + 2 * UP_ROWS
    loads = [
        pltpu.make_async_copy(
            w_any.at[pl.ds((3 + i) * WIDTH, WIDTH)], w_ref.at[i], in_sem.at[i]
        )
        for i in range(parts)
    ]
    for load in loads:
        load.start()
    per = WIDTH // ROWS

    def keep(part, value):
        stage_ref[pl.ds(part * per, per)] = value.astype(BF).reshape(per, ROWS, WIDTH)

    gain_one, shift_one = vec_ref[8:9], vec_ref[9:10]
    gain_two = vec_ref[10:11]
    cm = cm_ref[...]
    loads[0].wait()
    resid_one = tm_ref[...].astype(F32) + mm(cm, w_ref[0]) + vec_ref[2:3]
    unit_one, inv_one = unit_of(resid_one)
    hidden_one = unit_one * gain_one + shift_one
    hid_ref[...] = hidden_one.astype(BF)
    hid = hid_ref[...]
    for c in range(UP_ROWS):
        cols = slice(c * WIDTH, (c + 1) * WIDTH)
        loads[1 + c].wait()
        up = mm_last(hid, w_ref[1 + c]) + vec_ref[3 + c : 4 + c]
        cdf = gelu_cdf(up)
        up_ref[:, cols] = cdf + up * jnp.exp(-0.5 * up * up) * INV_ROOT_TAU
        act_ref[:, cols] = (up * cdf).astype(BF)
    resid_two = hidden_one + vec_ref[7:8]
    for c in range(UP_ROWS):
        cols = slice(c * WIDTH, (c + 1) * WIDTH)
        loads[1 + UP_ROWS + c].wait()
        resid_two = resid_two + mm(act_ref[:, cols], w_ref[1 + UP_ROWS + c])
    unit_two, inv_two = unit_of(resid_two)
    cot = cot_ref[...].astype(F32)
    grad_two = unit_back(cot, gain_two, unit_two, inv_two)
    gv_ref[...] = jnp.zeros_like(gv_ref)
    gv_ref[10:11] = row_sum(cot * unit_two)
    gv_ref[11:12] = row_sum(cot)
    down = grad_two.astype(BF)
    gv_ref[7:8] = row_sum(down.astype(F32))
    grad_hidden = grad_two
    for c in range(UP_ROWS):
        cols = slice(c * WIDTH, (c + 1) * WIDTH)
        keep(1 + UP_ROWS + c, mm_first(act_ref[:, cols], down))
        grad_up = (mm_last(down, w_ref[1 + UP_ROWS + c]) * up_ref[:, cols]).astype(BF)
        gv_ref[3 + c : 4 + c] = row_sum(grad_up.astype(F32))
        keep(1 + c, mm_first(grad_up, hid))
        grad_hidden = grad_hidden + mm(grad_up, w_ref[1 + c])
    send_blocks(stage_ref, per, 2 * UP_ROWS * per, place_ref, 3 * per, dws, out_sem.at[1])
    gv_ref[8:9] = row_sum(grad_hidden * unit_one)
    gv_ref[9:10] = row_sum(grad_hidden)
    grad_one = unit_back(grad_hidden, gain_one, unit_one, inv_one)
    gr_ref[...] = grad_one
    attn = grad_one.astype(BF)
    gv_ref[2:3] = row_sum(attn.astype(F32))
    keep(0, mm_first(cm, attn))
    send_blocks(stage_ref, 0, per, place_ref, 3 * per, dws, out_sem.at[0])
    gc_ref[...] = mm_last(attn, w_ref[0]).astype(BF)
    wait_blocks(stage_ref, 0, per, out_sem.at[0])
    wait_blocks(stage_ref, per, 2 * UP_ROWS * per, out_sem.at[1])


def masked_part(place, sizes, tm, cm, cot, vectors, stack):
    rows = tm.shape[0]
    parts = 1 + 2 * UP_ROWS
    vm = pl.BlockSpec(memory_space=pltpu.VMEM)
    return pl.pallas_call(
        masked_kernel,
        grid_spec=pltpu.PrefetchScalarGridSpec(
            num_scalar_prefetch=1,
            grid=(),
            in_specs=[vm, vm, vm, vm, ANY],
            out_specs=[vm, vm, vm] + [ANY] * len(sizes),
            scratch_shapes=[
                pltpu.VMEM((parts, WIDTH, WIDTH), BF),
                pltpu.VMEM((rows, FF), F32),
                pltpu.VMEM((rows, FF), BF),
                pltpu.VMEM((rows, WIDTH), BF),
                pltpu.VMEM((parts * WIDTH // ROWS, ROWS, WIDTH), BF),
                pltpu.SemaphoreType.DMA((parts,)),
                pltpu.SemaphoreType.DMA((2,)),
            ],
        ),
        out_shape=[
            jax.ShapeDtypeStruct((rows, WIDTH), F32),
            jax.ShapeDtypeStruct((rows, WIDTH), BF),
            jax.ShapeDtypeStruct((16, WIDTH), F32),
        ]
        + [jax.ShapeDtypeStruct((size, ROWS, WIDTH), BF) for size in sizes],
        compiler_params=pltpu.CompilerParams(vmem_limit_bytes=VMEM_LIMIT),
        cost_estimate=cost(0.024, 30),
        name="masked",
    )(place, tm, cm, cot, vectors, stack)


def attention_back_kernel(
    place_ref,
    tok_ref,
    k_ref,
    v_ref,
    tm_ref,
    qm_ref,
    gc_ref,
    *rest,
):
    arrays = (len(rest) - 7) // 2
    dq_ref, dk_ref, dv_ref, gv_ref, *dws, sum_ref, stage_ref, out_sem = rest[arrays:]
    page, last = pl.program_id(0), pl.num_programs(0) - 1
    per = WIDTH // ROWS
    masks, low = half_masks()

    @pl.when(page == 0)
    def _():
        sum_ref[...] = jnp.zeros_like(sum_ref)
        gv_ref[...] = jnp.zeros_like(gv_ref)

    pairs = [slice(pair * 2 * HD, (pair + 1) * 2 * HD) for pair in range(HEADS // 2)]

    def begin(cols):
        qh, gh = both_heads(qm_ref[:, cols], masks), both_heads(gc_ref[:, cols], masks)
        return qh, gh, mm_last(k_ref[:, cols], qh), mm_last(v_ref[:, cols], gh)

    ahead = begin(pairs[0])
    for i, cols in enumerate(pairs):
        qh, gh, scores, grad_prob = ahead
        if i + 1 < len(pairs):
            ahead = begin(pairs[i + 1])
        top = jnp.max(scores, axis=0, keepdims=True)
        exponent = jnp.exp(scores - top)
        prob = exponent * (1.0 / jnp.sum(exponent, axis=0, keepdims=True))
        spread = jnp.sum(prob * grad_prob, axis=0, keepdims=True)
        grad_s = (prob * (grad_prob - spread)).astype(BF)
        dv_ref[:, cols] = mm(prob.astype(BF), gh).astype(BF)
        dk_ref[:, cols] = mm(grad_s, qh).astype(BF)
        dq = own_lanes(mm_first(grad_s, k_ref[:, cols]), low)
        dq_ref[:, cols] = dq.astype(BF) * QUERY_SCALE
    dq, dk, dv = dq_ref[...], dk_ref[...], dv_ref[...]
    gv_ref[0:1] += row_sum(dq.astype(F32))
    gv_ref[1:2] += row_sum(dv.astype(F32))
    tok = tok_ref[...]
    sum_ref[0] += mm_first(tm_ref[...], dq)
    sum_ref[1] += mm_first(tok, dk)
    sum_ref[2] += mm_first(tok, dv)

    @pl.when(page == last)
    def _():
        for i in range(3):
            stage_ref[pl.ds(i * per, per)] = (
                sum_ref[i].astype(BF).reshape(per, ROWS, WIDTH)
            )

            send_blocks(stage_ref, i * per, per, place_ref, 0, dws, out_sem.at[i])
        for i in range(3):
            wait_blocks(stage_ref, i * per, per, out_sem.at[i])


def attention_back(place, tokens, k, v, tm, qm, gc, dws):
    pages = tokens.shape[0] // PAGE
    page = pl.BlockSpec((PAGE, WIDTH), lambda i, s: (i, 0))
    few = pl.BlockSpec((PAD, WIDTH), lambda i, s: (i, 0))
    tall = jax.ShapeDtypeStruct((pages * PAGE, WIDTH), BF)
    return pl.pallas_call(
        attention_back_kernel,
        grid_spec=pltpu.PrefetchScalarGridSpec(
            num_scalar_prefetch=1,
            grid=(pages,),
            in_specs=[page, page, page, few, few, few] + [ANY] * len(dws),
            out_specs=[few, page, page, pl.BlockSpec((8, WIDTH), lambda i, s: (0, 0))]
            + [ANY] * len(dws),
            scratch_shapes=[
                pltpu.VMEM((3, WIDTH, WIDTH), F32),
                pltpu.VMEM((3 * WIDTH // ROWS, ROWS, WIDTH), BF),
                pltpu.SemaphoreType.DMA((3,)),
            ],
        ),
        out_shape=[
            jax.ShapeDtypeStruct((pages * PAD, WIDTH), BF),
            tall,
            tall,
            jax.ShapeDtypeStruct((8, WIDTH), F32),
        ]
        + [jax.ShapeDtypeStruct(dw.shape, BF) for dw in dws],
        input_output_aliases={7 + i: 4 + i for i in range(len(dws))},
        compiler_params=pltpu.CompilerParams(vmem_limit_bytes=VMEM_LIMIT),
        cost_estimate=cost(0.025, 30),
        name="attention_back",
    )(place, tokens, k, v, tm, qm, gc, *dws)


def forward_kernel(tok_ref, q_ref, k_ref, v_ref, vec_ref, w_any, *rest):
    out_ref, w_ref, ctx_ref, sem = rest[-4:]
    parts = 1 + 2 * UP_ROWS
    load = pltpu.make_async_copy(w_any.at[pl.ds(3 * WIDTH, parts * WIDTH)], w_ref, sem)
    load.start()

    masks, low = half_masks()
    for pair in range(HEADS // 2):
        cols = slice(pair * 2 * HD, (pair + 1) * 2 * HD)
        prob = softmax(mm_last(both_heads(q_ref[:, cols], masks), k_ref[:, cols])).astype(BF)
        ctx_ref[:, cols] = own_lanes(mm(prob, v_ref[:, cols]), low).astype(BF)
    load.wait()
    resid_one = tok_ref[...].astype(F32) + mm(ctx_ref[...], w_ref[0:WIDTH]) + vec_ref[2:3]
    unit_one, _ = unit_of(resid_one)
    hidden_one = unit_one * vec_ref[8:9] + vec_ref[9:10]
    hid = hidden_one.astype(BF)
    resid_two = hidden_one + vec_ref[7:8]
    for c in range(UP_ROWS):
        at, to = (1 + c) * WIDTH, (1 + UP_ROWS + c) * WIDTH
        up = mm_last(hid, w_ref[at : at + WIDTH]) + vec_ref[3 + c : 4 + c]
        act = (up * gelu_cdf(up)).astype(BF)
        resid_two = resid_two + mm(act, w_ref[to : to + WIDTH])
    unit_two, _ = unit_of(resid_two)
    out_ref[...] = (unit_two * vec_ref[10:11] + vec_ref[11:12]).astype(BF)


def forward_page(index, tokens, q, k, v, vectors, stack, before, *after):
    extra = before + after
    page = pl.BlockSpec((PAGE, WIDTH), lambda i: (index, 0))
    whole = pl.BlockSpec((12, WIDTH), lambda i: (0, 0))
    return pl.pallas_call(
        forward_kernel,
        grid=(1,),
        in_specs=[page, page, page, page, whole, ANY] + [ANY] * len(extra),
        out_specs=page,
        out_shape=jax.ShapeDtypeStruct(tokens.shape, BF),
        scratch_shapes=[
            pltpu.VMEM(((1 + 2 * UP_ROWS) * WIDTH, WIDTH), BF),
            pltpu.VMEM((PAGE, WIDTH), BF),
            pltpu.SemaphoreType.DMA,
        ],
        input_output_aliases={6: 0} if before else {},
        compiler_params=pltpu.CompilerParams(vmem_limit_bytes=VMEM_LIMIT),
        cost_estimate=cost(0.0, 0.001),
        name="forward_page",
    )(tokens, q, k, v, vectors, stack, *extra)


def input_grad_kernel(pos_ref, dq_ref, dk_ref, dv_ref, gr_ref, w_any, *rest):
    out_ref, w_ref, sem = rest[-3:]

    @pl.when(pl.program_id(0) == 0)
    def _():
        copy = pltpu.make_async_copy(w_any.at[pl.ds(0, 3 * WIDTH)], w_ref, sem)
        copy.start()
        copy.wait()

    few = gr_ref[...] + mm_last(dq_ref[...], w_ref[0:WIDTH])
    high = few.astype(BF)
    rest = (few - high.astype(F32)).astype(BF)
    pick = one_hot_rows(pos_ref[0])
    out_ref[...] = (
        mm_last(dk_ref[...], w_ref[WIDTH : 2 * WIDTH])
        + mm_last(dv_ref[...], w_ref[2 * WIDTH : 3 * WIDTH])
        + (mm_first(pick, high) + mm_first(pick, rest))
    )


def input_grad(pos, dq, dk, dv, gr, stack, *after):
    pages = dk.shape[0] // PAGE
    page = pl.BlockSpec((PAGE, WIDTH), lambda i: (i, 0))
    few = pl.BlockSpec((PAD, WIDTH), lambda i: (i, 0))
    return pl.pallas_call(
        input_grad_kernel,
        grid=(pages,),
        in_specs=[pl.BlockSpec((1, PAD, 1), lambda i: (i, 0, 0)), few, page, page, few, ANY]
        + [ANY] * len(after),
        out_specs=page,
        out_shape=jax.ShapeDtypeStruct(dk.shape, F32),
        scratch_shapes=[pltpu.VMEM((3 * WIDTH, WIDTH), BF), pltpu.SemaphoreType.DMA],
        compiler_params=pltpu.CompilerParams(vmem_limit_bytes=VMEM_LIMIT),
        cost_estimate=cost(0.0, 0.001),
        name="input_grad",
    )(pos, dq, dk, dv, gr, stack, *after)


def adam_step(parameter, moment_one, moment_two, gradient, rate):
    moment_one = FIRST_DECAY * moment_one + (1.0 - FIRST_DECAY) * gradient
    moment_two = SECOND_DECAY * moment_two + (1.0 - SECOND_DECAY) * gradient * gradient
    ascent = (
        moment_one
        / (1.0 - FIRST_DECAY**STEP)
        / (jnp.sqrt(moment_two / (1.0 - SECOND_DECAY**STEP)) + ADAM_EPSILON)
    )
    return (parameter - rate * (ascent + WEIGHT_DECAY * parameter), moment_one, moment_two)


ORDER = (2, 1, 3, 0)
SIZES = (96, 24, 48, 24)


def swap_dp(x):
    return lax.ppermute(x, "dp", [(0, 1), (1, 0)])


def swap_y(x):
    return lax.ppermute(x, "fsdp", [(f, f ^ 2) for f in range(16)])


def swap_core(x):
    return lax.ppermute(x, "fsdp", [(f, f ^ 1) for f in range(16)])


def up_z(x, steps):
    return lax.ppermute(x, "fsdp", [(f, (f + 4 * steps) % 16) for f in range(16)])


def apart(group, spot):
    me_d, me_f = lax.axis_index("dp"), lax.axis_index("fsdp")
    steps = (spot // 4 - me_f // 4) % 4
    dy = (spot // 2 % 2 + me_f // 2) % 2
    return steps, (group + me_d) % 2, dy, (spot + me_f) % 2


def relative_place(group, spot, turn):
    steps, dx, dy, core = apart(group, spot)
    half, third = turn // 3, turn % 3
    first = jnp.where(dx == 1, 0, 12) + dy * 3
    second = jnp.where(dy == 1, 6, 18) + dx * 3
    inner = jnp.where(half == 0, first, second) + third
    rank = jnp.where(steps == 2, 0, jnp.where(steps == 0, 3, jnp.where(steps == 1, 1, 2)))
    return core * 96 + rank * 24 + inner


def blocks_spec(shape, first=0):
    return pl.BlockSpec(shape, lambda i: (i + first,) + (0,) * (len(shape) - 1))


def core_sum_kernel(keep_ref, from_ref, *rest):
    for part, out in enumerate(rest[-4:]):
        out[0] = keep_ref[0, part] + from_ref[0, part]


def core_sum(keep, got, first, *after):
    count = got.shape[0] // 24
    whole, six = (1, 4, 6, ROWS, WIDTH), (1, 6, ROWS, WIDTH)
    return pl.pallas_call(
        core_sum_kernel,
        grid=(count,),
        in_specs=[blocks_spec(whole, first), blocks_spec(whole)] + [ANY] * len(after),
        out_specs=[blocks_spec(six)] * 4,
        out_shape=[jax.ShapeDtypeStruct((count,) + six[1:], BF)] * 4,
        compiler_params=pltpu.CompilerParams(vmem_limit_bytes=VMEM_LIMIT),
        cost_estimate=cost(0.0, 0.001),
        name="core_sum",
    )(keep.reshape((4,) + whole[1:]), got.reshape((count,) + whole[1:]), *after)


def first_sum_kernel(a_ref, b_ref, to_a_ref, to_b_ref, *rest):
    keep_a, keep_b, send_a, send_b = rest[-4:]
    half_a, half_b = a_ref[0] + to_a_ref[0], b_ref[0] + to_b_ref[0]
    keep_a[0], keep_b[0], send_a[0], send_b[0] = half_a[:3], half_b[:3], half_a[3:], half_b[3:]


def first_sum(a, b, to_a, to_b, *after, weight=0.001):
    count, six, three = a.shape[0], (1, 6, ROWS, WIDTH), (1, 3, ROWS, WIDTH)
    return pl.pallas_call(
        first_sum_kernel,
        grid=(count,),
        in_specs=[blocks_spec(six)] * 4 + [ANY] * len(after),
        out_specs=[blocks_spec(three)] * 4,
        out_shape=[jax.ShapeDtypeStruct((count,) + three[1:], BF)] * 4,
        compiler_params=pltpu.CompilerParams(vmem_limit_bytes=VMEM_LIMIT),
        cost_estimate=cost(0.0, weight),
        name="first_sum",
    )(a, b, to_a, to_b, *after)


def last_sum_kernel(count, passing, a_ref, b_ref, to_a_ref, to_b_ref, *rest):
    for i, out in enumerate(rest[-count:]):
        for low, one, two in ((0, a_ref, to_a_ref), (3, b_ref, to_b_ref)):
            total = one[i].astype(F32) + two[i].astype(F32)
            if i == 0 and passing:
                total = total + rest[0][low : low + 3].astype(F32)
            out[low : low + 3] = total.astype(BF)


def last_sum(a, b, to_a, to_b, passing, *after):
    count = a.shape[0]
    return pl.pallas_call(
        functools.partial(last_sum_kernel, count, len(passing)),
        in_specs=[VM] * (4 + len(passing)) + [ANY] * len(after),
        out_specs=[VM] * count,
        out_shape=[jax.ShapeDtypeStruct((6, ROWS, WIDTH), BF)] * count,
        compiler_params=pltpu.CompilerParams(vmem_limit_bytes=VMEM_LIMIT),
        cost_estimate=cost(0.0, 0.001),
        name="last_sum",
    )(a, b, to_a, to_b, *passing, *after)


def reduce_blocks(dws, tasks, early):
    keep = dws[0]
    got = [swap_core(send) for send in dws[1:]]
    xs_far, ys_far, a_far, b_far = core_sum(keep, got[0], 0)
    to_far = swap_dp(xs_far), swap_y(ys_far)
    a_far, b_far, ys_far, xs_far = first_sum(a_far, b_far, *to_far)
    to_far = swap_y(ys_far), swap_dp(xs_far)
    xs_near, ys_near, a_near, b_near = core_sum(keep, got[1], 1, ys_far, early)
    to_near = swap_dp(xs_near), swap_y(ys_near)
    done = tasks[0](xs_near)
    a_near, b_near, ys_near, xs_near = first_sum(a_near, b_near, *to_near, done)
    to_near = swap_y(ys_near), swap_dp(xs_near)
    (far,) = last_sum(a_far, b_far, *to_far, (), ys_near)
    xs_own, ys_own, a_own, b_own = core_sum(keep, got[2], 3, far)
    far = up_z(far, 1)
    to_own = swap_dp(xs_own), swap_y(ys_own)
    up, down = last_sum(a_near, b_near, *to_near, (far,), xs_own)
    near = up_z(up, 1), up_z(down, 3)
    a_own, b_own, ys_own, xs_own = first_sum(a_own, b_own, *to_own, up)
    to_own = swap_y(ys_own), swap_dp(xs_own)
    done = tasks[1](ys_own)
    return (a_own, to_own[0], b_own, to_own[1]), near, done


def weight_step_kernel(halves, wholes, *refs):
    half_refs, refs = refs[:halves], refs[halves:]
    whole_refs, refs = refs[:wholes], refs[wholes:]
    state_ref, grad_out, new_out = refs[0], refs[-2], refs[-1]
    for i in range(grad_out.shape[0]):
        parts = [ref[i] for ref in whole_refs]
        if halves:
            first = 2 * (i // 3)
            parts += [ref[0, i % 3] for ref in half_refs[first : first + 2]]
        total = parts[0].astype(F32)
        for part in parts[1:]:
            total = total + part.astype(F32)
        grad = total.astype(BF)
        grad_out[i] = grad
        new, _, _ = adam_step(
            state_ref[i, 0].astype(F32),
            state_ref[i, 1].astype(F32),
            state_ref[i, 2].astype(F32),
            grad.astype(F32),
            LEARN_RATE,
        )
        new_out[i] = new.astype(BF)


def weight_step(halves, wholes, states, *after):
    count = states.shape[0]
    shape = jax.ShapeDtypeStruct((count, ROWS, WIDTH), BF)
    return pl.pallas_call(
        functools.partial(weight_step_kernel, len(halves), len(wholes)),
        in_specs=[VM] * (len(halves) + len(wholes) + 1) + [ANY] * len(after),
        out_specs=[VM] * 2,
        out_shape=[shape, shape],
        compiler_params=pltpu.CompilerParams(vmem_limit_bytes=VMEM_LIMIT),
        cost_estimate=cost(0.0, 0.001),
        name="weight_step",
    )(*halves, *wholes, states, *after)


def moment_step_kernel(info_ref, grad_ref, first_ref, second_ref, *rest):
    one_ref, two_ref = rest[-2:]
    count = first_ref.shape[0]
    for i in range(count):
        slot = 2 * (pl.program_id(0) * count + i) + info_ref[0]
        grad = jnp.where(slot < info_ref[1], grad_ref[i].astype(F32), 0.0)
        one_ref[i, 0] = FIRST_DECAY * first_ref[i, 0] + (1.0 - FIRST_DECAY) * grad
        two_ref[i, 0] = SECOND_DECAY * second_ref[i, 0] + (1.0 - SECOND_DECAY) * grad * grad


def moment_step(info, grads, first, second, before, *after):
    half = grads.shape[0]
    each = 4 if half % 4 == 0 else 2
    pairs = (half, 2, ROWS, WIDTH)
    slots = pl.BlockSpec((each, 1, ROWS, WIDTH), lambda i, s: (i, s[0], 0, 0))
    shape = jax.ShapeDtypeStruct(pairs, F32)
    extra = before + after
    return tuple(
        pl.pallas_call(
            moment_step_kernel,
            grid_spec=pltpu.PrefetchScalarGridSpec(
                num_scalar_prefetch=1,
                grid=(half // each,),
                in_specs=[pl.BlockSpec((each, ROWS, WIDTH), lambda i, s: (i, 0, 0)), slots, slots]
                + [ANY] * len(extra),
                out_specs=[slots, slots],
            ),
            out_shape=[shape, shape],
            input_output_aliases={4: 0, 5: 1} if before else {},
            compiler_params=pltpu.CompilerParams(vmem_limit_bytes=VMEM_LIMIT),
            cost_estimate=cost(0.0, 0.001),
            name="moment_step",
        )(info, grads, first.reshape(pairs), second.reshape(pairs), *extra)
    )


def pick_kernel(sizes, arrays, from_ref, *refs):
    outs, sem = refs[-1 - len(sizes) : -1], refs[-1]
    slot = 0
    for out, size in zip(outs, sizes):

        @pl.loop(0, size)
        def _(i, out=out, slot=slot):
            number, low = from_ref[slot + i], 0
            for array in refs[:arrays]:
                high = low + array.shape[0]

                @pl.when((number >= low) & (number < high))
                def _(array=array, low=low):
                    pltpu.make_async_copy(
                        array.at[number - low], out.at[i], sem.at[slot + i]
                    ).start()

                low = high

        slot += size
    slot = 0
    for out, size in zip(outs, sizes):

        @pl.loop(0, size)
        def _(i, out=out, slot=slot):
            pltpu.make_async_copy(refs[0].at[0], out.at[i], sem.at[slot + i]).wait()

        slot += size


def pick_blocks(source, arrays, sizes, *after):
    arrays = [array.reshape(-1, ROWS, WIDTH) for array in arrays]
    return pl.pallas_call(
        functools.partial(pick_kernel, sizes, len(arrays)),
        grid_spec=pltpu.PrefetchScalarGridSpec(
            num_scalar_prefetch=1,
            grid=(),
            in_specs=[ANY] * (len(arrays) + len(after)),
            out_specs=[VM] * len(sizes),
            scratch_shapes=[pltpu.SemaphoreType.DMA((sum(sizes),))],
        ),
        out_shape=[jax.ShapeDtypeStruct((size, ROWS, WIDTH), BF) for size in sizes],
        compiler_params=pltpu.CompilerParams(vmem_limit_bytes=VMEM_LIMIT),
        cost_estimate=cost(0.0, 0.001),
        name="pick_blocks",
    )(source, *arrays, *after)


def move_kernel(plan, *refs):
    for out, pieces in zip(refs[-len(plan) :], plan):
        at = 0
        for source, low, high in pieces:
            out[at : at + high - low] = refs[source][low:high]
            at += high - low


def move(plan, arrays, *after):
    return pl.pallas_call(
        functools.partial(move_kernel, plan),
        in_specs=[VM] * len(arrays) + [ANY] * len(after),
        out_specs=[VM] * len(plan),
        out_shape=[
            jax.ShapeDtypeStruct((sum(high - low for _, low, high in pieces), ROWS, WIDTH), BF)
            for pieces in plan
        ],
        compiler_params=pltpu.CompilerParams(vmem_limit_bytes=VMEM_LIMIT),
        cost_estimate=cost(0.0, 0.001),
        name="move",
    )(*arrays, *after)


ENDS = (((0, 0, 3),), ((1, 3, 6),))
TWO_ENDS = (((0, 0, 3), (0, 6, 9)), ((1, 3, 6), (1, 9, 12)))


def gather_blocks(mine, tasks):
    up, down = up_z(mine, 1), up_z(mine, 3)
    far = up_z(up, 1)
    own_x, own_y = swap_dp(mine), swap_y(mine)
    done = tasks[0](mine)
    end_x, end_y = move(ENDS, [own_x, own_y], *done)
    own = [mine, own_x, own_y, swap_y(end_x), swap_dp(end_y)]
    (near,) = move((((0, 0, 6), (1, 0, 6)),), [up, down], end_x)
    near_x, near_y = swap_dp(near), swap_y(near)
    done = tasks[1](near)
    if len(tasks) == 2:
        far_x, far_y = swap_dp(far), swap_y(far)
        end_x, end_y = move(TWO_ENDS, [near_x, near_y], *done, far)
        near = [near, near_x, near_y, swap_y(end_x), swap_dp(end_y)]
        end_x, end_y = move(ENDS, [far_x, far_y], end_x)
    else:
        (far,) = move((((0, 0, 6),),), [far], *done)
        far_x, far_y = swap_dp(far), swap_y(far)
        end_x, end_y = move(TWO_ENDS, [near_x, near_y], far, *own[3:])
        near = [near, near_x, near_y, swap_y(end_x), swap_dp(end_y)]
        done = tasks[2](end_x)
        end_x, end_y = move(ENDS, [far_x, far_y], *done)
    far = [far, far_x, far_y, swap_y(end_x), swap_dp(end_y)]
    return own + far + near, end_x


PIECES = ((1, 288), (1, 288), (1, 288), (1, 144), (1, 144))
PIECES += PIECES + tuple((2 * number, rows) for number, rows in PIECES)
PIECES += PIECES


def piece_rows():
    me_d, me_f = lax.axis_index("dp"), lax.axis_index("fsdp")
    rows = []
    for core in (0, 1):
        for steps in ((0,), (2,), (1, 3)):
            for dx, dy, low in ((0, 0, 0), (1, 0, 0), (0, 1, 0), (1, 1, 0), (1, 1, 144)):
                for step in steps:
                    z = (me_f // 4 - step) % 4
                    y, c = (me_f // 2 + dy) % 2, (me_f + core) % 2
                    rows.append((((z * 2 + y) * 2 + c) * 2 + (me_d + dx) % 2) * 288 + low)
    return jnp.stack(rows).astype(jnp.int32)


def gather_stack(weights, early):
    half = weights.shape[0] // 2
    mine = lax.dynamic_slice(weights, (lax.axis_index("dp") * half, 0), (half, WIDTH))
    tasks = [lambda *after: early, lambda *after: after]
    arrays, done = gather_blocks(mine.reshape(-1, ROWS, WIDTH), tasks)
    arrays += [swap_core(array) for array in arrays]
    return [array.reshape(-1, WIDTH) for array in arrays], done


def gathered_place(group, spot, turn):
    ahead, dx, dy, core = apart(group, spot)
    steps = (4 - ahead) % 4
    side, pair = dx + 2 * dy, steps // 2
    plain = jnp.where(steps == 2, 24, 0) + side * 6 + turn
    corner = jnp.where(turn < 3, 84 + pair * 3 + turn, 90 + pair * 3 + turn - 3)
    near = jnp.where(side == 3, corner, 48 + side * 12 + pair * 6 + turn)
    steps_odd = steps % 2 == 1
    return jnp.where(steps_odd, near, plain), core == 0


def local(
    groups,
    tokens,
    masked_pos,
    masked_count,
    out_grad,
    weights,
    vectors,
    owner_list,
    master_slots,
    first_slots,
    second_slots,
    vector_first,
    vector_second,
):
    pages = masked_pos.shape[0]
    capacity = master_slots.shape[0]
    held = weights.shape[0] // ROWS
    spread = lax.axis_size("fsdp")
    me_f = lax.axis_index("fsdp")
    ids = groups * spread
    each = NBLK // ids
    lanes = -(-capacity // ids)
    my_group = lax.axis_index("dp") if groups > 1 else 0
    me = me_f * groups + my_group

    blocks = jnp.arange(NBLK, dtype=jnp.int32)
    lower = owner_list[None, :] < owner_list[:, None]
    tied = (owner_list[None, :] == owner_list[:, None]) & (blocks[None, :] < blocks[:, None])
    rank = jnp.sum((lower | tied).astype(jnp.int32), axis=1)
    group, spot, turn = rank % groups, rank % ids // groups, rank // ids
    place = (group * spread + spot) * each + turn
    direct = groups == 2 and spread == 16 and each == 6 and pages == 3
    if direct:
        sizes = SIZES
        put = relative_place(group, spot, turn)
    else:
        sizes, put = (NBLK,), place
    owners = jnp.arange(spread, dtype=jnp.int32)
    start = jnp.sum((owner_list[None, :] < owners[:, None]).astype(jnp.int32), axis=1)
    count = jnp.sum((owner_list[None, :] == owners[:, None]).astype(jnp.int32), axis=1)
    lane = jnp.arange(lanes, dtype=jnp.int32) * ids

    my_start, my_count = start[me_f], count[me_f]
    slot_to = ((owners * groups + my_group - my_start) % ids)[:, None] + lane[None, :]
    slot_to = jnp.minimum(slot_to, capacity - 1).reshape(-1)
    slot_at = ((me - start) % ids)[:, None] + lane[None, :]
    send_to = jnp.clip((start[:, None] + slot_at) // ids, 0, each - 1).reshape(-1)
    my_rank = me + ids * jnp.arange(each, dtype=jnp.int32)
    my_owner = jnp.sum((start + count)[None, :] <= my_rank[:, None], axis=1).astype(jnp.int32)
    my_lane = (my_rank - start[my_owner]) // ids
    state_at = my_owner * lanes + my_lane
    lead = (my_group - my_start) % 2 if groups > 1 else 0
    slots = jnp.arange(capacity // 2, dtype=jnp.int32) * 2

    def grad_at(first):
        which = slots + first
        return ((my_start + which) % ids // groups) * lanes + which // ids

    info = [jnp.stack([jnp.asarray(side, jnp.int32), my_count]) for side in (lead, 1 - lead)]

    states = jnp.stack(
        [
            jnp.take(master_slots, slot_to, axis=0, mode="clip").astype(BF),
            jnp.take(first_slots, slot_to, axis=0, mode="clip").astype(BF),
            jnp.take(second_slots, slot_to, axis=0, mode="clip").astype(BF),
        ],
        axis=1,
    )

    live = jnp.arange(MASKM, dtype=jnp.int32)[None, :] < masked_count[:, None]
    pos = jnp.pad(
        jnp.where(live, masked_pos, -1), ((0, 0), (0, PAD - MASKM)), constant_values=-1
    )[:, :, None]
    cot = jnp.pad(
        jnp.where(live[:, :, None], out_grad, jnp.zeros((), BF)), ((0, 0), (0, PAD - MASKM), (0, 0))
    ).reshape(pages * PAD, WIDTH)

    if direct:
        pieces, done = gather_stack(weights, (states, cot))
        rows, counts = piece_rows(), PIECES
        done, states = lax.optimization_barrier((done, states))
    else:
        pieces, rows, counts = [lax.all_gather(weights, "fsdp", axis=0, tiled=True)], jnp.zeros((1,), jnp.int32), ()
    states = lax.all_to_all(states, "fsdp", 0, 0, tiled=True)
    q, k, v, tm, qm, cm, *stack = project(tokens, pos, vectors, pieces, rows, counts)
    stack = stack[0] if direct else pieces[0]
    gr, gc, gv, *dws = masked_part(put, sizes, tm, cm, cot, vectors, stack)
    dq, dk, dv, gv_attn, *dws = attention_back(put, tokens, k, v, tm, qm, gc, dws)
    grad_vectors = jnp.concatenate([gv_attn[0:2], gv[2:12]], axis=0)
    layer_out, token_grad = [], []

    def page_task(page, *after):
        layer_out[:] = [
            forward_page(page, tokens, q, k, v, vectors, stack, tuple(layer_out), *after)
        ]
        return layer_out[0]

    def grad_task(*after):
        token_grad.append(input_grad(pos, dq, dk, dv, gr, stack, *after))
        return token_grad[0]

    tasks = [functools.partial(page_task, page) for page in range(pages)] + [grad_task]
    arrived = states
    states = jnp.take(states, state_at, axis=0, mode="clip")
    if direct:
        halves, wholes, done = reduce_blocks(dws, tasks, arrived)
    else:
        if groups > 1:
            mine = lax.psum_scatter(dws[0], ("dp", "fsdp"), scatter_dimension=0, tiled=True)
        else:
            mine = lax.psum_scatter(dws[0], "fsdp", scatter_dimension=0, tiled=True)
            mine = lax.psum(mine, "dp")
        for task in tasks:
            done = task()
        halves, wholes = (), (mine,)
    mine, new_mine = weight_step(halves, wholes, states, done)
    mine, grad_vectors = lax.optimization_barrier((mine, grad_vectors))
    grad_vectors = jnp.sum(lax.all_gather(grad_vectors, ("dp", "fsdp")), axis=0)

    held_first = me_f * held

    def held_table(table, first):
        return lax.dynamic_slice(table, (first,), (held,))

    def exchange(*after):
        (send,) = pick_blocks(send_to, [mine], (spread * lanes,), *after)
        return send, lax.all_to_all(send, "fsdp", 0, 0, tiled=True)

    if direct:
        kept = []

        def send_task(*after):
            send, owned = exchange(*after)
            kept.append(owned)
            return (tasks[2](send),)

        def swap_task(*after):
            (even,) = pick_blocks(grad_at(lead), kept, (capacity // 2,), *after)
            kept[:] = even, swap_dp(even)
            return (even,)

        def last_task(*after):
            return (tasks[pages](*after),)

        arrays, done = gather_blocks(new_mine, (last_task, send_task, swap_task))
        at, near = gathered_place(group, spot, turn)
        at = jnp.where(near, at, 0)
        sibling = (me_f + 1 - 2 * (me_f % 2)) * held
        table = jnp.concatenate([held_table(at, held_first), held_table(at, sibling)])
        moments = moment_step(info[0], kept[0], first_slots, second_slots, (), done)
        mine, handed = pick_blocks(table, arrays, (held, held), moments[0])
        new_first, new_second = moment_step(
            info[1], kept[1], first_slots, second_slots, moments, mine
        )
        handed = swap_core(handed)
        ours = held_table(near, held_first)
        new_weights = jnp.where(ours[:, None, None], mine, handed).astype(F32)
    else:
        _, owned = exchange()
        axes = ("dp", "fsdp") if groups > 1 else "fsdp"
        new_all = lax.all_gather(new_mine, axes, axis=0, tiled=True)
        (kept,) = pick_blocks(held_table(place, held_first), [new_all], (held,))
        new_weights = kept.astype(F32)
        if groups > 1:
            (even,) = pick_blocks(grad_at(lead), [owned], (capacity // 2,))
            odd = swap_dp(even)
        else:
            even, odd = pick_blocks(
                jnp.concatenate([grad_at(0), grad_at(1)]), [owned], (capacity // 2, capacity // 2)
            )
        moments = moment_step(info[0], even, first_slots, second_slots, ())
        new_first, new_second = moment_step(info[1], odd, first_slots, second_slots, moments)
    (layer_out,), (token_grad,) = layer_out, token_grad
    new_weights = new_weights.reshape(held * ROWS, WIDTH)
    new_first, new_second = (x.reshape(first_slots.shape) for x in (new_first, new_second))
    new_vectors, new_vector_first, new_vector_second = adam_step(
        vectors, vector_first, vector_second, grad_vectors, VECTOR_RATE
    )
    return (
        layer_out,
        token_grad,
        new_weights,
        new_first,
        new_second,
        new_vectors,
        new_vector_first,
        new_vector_second,
    )


def solution(mesh):
    dp, fsdp = mesh.shape["dp"], mesh.shape["fsdp"]
    groups = 2 if dp == 2 and NBLK % (2 * fsdp) == 0 else 1
    both = ("dp", "fsdp")
    return jax.shard_map(
        functools.partial(local, groups),
        mesh=mesh,
        in_specs=(
            P(both, None),
            P(both, None),
            P(both),
            P(both, None, None),
            P("fsdp", None),
            P(),
            P(),
            P("fsdp", None, None),
            P("fsdp", None, None),
            P("fsdp", None, None),
            P(),
            P(),
        ),
        out_specs=(
            P(both, None),
            P(both, None),
            P("fsdp", None),
            P("fsdp", None, None),
            P("fsdp", None, None),
            P(),
            P(),
            P(),
        ),
        check_vma=False,
    )
```

```python
import functools

import jax
import jax.numpy as jnp
from jax import lax
from jax.experimental import pallas as pl
from jax.experimental.pallas import tpu as pltpu
from jax.sharding import PartitionSpec as P

WIDTH = 768
HEADS = 12
HD = 64
FF = 3072
PAGE = 512
MASKM = 104
ROWS = 48
STEP = 10
NBLK = 192
PAD = 112
STACK = NBLK * ROWS
UP_ROWS = FF // WIDTH

QUERY_SCALE = 0.125
NORM_EPSILON = 1e-06
INV_ROOT_TWO = 0.7071067811865476
INV_ROOT_TAU = 0.3989422804014327
FIRST_DECAY = 0.5
SECOND_DECAY = 0.5
LEARN_RATE = 0.05
VECTOR_RATE = 0.3
WEIGHT_DECAY = 0.01
ADAM_EPSILON = 1e-08

BF = jnp.bfloat16
F32 = jnp.float32
VMEM_LIMIT = 60 * 1024 * 1024
ANY = pl.BlockSpec(memory_space=pl.ANY)
VM = pl.BlockSpec(memory_space=pltpu.VMEM)


def cost(tflop, mbytes):
    return pl.CostEstimate(
        flops=int(tflop * 1e12), bytes_accessed=int(mbytes * 1e6), transcendentals=0
    )


def mm(a, b):
    return lax.dot_general(a, b, (((1,), (0,)), ((), ())), preferred_element_type=F32)


def mm_last(a, b):
    return lax.dot_general(a, b, (((1,), (1,)), ((), ())), preferred_element_type=F32)


def mm_first(a, b):
    return lax.dot_general(a, b, (((0,), (0,)), ((), ())), preferred_element_type=F32)


def send_blocks(stage_ref, first, count, place_ref, shift, arrays, sem):
    @pl.loop(first, first + count)
    def _(i):
        place, low = place_ref[shift + i], 0
        for array in arrays:
            high = low + array.shape[0]

            @pl.when((place >= low) & (place < high))
            def _(array=array, low=low):
                pltpu.make_async_copy(stage_ref.at[i], array.at[place - low], sem).start()

            low = high


def wait_blocks(stage_ref, first, count, sem):
    blocks = stage_ref.at[pl.ds(first, count)]
    pltpu.make_async_copy(blocks, blocks, sem).wait()


def row_sum(x):
    return jnp.sum(x, axis=0, keepdims=True)


def unit_of(x):
    center = x - jnp.mean(x, axis=1, keepdims=True)
    inverse = lax.rsqrt(jnp.mean(center * center, axis=1, keepdims=True) + NORM_EPSILON)
    return center * inverse, inverse


def unit_back(grad_out, gain, unit, inverse):
    grad_unit = grad_out * gain
    centered = grad_unit - jnp.mean(grad_unit, axis=1, keepdims=True)
    return inverse * (centered - unit * jnp.mean(grad_unit * unit, axis=1, keepdims=True))


def gelu_cdf(u):
    return 0.5 * (1.0 + lax.erf(u * INV_ROOT_TWO))


def half_masks():
    lane = lax.broadcasted_iota(jnp.int32, (1, 2 * HD), 1)
    low = jnp.where(lane < HD, 1.0, 0.0)
    return (low.astype(BF), (1.0 - low).astype(BF)), lane < HD


def both_heads(x, masks):
    return jnp.concatenate([x * masks[0], x * masks[1]], axis=0)


def own_lanes(x, low):
    rows = x.shape[0] // 2
    return jnp.where(low, x[:rows], x[rows:])


def softmax(scores):
    top = jnp.max(scores, axis=1, keepdims=True)
    exponent = jnp.exp(scores - top)
    total = jnp.sum(exponent, axis=1, keepdims=True)
    return exponent * (1.0 / total)


def one_hot_rows(pos):
    return jnp.where(
        pos == lax.broadcasted_iota(jnp.int32, (PAD, PAGE), 1), 1.0, 0.0
    ).astype(BF)


def project_kernel(counts, rows_ref, pos_ref, tok_ref, vec_ref, *rest):
    pieces, rest = rest[: max(1, len(counts))], rest[max(1, len(counts)) :]
    q_ref, k_ref, v_ref, tm_ref, qm_ref, cm_ref, *stacks, w_ref, sem = rest
    step, last = pl.program_id(0), pl.num_programs(0) - 1

    def cut(first, act):
        at = 0
        for piece, (number, size) in zip(pieces, counts):

            @pl.loop(0, number)
            def _(i, piece=piece, size=size, at=at):
                row = pl.multiple_of(rows_ref[at + i], 16)

                @pl.when((row < 3 * WIDTH) == first)
                def _():
                    source = piece.at[pl.ds(pl.multiple_of(i * size, 16), size)]
                    target = w_ref.at[pl.ds(row, size)]
                    act(pltpu.make_async_copy(source, target, sem.at[1 + at + i]))

            at += number

    @pl.when(step == 0)
    def _():
        if counts:
            cut(True, lambda copy: copy.start())
            cut(False, lambda copy: copy.start())
            cut(True, lambda copy: copy.wait())
        else:
            copy = pltpu.make_async_copy(pieces[0].at[pl.ds(0, 3 * WIDTH)], w_ref, sem.at[0])
            copy.start()
            copy.wait()

    if counts:

        @pl.when(step == 1)
        def _():
            cut(False, lambda copy: copy.wait())
            pltpu.make_async_copy(w_ref, stacks[0], sem.at[0]).start()

    tok = tok_ref[...]
    q = ((mm(tok, w_ref[0:WIDTH]) + vec_ref[0:1]) * QUERY_SCALE).astype(BF)
    k = mm(tok, w_ref[WIDTH : 2 * WIDTH]).astype(BF)
    v = (mm(tok, w_ref[2 * WIDTH : 3 * WIDTH]) + vec_ref[1:2]).astype(BF)
    q_ref[...] = q
    k_ref[...] = k
    v_ref[...] = v
    pick = one_hot_rows(pos_ref[0])
    tm_ref[...] = mm(pick, tok).astype(BF)
    qm = mm(pick, q).astype(BF)
    qm_ref[...] = qm
    masks, low = half_masks()
    pairs = [slice(pair * 2 * HD, (pair + 1) * 2 * HD) for pair in range(HEADS // 2)]

    def scores_of(cols):
        return mm_last(both_heads(qm[:, cols], masks), k[:, cols])

    ahead = scores_of(pairs[0])
    for i, cols in enumerate(pairs):
        scores = ahead
        if i + 1 < len(pairs):
            ahead = scores_of(pairs[i + 1])
        prob = softmax(scores).astype(BF)
        cm_ref[:, cols] = own_lanes(mm(prob, v[:, cols]), low).astype(BF)

    if counts:

        @pl.when(step == last)
        def _():
            pltpu.make_async_copy(w_ref, stacks[0], sem.at[0]).wait()


def project(tokens, pos, vectors, pieces, rows, counts):
    pages = tokens.shape[0] // PAGE
    tall = jax.ShapeDtypeStruct((pages * PAGE, WIDTH), BF)
    short = jax.ShapeDtypeStruct((pages * PAD, WIDTH), BF)
    page = pl.BlockSpec((PAGE, WIDTH), lambda i, s: (i, 0))
    few = pl.BlockSpec((PAD, WIDTH), lambda i, s: (i, 0))
    stack = [jax.ShapeDtypeStruct((STACK, WIDTH), BF)] if counts else []
    total = sum(number for number, _ in counts)
    return pl.pallas_call(
        functools.partial(project_kernel, counts),
        grid_spec=pltpu.PrefetchScalarGridSpec(
            num_scalar_prefetch=1,
            grid=(pages,),
            in_specs=[
                pl.BlockSpec((1, PAD, 1), lambda i, s: (i, 0, 0)),
                page,
                pl.BlockSpec((12, WIDTH), lambda i, s: (0, 0)),
            ]
            + [ANY] * len(pieces),
            out_specs=[page, page, page, few, few, few] + [ANY] * len(stack),
            scratch_shapes=[
                pltpu.VMEM((STACK if counts else 3 * WIDTH, WIDTH), BF),
                pltpu.SemaphoreType.DMA((1 + total,)),
            ],
        ),
        out_shape=[tall, tall, tall, short, short, short] + stack,
        compiler_params=pltpu.CompilerParams(vmem_limit_bytes=VMEM_LIMIT),
        cost_estimate=cost(0.018, 20),
        name="project",
    )(rows, pos, tokens, vectors, *pieces)


def masked_kernel(
    place_ref,
    tm_ref,
    cm_ref,
    cot_ref,
    vec_ref,
    w_any,
    gr_ref,
    gc_ref,
    gv_ref,
    *rest,
):
    *dws, w_ref, up_ref, act_ref, hid_ref, stage_ref, in_sem, out_sem = rest
    parts = 1 + 2 * UP_ROWS
    loads = [
        pltpu.make_async_copy(
            w_any.at[pl.ds((3 + i) * WIDTH, WIDTH)], w_ref.at[i], in_sem.at[i]
        )
        for i in range(parts)
    ]
    for load in loads:
        load.start()
    per = WIDTH // ROWS

    def keep(part, value):
        stage_ref[pl.ds(part * per, per)] = value.astype(BF).reshape(per, ROWS, WIDTH)

    gain_one, shift_one = vec_ref[8:9], vec_ref[9:10]
    gain_two = vec_ref[10:11]
    cm = cm_ref[...]
    loads[0].wait()
    resid_one = tm_ref[...].astype(F32) + mm(cm, w_ref[0]) + vec_ref[2:3]
    unit_one, inv_one = unit_of(resid_one)
    hidden_one = unit_one * gain_one + shift_one
    hid_ref[...] = hidden_one.astype(BF)
    hid = hid_ref[...]
    for c in range(UP_ROWS):
        cols = slice(c * WIDTH, (c + 1) * WIDTH)
        loads[1 + c].wait()
        up = mm_last(hid, w_ref[1 + c]) + vec_ref[3 + c : 4 + c]
        cdf = gelu_cdf(up)
        up_ref[:, cols] = cdf + up * jnp.exp(-0.5 * up * up) * INV_ROOT_TAU
        act_ref[:, cols] = (up * cdf).astype(BF)
    resid_two = hidden_one + vec_ref[7:8]
    for c in range(UP_ROWS):
        cols = slice(c * WIDTH, (c + 1) * WIDTH)
        loads[1 + UP_ROWS + c].wait()
        resid_two = resid_two + mm(act_ref[:, cols], w_ref[1 + UP_ROWS + c])
    unit_two, inv_two = unit_of(resid_two)
    cot = cot_ref[...].astype(F32)
    grad_two = unit_back(cot, gain_two, unit_two, inv_two)
    gv_ref[...] = jnp.zeros_like(gv_ref)
    gv_ref[10:11] = row_sum(cot * unit_two)
    gv_ref[11:12] = row_sum(cot)
    down = grad_two.astype(BF)
    gv_ref[7:8] = row_sum(down.astype(F32))
    grad_hidden = grad_two
    for c in range(UP_ROWS):
        cols = slice(c * WIDTH, (c + 1) * WIDTH)
        keep(1 + UP_ROWS + c, mm_first(act_ref[:, cols], down))
        grad_up = (mm_last(down, w_ref[1 + UP_ROWS + c]) * up_ref[:, cols]).astype(BF)
        gv_ref[3 + c : 4 + c] = row_sum(grad_up.astype(F32))
        keep(1 + c, mm_first(grad_up, hid))
        grad_hidden = grad_hidden + mm(grad_up, w_ref[1 + c])
    send_blocks(stage_ref, per, 2 * UP_ROWS * per, place_ref, 3 * per, dws, out_sem.at[1])
    gv_ref[8:9] = row_sum(grad_hidden * unit_one)
    gv_ref[9:10] = row_sum(grad_hidden)
    grad_one = unit_back(grad_hidden, gain_one, unit_one, inv_one)
    gr_ref[...] = grad_one
    attn = grad_one.astype(BF)
    gv_ref[2:3] = row_sum(attn.astype(F32))
    keep(0, mm_first(cm, attn))
    send_blocks(stage_ref, 0, per, place_ref, 3 * per, dws, out_sem.at[0])
    gc_ref[...] = mm_last(attn, w_ref[0]).astype(BF)
    wait_blocks(stage_ref, 0, per, out_sem.at[0])
    wait_blocks(stage_ref, per, 2 * UP_ROWS * per, out_sem.at[1])


def masked_part(place, sizes, tm, cm, cot, vectors, stack):
    rows = tm.shape[0]
    parts = 1 + 2 * UP_ROWS
    vm = pl.BlockSpec(memory_space=pltpu.VMEM)
    return pl.pallas_call(
        masked_kernel,
        grid_spec=pltpu.PrefetchScalarGridSpec(
            num_scalar_prefetch=1,
            grid=(),
            in_specs=[vm, vm, vm, vm, ANY],
            out_specs=[vm, vm, vm] + [ANY] * len(sizes),
            scratch_shapes=[
                pltpu.VMEM((parts, WIDTH, WIDTH), BF),
                pltpu.VMEM((rows, FF), F32),
                pltpu.VMEM((rows, FF), BF),
                pltpu.VMEM((rows, WIDTH), BF),
                pltpu.VMEM((parts * WIDTH // ROWS, ROWS, WIDTH), BF),
                pltpu.SemaphoreType.DMA((parts,)),
                pltpu.SemaphoreType.DMA((2,)),
            ],
        ),
        out_shape=[
            jax.ShapeDtypeStruct((rows, WIDTH), F32),
            jax.ShapeDtypeStruct((rows, WIDTH), BF),
            jax.ShapeDtypeStruct((16, WIDTH), F32),
        ]
        + [jax.ShapeDtypeStruct((size, ROWS, WIDTH), BF) for size in sizes],
        compiler_params=pltpu.CompilerParams(vmem_limit_bytes=VMEM_LIMIT),
        cost_estimate=cost(0.024, 30),
        name="masked",
    )(place, tm, cm, cot, vectors, stack)


def attention_back_kernel(
    place_ref,
    tok_ref,
    k_ref,
    v_ref,
    tm_ref,
    qm_ref,
    gc_ref,
    *rest,
):
    arrays = (len(rest) - 7) // 2
    dq_ref, dk_ref, dv_ref, gv_ref, *dws, sum_ref, stage_ref, out_sem = rest[arrays:]
    page, last = pl.program_id(0), pl.num_programs(0) - 1
    per = WIDTH // ROWS
    masks, low = half_masks()

    @pl.when(page == 0)
    def _():
        sum_ref[...] = jnp.zeros_like(sum_ref)
        gv_ref[...] = jnp.zeros_like(gv_ref)

    pairs = [slice(pair * 2 * HD, (pair + 1) * 2 * HD) for pair in range(HEADS // 2)]

    def begin(cols):
        qh, gh = both_heads(qm_ref[:, cols], masks), both_heads(gc_ref[:, cols], masks)
        return qh, gh, mm_last(k_ref[:, cols], qh), mm_last(v_ref[:, cols], gh)

    ahead = begin(pairs[0])
    for i, cols in enumerate(pairs):
        qh, gh, scores, grad_prob = ahead
        if i + 1 < len(pairs):
            ahead = begin(pairs[i + 1])
        top = jnp.max(scores, axis=0, keepdims=True)
        exponent = jnp.exp(scores - top)
        prob = exponent * (1.0 / jnp.sum(exponent, axis=0, keepdims=True))
        spread = jnp.sum(prob * grad_prob, axis=0, keepdims=True)
        grad_s = (prob * (grad_prob - spread)).astype(BF)
        dv_ref[:, cols] = mm(prob.astype(BF), gh).astype(BF)
        dk_ref[:, cols] = mm(grad_s, qh).astype(BF)
        dq = own_lanes(mm_first(grad_s, k_ref[:, cols]), low)
        dq_ref[:, cols] = dq.astype(BF) * QUERY_SCALE
    dq, dk, dv = dq_ref[...], dk_ref[...], dv_ref[...]
    gv_ref[0:1] += row_sum(dq.astype(F32))
    gv_ref[1:2] += row_sum(dv.astype(F32))
    tok = tok_ref[...]
    sum_ref[0] += mm_first(tm_ref[...], dq)
    sum_ref[1] += mm_first(tok, dk)
    sum_ref[2] += mm_first(tok, dv)

    @pl.when(page == last)
    def _():
        for i in range(3):
            stage_ref[pl.ds(i * per, per)] = (
                sum_ref[i].astype(BF).reshape(per, ROWS, WIDTH)
            )

            send_blocks(stage_ref, i * per, per, place_ref, 0, dws, out_sem.at[i])
        for i in range(3):
            wait_blocks(stage_ref, i * per, per, out_sem.at[i])


def attention_back(place, tokens, k, v, tm, qm, gc, dws):
    pages = tokens.shape[0] // PAGE
    page = pl.BlockSpec((PAGE, WIDTH), lambda i, s: (i, 0))
    few = pl.BlockSpec((PAD, WIDTH), lambda i, s: (i, 0))
    tall = jax.ShapeDtypeStruct((pages * PAGE, WIDTH), BF)
    return pl.pallas_call(
        attention_back_kernel,
        grid_spec=pltpu.PrefetchScalarGridSpec(
            num_scalar_prefetch=1,
            grid=(pages,),
            in_specs=[page, page, page, few, few, few] + [ANY] * len(dws),
            out_specs=[few, page, page, pl.BlockSpec((8, WIDTH), lambda i, s: (0, 0))]
            + [ANY] * len(dws),
            scratch_shapes=[
                pltpu.VMEM((3, WIDTH, WIDTH), F32),
                pltpu.VMEM((3 * WIDTH // ROWS, ROWS, WIDTH), BF),
                pltpu.SemaphoreType.DMA((3,)),
            ],
        ),
        out_shape=[
            jax.ShapeDtypeStruct((pages * PAD, WIDTH), BF),
            tall,
            tall,
            jax.ShapeDtypeStruct((8, WIDTH), F32),
        ]
        + [jax.ShapeDtypeStruct(dw.shape, BF) for dw in dws],
        input_output_aliases={7 + i: 4 + i for i in range(len(dws))},
        compiler_params=pltpu.CompilerParams(vmem_limit_bytes=VMEM_LIMIT),
        cost_estimate=cost(0.025, 30),
        name="attention_back",
    )(place, tokens, k, v, tm, qm, gc, *dws)


def forward_kernel(tok_ref, q_ref, k_ref, v_ref, vec_ref, w_any, *rest):
    out_ref, w_ref, ctx_ref, sem = rest[-4:]
    parts = 1 + 2 * UP_ROWS
    load = pltpu.make_async_copy(w_any.at[pl.ds(3 * WIDTH, parts * WIDTH)], w_ref, sem)
    load.start()

    masks, low = half_masks()
    pairs = [slice(pair * 2 * HD, (pair + 1) * 2 * HD) for pair in range(HEADS // 2)]

    def scores_of(cols):
        return mm_last(both_heads(q_ref[:, cols], masks), k_ref[:, cols])

    ahead = scores_of(pairs[0])
    for i, cols in enumerate(pairs):
        scores = ahead
        if i + 1 < len(pairs):
            ahead = scores_of(pairs[i + 1])
        prob = softmax(scores).astype(BF)
        ctx_ref[:, cols] = own_lanes(mm(prob, v_ref[:, cols]), low).astype(BF)
    load.wait()
    resid_one = tok_ref[...].astype(F32) + mm(ctx_ref[...], w_ref[0:WIDTH]) + vec_ref[2:3]
    unit_one, _ = unit_of(resid_one)
    hidden_one = unit_one * vec_ref[8:9] + vec_ref[9:10]
    hid = hidden_one.astype(BF)
    resid_two = hidden_one + vec_ref[7:8]
    for c in range(UP_ROWS):
        at, to = (1 + c) * WIDTH, (1 + UP_ROWS + c) * WIDTH
        up = mm_last(hid, w_ref[at : at + WIDTH]) + vec_ref[3 + c : 4 + c]
        act = (up * gelu_cdf(up)).astype(BF)
        resid_two = resid_two + mm(act, w_ref[to : to + WIDTH])
    unit_two, _ = unit_of(resid_two)
    out_ref[...] = (unit_two * vec_ref[10:11] + vec_ref[11:12]).astype(BF)


def forward_page(index, tokens, q, k, v, vectors, stack, before, *after):
    extra = before + after
    page = pl.BlockSpec((PAGE, WIDTH), lambda i: (index, 0))
    whole = pl.BlockSpec((12, WIDTH), lambda i: (0, 0))
    return pl.pallas_call(
        forward_kernel,
        grid=(1,),
        in_specs=[page, page, page, page, whole, ANY] + [ANY] * len(extra),
        out_specs=page,
        out_shape=jax.ShapeDtypeStruct(tokens.shape, BF),
        scratch_shapes=[
            pltpu.VMEM(((1 + 2 * UP_ROWS) * WIDTH, WIDTH), BF),
            pltpu.VMEM((PAGE, WIDTH), BF),
            pltpu.SemaphoreType.DMA,
        ],
        input_output_aliases={6: 0} if before else {},
        compiler_params=pltpu.CompilerParams(vmem_limit_bytes=VMEM_LIMIT),
        cost_estimate=cost(0.0, 0.001),
        name="forward_page",
    )(tokens, q, k, v, vectors, stack, *extra)


def input_grad_kernel(pos_ref, dq_ref, dk_ref, dv_ref, gr_ref, w_any, *rest):
    out_ref, w_ref, sem = rest[-3:]

    @pl.when(pl.program_id(0) == 0)
    def _():
        copy = pltpu.make_async_copy(w_any.at[pl.ds(0, 3 * WIDTH)], w_ref, sem)
        copy.start()
        copy.wait()

    few = gr_ref[...] + mm_last(dq_ref[...], w_ref[0:WIDTH])
    high = few.astype(BF)
    rest = (few - high.astype(F32)).astype(BF)
    pick = one_hot_rows(pos_ref[0])
    out_ref[...] = (
        mm_last(dk_ref[...], w_ref[WIDTH : 2 * WIDTH])
        + mm_last(dv_ref[...], w_ref[2 * WIDTH : 3 * WIDTH])
        + (mm_first(pick, high) + mm_first(pick, rest))
    )


def input_grad(pos, dq, dk, dv, gr, stack, *after):
    pages = dk.shape[0] // PAGE
    page = pl.BlockSpec((PAGE, WIDTH), lambda i: (i, 0))
    few = pl.BlockSpec((PAD, WIDTH), lambda i: (i, 0))
    return pl.pallas_call(
        input_grad_kernel,
        grid=(pages,),
        in_specs=[pl.BlockSpec((1, PAD, 1), lambda i: (i, 0, 0)), few, page, page, few, ANY]
        + [ANY] * len(after),
        out_specs=page,
        out_shape=jax.ShapeDtypeStruct(dk.shape, F32),
        scratch_shapes=[pltpu.VMEM((3 * WIDTH, WIDTH), BF), pltpu.SemaphoreType.DMA],
        compiler_params=pltpu.CompilerParams(vmem_limit_bytes=VMEM_LIMIT),
        cost_estimate=cost(0.0, 0.001),
        name="input_grad",
    )(pos, dq, dk, dv, gr, stack, *after)


def adam_step(parameter, moment_one, moment_two, gradient, rate):
    moment_one = FIRST_DECAY * moment_one + (1.0 - FIRST_DECAY) * gradient
    moment_two = SECOND_DECAY * moment_two + (1.0 - SECOND_DECAY) * gradient * gradient
    ascent = (
        moment_one
        / (1.0 - FIRST_DECAY**STEP)
        / (jnp.sqrt(moment_two / (1.0 - SECOND_DECAY**STEP)) + ADAM_EPSILON)
    )
    return (parameter - rate * (ascent + WEIGHT_DECAY * parameter), moment_one, moment_two)


ORDER = (2, 1, 3, 0)
SIZES = (96, 24, 24, 24, 24)


def swap_dp(x):
    return lax.ppermute(x, "dp", [(0, 1), (1, 0)])


def swap_y(x):
    return lax.ppermute(x, "fsdp", [(f, f ^ 2) for f in range(16)])


def swap_core(x):
    return lax.ppermute(x, "fsdp", [(f, f ^ 1) for f in range(16)])


def up_z(x, steps):
    return lax.ppermute(x, "fsdp", [(f, (f + 4 * steps) % 16) for f in range(16)])


def apart(group, spot):
    me_d, me_f = lax.axis_index("dp"), lax.axis_index("fsdp")
    steps = (spot // 4 - me_f // 4) % 4
    dy = (spot // 2 % 2 + me_f // 2) % 2
    return steps, (group + me_d) % 2, dy, (spot + me_f) % 2


def relative_place(group, spot, turn):
    steps, dx, dy, core = apart(group, spot)
    half, third = turn // 3, turn % 3
    first = jnp.where(dx == 1, 0, 12) + dy * 3
    second = jnp.where(dy == 1, 6, 18) + dx * 3
    inner = jnp.where(half == 0, first, second) + third
    rank = jnp.where(steps == 2, 0, jnp.where(steps == 0, 3, jnp.where(steps == 1, 1, 2)))
    return core * 96 + rank * 24 + inner


def blocks_spec(shape, first=0):
    return pl.BlockSpec(shape, lambda i: (i + first,) + (0,) * (len(shape) - 1))


def core_sum_kernel(count, keep_ref, *rest):
    for i in range(count):

        @pl.when(pl.program_id(0) == i)
        def _(i=i):
            for part, out in enumerate(rest[-4:]):
                out[0] = keep_ref[0, part] + rest[i][0, part]


def core_sum(keep, got, first, *after):
    count = len(got)
    whole, six = (1, 4, 6, ROWS, WIDTH), (1, 6, ROWS, WIDTH)
    part = pl.BlockSpec(whole, lambda i: (0, 0, 0, 0, 0))
    return pl.pallas_call(
        functools.partial(core_sum_kernel, count),
        grid=(count,),
        in_specs=[blocks_spec(whole, first)] + [part] * count + [ANY] * len(after),
        out_specs=[blocks_spec(six)] * 4,
        out_shape=[jax.ShapeDtypeStruct((count,) + six[1:], BF)] * 4,
        compiler_params=pltpu.CompilerParams(vmem_limit_bytes=VMEM_LIMIT),
        cost_estimate=cost(0.0, 0.001),
        name="core_sum",
    )(keep.reshape((4,) + whole[1:]), *[x.reshape(whole) for x in got], *after)


def first_sum_kernel(a_ref, b_ref, to_a_ref, to_b_ref, *rest):
    keep_a, keep_b, send_a, send_b = rest[-4:]
    half_a, half_b = a_ref[0] + to_a_ref[0], b_ref[0] + to_b_ref[0]
    keep_a[0], keep_b[0], send_a[0], send_b[0] = half_a[:3], half_b[:3], half_a[3:], half_b[3:]


def first_sum(a, b, to_a, to_b, *after, weight=0.001):
    count, six, three = a.shape[0], (1, 6, ROWS, WIDTH), (1, 3, ROWS, WIDTH)
    return pl.pallas_call(
        first_sum_kernel,
        grid=(count,),
        in_specs=[blocks_spec(six)] * 4 + [ANY] * len(after),
        out_specs=[blocks_spec(three)] * 4,
        out_shape=[jax.ShapeDtypeStruct((count,) + three[1:], BF)] * 4,
        compiler_params=pltpu.CompilerParams(vmem_limit_bytes=VMEM_LIMIT),
        cost_estimate=cost(0.0, weight),
        name="first_sum",
    )(a, b, to_a, to_b, *after)


def last_sum_kernel(count, passing, a_ref, b_ref, to_a_ref, to_b_ref, *rest):
    for i, out in enumerate(rest[-count:]):
        for low, one, two in ((0, a_ref, to_a_ref), (3, b_ref, to_b_ref)):
            total = one[i].astype(F32) + two[i].astype(F32)
            if i == 0 and passing:
                total = total + rest[0][low : low + 3].astype(F32)
            out[low : low + 3] = total.astype(BF)


def last_sum(a, b, to_a, to_b, passing, *after):
    count = a.shape[0]
    return pl.pallas_call(
        functools.partial(last_sum_kernel, count, len(passing)),
        in_specs=[VM] * (4 + len(passing)) + [ANY] * len(after),
        out_specs=[VM] * count,
        out_shape=[jax.ShapeDtypeStruct((6, ROWS, WIDTH), BF)] * count,
        compiler_params=pltpu.CompilerParams(vmem_limit_bytes=VMEM_LIMIT),
        cost_estimate=cost(0.0, 0.001),
        name="last_sum",
    )(a, b, to_a, to_b, *passing, *after)


def reduce_blocks(dws, tasks, early):
    keep = dws[0]
    got = [swap_core(send) for send in dws[1:]]
    xs_far, ys_far, a_far, b_far = core_sum(keep, got[:1], 0)
    to_far = swap_dp(xs_far), swap_y(ys_far)
    a_far, b_far, ys_far, xs_far = first_sum(a_far, b_far, *to_far)
    to_far = swap_y(ys_far), swap_dp(xs_far)
    xs_near, ys_near, a_near, b_near = core_sum(keep, got[1:3], 1, ys_far, early)
    to_near = swap_dp(xs_near), swap_y(ys_near)
    done = tasks[0](xs_near)
    a_near, b_near, ys_near, xs_near = first_sum(a_near, b_near, *to_near, done)
    to_near = swap_y(ys_near), swap_dp(xs_near)
    (far,) = last_sum(a_far, b_far, *to_far, (), ys_near)
    xs_own, ys_own, a_own, b_own = core_sum(keep, got[3:], 3, far)
    far = up_z(far, 1)
    to_own = swap_dp(xs_own), swap_y(ys_own)
    up, down = last_sum(a_near, b_near, *to_near, (far,), xs_own)
    near = up_z(up, 1), up_z(down, 3)
    a_own, b_own, ys_own, xs_own = first_sum(a_own, b_own, *to_own, up)
    to_own = swap_y(ys_own), swap_dp(xs_own)
    done = tasks[1](ys_own)
    return (a_own, to_own[0], b_own, to_own[1]), near, done


def weight_step_kernel(halves, wholes, from_ref, *refs):
    half_refs, refs = refs[:halves], refs[halves:]
    whole_refs, refs = refs[:wholes], refs[wholes:]
    states, (grad_out, new_out, state_ref, sem) = refs[0], refs[-4:]
    count = grad_out.shape[0]
    loads = [
        pltpu.make_async_copy(states.at[from_ref[i]], state_ref.at[i], sem.at[i])
        for i in range(count)
    ]
    for load in loads:
        load.start()
    for i in range(count):
        parts = [ref[i] for ref in whole_refs]
        if halves:
            first = 2 * (i // 3)
            parts += [ref[0, i % 3] for ref in half_refs[first : first + 2]]
        total = parts[0].astype(F32)
        for part in parts[1:]:
            total = total + part.astype(F32)
        grad_out[i] = total.astype(BF)
    for i in range(count):
        loads[i].wait()
        new, _, _ = adam_step(
            state_ref[i, 0].astype(F32),
            state_ref[i, 1].astype(F32),
            state_ref[i, 2].astype(F32),
            grad_out[i].astype(F32),
            LEARN_RATE,
        )
        new_out[i] = new.astype(BF)


def weight_step(source, halves, wholes, states, *after):
    count = source.shape[0]
    shape = jax.ShapeDtypeStruct((count, ROWS, WIDTH), BF)
    return pl.pallas_call(
        functools.partial(weight_step_kernel, len(halves), len(wholes)),
        grid_spec=pltpu.PrefetchScalarGridSpec(
            num_scalar_prefetch=1,
            grid=(),
            in_specs=[VM] * (len(halves) + len(wholes)) + [ANY] * (1 + len(after)),
            out_specs=[VM] * 2,
            scratch_shapes=[
                pltpu.VMEM((count, 3, ROWS, WIDTH), BF),
                pltpu.SemaphoreType.DMA((count,)),
            ],
        ),
        out_shape=[shape, shape],
        compiler_params=pltpu.CompilerParams(vmem_limit_bytes=VMEM_LIMIT),
        cost_estimate=cost(0.0, 0.001),
        name="weight_step",
    )(source, *halves, *wholes, states, *after)


def moment_step_kernel(info_ref, grad_ref, first_ref, second_ref, *rest):
    one_ref, two_ref = rest[-2:]
    count = first_ref.shape[0]
    for i in range(count):
        slot = 2 * (pl.program_id(0) * count + i) + info_ref[0]
        grad = jnp.where(slot < info_ref[1], grad_ref[i].astype(F32), 0.0)
        one_ref[i, 0] = FIRST_DECAY * first_ref[i, 0] + (1.0 - FIRST_DECAY) * grad
        two_ref[i, 0] = SECOND_DECAY * second_ref[i, 0] + (1.0 - SECOND_DECAY) * grad * grad


def moment_step(info, grads, first, second, before, *after):
    half = grads.shape[0]
    each = 4 if half % 4 == 0 else 2
    pairs = (half, 2, ROWS, WIDTH)
    slots = pl.BlockSpec((each, 1, ROWS, WIDTH), lambda i, s: (i, s[0], 0, 0))
    shape = jax.ShapeDtypeStruct(pairs, F32)
    extra = before + after
    return tuple(
        pl.pallas_call(
            moment_step_kernel,
            grid_spec=pltpu.PrefetchScalarGridSpec(
                num_scalar_prefetch=1,
                grid=(half // each,),
                in_specs=[pl.BlockSpec((each, ROWS, WIDTH), lambda i, s: (i, 0, 0)), slots, slots]
                + [ANY] * len(extra),
                out_specs=[slots, slots],
            ),
            out_shape=[shape, shape],
            input_output_aliases={4: 0, 5: 1} if before else {},
            compiler_params=pltpu.CompilerParams(vmem_limit_bytes=VMEM_LIMIT),
            cost_estimate=cost(0.0, 0.001),
            name="moment_step",
        )(info, grads, first.reshape(pairs), second.reshape(pairs), *extra)
    )


def pick_kernel(sizes, arrays, from_ref, *refs):
    outs, sem = refs[-1 - len(sizes) : -1], refs[-1]
    slot = 0
    for out, size in zip(outs, sizes):

        @pl.loop(0, size)
        def _(i, out=out, slot=slot):
            number, low = from_ref[slot + i], 0
            for array in refs[:arrays]:
                high = low + array.shape[0]

                @pl.when((number >= low) & (number < high))
                def _(array=array, low=low):
                    pltpu.make_async_copy(
                        array.at[number - low], out.at[i], sem.at[slot + i]
                    ).start()

                low = high

        slot += size
    slot = 0
    for out, size in zip(outs, sizes):

        @pl.loop(0, size)
        def _(i, out=out, slot=slot):
            pltpu.make_async_copy(refs[0].at[0], out.at[i], sem.at[slot + i]).wait()

        slot += size


def pick_blocks(source, arrays, sizes, *after):
    arrays = [array.reshape(-1, ROWS, WIDTH) for array in arrays]
    return pl.pallas_call(
        functools.partial(pick_kernel, sizes, len(arrays)),
        grid_spec=pltpu.PrefetchScalarGridSpec(
            num_scalar_prefetch=1,
            grid=(),
            in_specs=[ANY] * (len(arrays) + len(after)),
            out_specs=[VM] * len(sizes),
            scratch_shapes=[pltpu.SemaphoreType.DMA((sum(sizes),))],
        ),
        out_shape=[jax.ShapeDtypeStruct((size, ROWS, WIDTH), BF) for size in sizes],
        compiler_params=pltpu.CompilerParams(vmem_limit_bytes=VMEM_LIMIT),
        cost_estimate=cost(0.0, 0.001),
        name="pick_blocks",
    )(source, *arrays, *after)


def move_kernel(plan, *refs):
    for out, pieces in zip(refs[-len(plan) :], plan):
        at = 0
        for source, low, high in pieces:
            out[at : at + high - low] = refs[source][low:high]
            at += high - low


def move(plan, arrays, *after):
    return pl.pallas_call(
        functools.partial(move_kernel, plan),
        in_specs=[VM] * len(arrays) + [ANY] * len(after),
        out_specs=[VM] * len(plan),
        out_shape=[
            jax.ShapeDtypeStruct((sum(high - low for _, low, high in pieces), ROWS, WIDTH), BF)
            for pieces in plan
        ],
        compiler_params=pltpu.CompilerParams(vmem_limit_bytes=VMEM_LIMIT),
        cost_estimate=cost(0.0, 0.001),
        name="move",
    )(*arrays, *after)


ENDS = (((0, 0, 3),), ((1, 3, 6),))
TWO_ENDS = (((0, 0, 3), (0, 6, 9)), ((1, 3, 6), (1, 9, 12)))


def gather_blocks(mine, tasks):
    up, down = up_z(mine, 1), up_z(mine, 3)
    far = up_z(up, 1)
    own_x, own_y = swap_dp(mine), swap_y(mine)
    done = tasks[0](mine)
    end_x, end_y = move(ENDS, [own_x, own_y], *done)
    own = [mine, own_x, own_y, swap_y(end_x), swap_dp(end_y)]
    (near,) = move((((0, 0, 6), (1, 0, 6)),), [up, down], end_x)
    near_x, near_y = swap_dp(near), swap_y(near)
    done = tasks[1](near)
    if len(tasks) == 2:
        far_x, far_y = swap_dp(far), swap_y(far)
        end_x, end_y = move(TWO_ENDS, [near_x, near_y], *done, far)
        near = [near, near_x, near_y, swap_y(end_x), swap_dp(end_y)]
        end_x, end_y = move(ENDS, [far_x, far_y], end_x)
    else:
        (far,) = move((((0, 0, 6),),), [far], *done)
        far_x, far_y = swap_dp(far), swap_y(far)
        end_x, end_y = move(TWO_ENDS, [near_x, near_y], far, *own[3:])
        near = [near, near_x, near_y, swap_y(end_x), swap_dp(end_y)]
        done = tasks[2](end_x)
        end_x, end_y = move(ENDS, [far_x, far_y], *done)
    far = [far, far_x, far_y, swap_y(end_x), swap_dp(end_y)]
    return own + far + near, end_x


PIECES = ((1, 288), (1, 288), (1, 288), (1, 144), (1, 144))
PIECES += PIECES + tuple((2 * number, rows) for number, rows in PIECES)
PIECES += PIECES


def piece_rows():
    me_d, me_f = lax.axis_index("dp"), lax.axis_index("fsdp")
    rows = []
    for core in (0, 1):
        for steps in ((0,), (2,), (1, 3)):
            for dx, dy, low in ((0, 0, 0), (1, 0, 0), (0, 1, 0), (1, 1, 0), (1, 1, 144)):
                for step in steps:
                    z = (me_f // 4 - step) % 4
                    y, c = (me_f // 2 + dy) % 2, (me_f + core) % 2
                    rows.append((((z * 2 + y) * 2 + c) * 2 + (me_d + dx) % 2) * 288 + low)
    return jnp.stack(rows).astype(jnp.int32)


def gather_stack(weights, early):
    half = weights.shape[0] // 2
    mine = lax.dynamic_slice(weights, (lax.axis_index("dp") * half, 0), (half, WIDTH))
    tasks = [lambda *after: early, lambda *after: after]
    arrays, done = gather_blocks(mine.reshape(-1, ROWS, WIDTH), tasks)
    arrays += [swap_core(array) for array in arrays]
    return [array.reshape(-1, WIDTH) for array in arrays], done


def gathered_place(group, spot, turn):
    ahead, dx, dy, core = apart(group, spot)
    steps = (4 - ahead) % 4
    side, pair = dx + 2 * dy, steps // 2
    plain = jnp.where(steps == 2, 24, 0) + side * 6 + turn
    corner = jnp.where(turn < 3, 84 + pair * 3 + turn, 90 + pair * 3 + turn - 3)
    near = jnp.where(side == 3, corner, 48 + side * 12 + pair * 6 + turn)
    steps_odd = steps % 2 == 1
    return jnp.where(steps_odd, near, plain), core == 0


def local(
    groups,
    tokens,
    masked_pos,
    masked_count,
    out_grad,
    weights,
    vectors,
    owner_list,
    master_slots,
    first_slots,
    second_slots,
    vector_first,
    vector_second,
):
    pages = masked_pos.shape[0]
    capacity = master_slots.shape[0]
    held = weights.shape[0] // ROWS
    spread = lax.axis_size("fsdp")
    me_f = lax.axis_index("fsdp")
    ids = groups * spread
    each = NBLK // ids
    lanes = -(-capacity // ids)
    my_group = lax.axis_index("dp") if groups > 1 else 0
    me = me_f * groups + my_group

    blocks = jnp.arange(NBLK, dtype=jnp.int32)
    lower = owner_list[None, :] < owner_list[:, None]
    tied = (owner_list[None, :] == owner_list[:, None]) & (blocks[None, :] < blocks[:, None])
    rank = jnp.sum((lower | tied).astype(jnp.int32), axis=1)
    group, spot, turn = rank % groups, rank % ids // groups, rank // ids
    place = (group * spread + spot) * each + turn
    direct = groups == 2 and spread == 16 and each == 6 and pages == 3
    if direct:
        sizes = SIZES
        put = relative_place(group, spot, turn)
    else:
        sizes, put = (NBLK,), place
    owners = jnp.arange(spread, dtype=jnp.int32)
    start = jnp.sum((owner_list[None, :] < owners[:, None]).astype(jnp.int32), axis=1)
    count = jnp.sum((owner_list[None, :] == owners[:, None]).astype(jnp.int32), axis=1)
    lane = jnp.arange(lanes, dtype=jnp.int32) * ids

    my_start, my_count = start[me_f], count[me_f]
    slot_to = ((owners * groups + my_group - my_start) % ids)[:, None] + lane[None, :]
    slot_to = jnp.minimum(slot_to, capacity - 1).reshape(-1)
    slot_at = ((me - start) % ids)[:, None] + lane[None, :]
    send_to = jnp.clip((start[:, None] + slot_at) // ids, 0, each - 1).reshape(-1)
    my_rank = me + ids * jnp.arange(each, dtype=jnp.int32)
    my_owner = jnp.sum((start + count)[None, :] <= my_rank[:, None], axis=1).astype(jnp.int32)
    my_lane = (my_rank - start[my_owner]) // ids
    state_at = my_owner * lanes + my_lane
    lead = (my_group - my_start) % 2 if groups > 1 else 0
    slots = jnp.arange(capacity // 2, dtype=jnp.int32) * 2

    def grad_at(first):
        which = slots + first
        return ((my_start + which) % ids // groups) * lanes + which // ids

    info = [jnp.stack([jnp.asarray(side, jnp.int32), my_count]) for side in (lead, 1 - lead)]

    states = jnp.stack(
        [
            jnp.take(master_slots, slot_to, axis=0, mode="clip").astype(BF),
            jnp.take(first_slots, slot_to, axis=0, mode="clip").astype(BF),
            jnp.take(second_slots, slot_to, axis=0, mode="clip").astype(BF),
        ],
        axis=1,
    )

    live = jnp.arange(MASKM, dtype=jnp.int32)[None, :] < masked_count[:, None]
    pos = jnp.pad(
        jnp.where(live, masked_pos, -1), ((0, 0), (0, PAD - MASKM)), constant_values=-1
    )[:, :, None]
    cot = jnp.pad(
        jnp.where(live[:, :, None], out_grad, jnp.zeros((), BF)), ((0, 0), (0, PAD - MASKM), (0, 0))
    ).reshape(pages * PAD, WIDTH)

    if direct:
        pieces, done = gather_stack(weights, (states, cot))
        rows, counts = piece_rows(), PIECES
        done, states = lax.optimization_barrier((done, states))
    else:
        pieces, rows, counts = [lax.all_gather(weights, "fsdp", axis=0, tiled=True)], jnp.zeros((1,), jnp.int32), ()
    states = lax.all_to_all(states, "fsdp", 0, 0, tiled=True)
    q, k, v, tm, qm, cm, *stack = project(tokens, pos, vectors, pieces, rows, counts)
    stack = stack[0] if direct else pieces[0]
    gr, gc, gv, *dws = masked_part(put, sizes, tm, cm, cot, vectors, stack)
    dq, dk, dv, gv_attn, *dws = attention_back(put, tokens, k, v, tm, qm, gc, dws)
    grad_vectors = jnp.concatenate([gv_attn[0:2], gv[2:12]], axis=0)
    layer_out, token_grad = [], []

    def page_task(page, *after):
        layer_out[:] = [
            forward_page(page, tokens, q, k, v, vectors, stack, tuple(layer_out), *after)
        ]
        return layer_out[0]

    def grad_task(*after):
        token_grad.append(input_grad(pos, dq, dk, dv, gr, stack, *after))
        return token_grad[0]

    tasks = [functools.partial(page_task, page) for page in range(pages)] + [grad_task]
    if direct:
        halves, wholes, done = reduce_blocks(dws, tasks, states)
    else:
        if groups > 1:
            mine = lax.psum_scatter(dws[0], ("dp", "fsdp"), scatter_dimension=0, tiled=True)
        else:
            mine = lax.psum_scatter(dws[0], "fsdp", scatter_dimension=0, tiled=True)
            mine = lax.psum(mine, "dp")
        for task in tasks:
            done = task()
        halves, wholes = (), (mine,)
    mine, new_mine = weight_step(state_at, halves, wholes, states, done)
    mine, grad_vectors = lax.optimization_barrier((mine, grad_vectors))
    grad_vectors = jnp.sum(lax.all_gather(grad_vectors, ("dp", "fsdp")), axis=0)

    held_first = me_f * held

    def held_table(table, first):
        return lax.dynamic_slice(table, (first,), (held,))

    def exchange(*after):
        (send,) = pick_blocks(send_to, [mine], (spread * lanes,), *after)
        return send, lax.all_to_all(send, "fsdp", 0, 0, tiled=True)

    if direct:
        kept = []

        def send_task(*after):
            send, owned = exchange(*after)
            kept.append(owned)
            return (tasks[2](send),)

        def swap_task(*after):
            (even,) = pick_blocks(grad_at(lead), kept, (capacity // 2,), *after)
            kept[:] = even, swap_dp(even)
            return (even,)

        def last_task(*after):
            return (tasks[pages](*after),)

        arrays, done = gather_blocks(new_mine, (last_task, send_task, swap_task))
        at, near = gathered_place(group, spot, turn)
        at = jnp.where(near, at, 0)
        sibling = (me_f + 1 - 2 * (me_f % 2)) * held
        table = jnp.concatenate([held_table(at, held_first), held_table(at, sibling)])
        moments = moment_step(info[0], kept[0], first_slots, second_slots, (), done)
        mine, handed = pick_blocks(table, arrays, (held, held), moments[0])
        new_first, new_second = moment_step(
            info[1], kept[1], first_slots, second_slots, moments, mine
        )
        handed = swap_core(handed)
        ours = held_table(near, held_first)
        new_weights = jnp.where(ours[:, None, None], mine, handed).astype(F32)
    else:
        _, owned = exchange()
        axes = ("dp", "fsdp") if groups > 1 else "fsdp"
        new_all = lax.all_gather(new_mine, axes, axis=0, tiled=True)
        (kept,) = pick_blocks(held_table(place, held_first), [new_all], (held,))
        new_weights = kept.astype(F32)
        if groups > 1:
            (even,) = pick_blocks(grad_at(lead), [owned], (capacity // 2,))
            odd = swap_dp(even)
        else:
            even, odd = pick_blocks(
                jnp.concatenate([grad_at(0), grad_at(1)]), [owned], (capacity // 2, capacity // 2)
            )
        moments = moment_step(info[0], even, first_slots, second_slots, ())
        new_first, new_second = moment_step(info[1], odd, first_slots, second_slots, moments)
    (layer_out,), (token_grad,) = layer_out, token_grad
    new_weights = new_weights.reshape(held * ROWS, WIDTH)
    new_first, new_second = (x.reshape(first_slots.shape) for x in (new_first, new_second))
    new_vectors, new_vector_first, new_vector_second = adam_step(
        vectors, vector_first, vector_second, grad_vectors, VECTOR_RATE
    )
    return (
        layer_out,
        token_grad,
        new_weights,
        new_first,
        new_second,
        new_vectors,
        new_vector_first,
        new_vector_second,
    )


def solution(mesh):
    dp, fsdp = mesh.shape["dp"], mesh.shape["fsdp"]
    groups = 2 if dp == 2 and NBLK % (2 * fsdp) == 0 else 1
    both = ("dp", "fsdp")
    return jax.shard_map(
        functools.partial(local, groups),
        mesh=mesh,
        in_specs=(
            P(both, None),
            P(both, None),
            P(both),
            P(both, None, None),
            P("fsdp", None),
            P(),
            P(),
            P("fsdp", None, None),
            P("fsdp", None, None),
            P("fsdp", None, None),
            P(),
            P(),
        ),
        out_specs=(
            P(both, None),
            P(both, None),
            P("fsdp", None),
            P("fsdp", None, None),
            P("fsdp", None, None),
            P(),
            P(),
            P(),
        ),
        check_vma=False,
    )
```

```python
import functools

import jax
import jax.numpy as jnp
from jax import lax
from jax.experimental import pallas as pl
from jax.experimental.pallas import tpu as pltpu
from jax.sharding import PartitionSpec as P

WIDTH = 768
HEADS = 12
HD = 64
FF = 3072
PAGE = 512
MASKM = 104
ROWS = 48
STEP = 10
NBLK = 192
PAD = 112
STACK = NBLK * ROWS
UP_ROWS = FF // WIDTH

QUERY_SCALE = 0.125
NORM_EPSILON = 1e-06
INV_ROOT_TWO = 0.7071067811865476
INV_ROOT_TAU = 0.3989422804014327
FIRST_DECAY = 0.5
SECOND_DECAY = 0.5
LEARN_RATE = 0.05
VECTOR_RATE = 0.3
WEIGHT_DECAY = 0.01
ADAM_EPSILON = 1e-08

BF = jnp.bfloat16
F32 = jnp.float32
VMEM_LIMIT = 60 * 1024 * 1024
ANY = pl.BlockSpec(memory_space=pl.ANY)
VM = pl.BlockSpec(memory_space=pltpu.VMEM)


def cost(tflop, mbytes):
    return pl.CostEstimate(
        flops=int(tflop * 1e12), bytes_accessed=int(mbytes * 1e6), transcendentals=0
    )


def mm(a, b):
    return lax.dot_general(a, b, (((1,), (0,)), ((), ())), preferred_element_type=F32)


def mm_last(a, b):
    return lax.dot_general(a, b, (((1,), (1,)), ((), ())), preferred_element_type=F32)


def mm_first(a, b):
    return lax.dot_general(a, b, (((0,), (0,)), ((), ())), preferred_element_type=F32)


def send_blocks(stage_ref, first, count, place_ref, shift, arrays, sem):
    @pl.loop(first, first + count)
    def _(i):
        place, low = place_ref[shift + i], 0
        for array in arrays:
            high = low + array.shape[0]

            @pl.when((place >= low) & (place < high))
            def _(array=array, low=low):
                pltpu.make_async_copy(stage_ref.at[i], array.at[place - low], sem).start()

            low = high


def wait_blocks(stage_ref, first, count, sem):
    blocks = stage_ref.at[pl.ds(first, count)]
    pltpu.make_async_copy(blocks, blocks, sem).wait()


def row_sum(x):
    return jnp.sum(x, axis=0, keepdims=True)


def unit_of(x):
    center = x - jnp.mean(x, axis=1, keepdims=True)
    inverse = lax.rsqrt(jnp.mean(center * center, axis=1, keepdims=True) + NORM_EPSILON)
    return center * inverse, inverse


def unit_back(grad_out, gain, unit, inverse):
    grad_unit = grad_out * gain
    centered = grad_unit - jnp.mean(grad_unit, axis=1, keepdims=True)
    return inverse * (centered - unit * jnp.mean(grad_unit * unit, axis=1, keepdims=True))


def gelu_cdf(u):
    return 0.5 * (1.0 + lax.erf(u * INV_ROOT_TWO))


def half_masks():
    lane = lax.broadcasted_iota(jnp.int32, (1, 2 * HD), 1)
    low = jnp.where(lane < HD, 1.0, 0.0)
    return (low.astype(BF), (1.0 - low).astype(BF)), lane < HD


def both_heads(x, masks):
    return jnp.concatenate([x * masks[0], x * masks[1]], axis=0)


def own_lanes(x, low):
    rows = x.shape[0] // 2
    return jnp.where(low, x[:rows], x[rows:])


def softmax(scores):
    top = jnp.max(scores, axis=1, keepdims=True)
    exponent = jnp.exp(scores - top)
    total = jnp.sum(exponent, axis=1, keepdims=True)
    return exponent * (1.0 / total)


def one_hot_rows(pos):
    return jnp.where(
        pos == lax.broadcasted_iota(jnp.int32, (PAD, PAGE), 1), 1.0, 0.0
    ).astype(BF)


def project_kernel(counts, rows_ref, pos_ref, tok_ref, vec_ref, *rest):
    pieces, rest = rest[: max(1, len(counts))], rest[max(1, len(counts)) :]
    q_ref, k_ref, v_ref, tm_ref, qm_ref, cm_ref, *stacks, w_ref, sem = rest
    step, last = pl.program_id(0), pl.num_programs(0) - 1

    def cut(first, act):
        at = 0
        for piece, (number, size) in zip(pieces, counts):

            @pl.loop(0, number)
            def _(i, piece=piece, size=size, at=at):
                row = pl.multiple_of(rows_ref[at + i], 16)

                @pl.when((row < 3 * WIDTH) == first)
                def _():
                    source = piece.at[pl.ds(pl.multiple_of(i * size, 16), size)]
                    target = w_ref.at[pl.ds(row, size)]
                    act(pltpu.make_async_copy(source, target, sem.at[1 + at + i]))

            at += number

    @pl.when(step == 0)
    def _():
        if counts:
            cut(True, lambda copy: copy.start())
            cut(False, lambda copy: copy.start())
            cut(True, lambda copy: copy.wait())
        else:
            copy = pltpu.make_async_copy(pieces[0].at[pl.ds(0, 3 * WIDTH)], w_ref, sem.at[0])
            copy.start()
            copy.wait()

    if counts:

        @pl.when(step == 1)
        def _():
            cut(False, lambda copy: copy.wait())
            pltpu.make_async_copy(w_ref, stacks[0], sem.at[0]).start()

    tok = tok_ref[...]
    q = ((mm(tok, w_ref[0:WIDTH]) + vec_ref[0:1]) * QUERY_SCALE).astype(BF)
    k = mm(tok, w_ref[WIDTH : 2 * WIDTH]).astype(BF)
    v = (mm(tok, w_ref[2 * WIDTH : 3 * WIDTH]) + vec_ref[1:2]).astype(BF)
    q_ref[...] = q
    k_ref[...] = k
    v_ref[...] = v
    pick = one_hot_rows(pos_ref[0])
    tm_ref[...] = mm(pick, tok).astype(BF)
    qm = mm(pick, q).astype(BF)
    qm_ref[...] = qm
    masks, low = half_masks()
    pairs = [slice(pair * 2 * HD, (pair + 1) * 2 * HD) for pair in range(HEADS // 2)]

    def scores_of(cols):
        return mm_last(both_heads(qm[:, cols], masks), k[:, cols])

    ahead = scores_of(pairs[0])
    for i, cols in enumerate(pairs):
        scores = ahead
        if i + 1 < len(pairs):
            ahead = scores_of(pairs[i + 1])
        prob = softmax(scores).astype(BF)
        cm_ref[:, cols] = own_lanes(mm(prob, v[:, cols]), low).astype(BF)

    if counts:

        @pl.when(step == last)
        def _():
            pltpu.make_async_copy(w_ref, stacks[0], sem.at[0]).wait()


def project(tokens, pos, vectors, pieces, rows, counts):
    pages = tokens.shape[0] // PAGE
    tall = jax.ShapeDtypeStruct((pages * PAGE, WIDTH), BF)
    short = jax.ShapeDtypeStruct((pages * PAD, WIDTH), BF)
    page = pl.BlockSpec((PAGE, WIDTH), lambda i, s: (i, 0))
    few = pl.BlockSpec((PAD, WIDTH), lambda i, s: (i, 0))
    stack = [jax.ShapeDtypeStruct((STACK, WIDTH), BF)] if counts else []
    total = sum(number for number, _ in counts)
    return pl.pallas_call(
        functools.partial(project_kernel, counts),
        grid_spec=pltpu.PrefetchScalarGridSpec(
            num_scalar_prefetch=1,
            grid=(pages,),
            in_specs=[
                pl.BlockSpec((1, PAD, 1), lambda i, s: (i, 0, 0)),
                page,
                pl.BlockSpec((12, WIDTH), lambda i, s: (0, 0)),
            ]
            + [ANY] * len(pieces),
            out_specs=[page, page, page, few, few, few] + [ANY] * len(stack),
            scratch_shapes=[
                pltpu.VMEM((STACK if counts else 3 * WIDTH, WIDTH), BF),
                pltpu.SemaphoreType.DMA((1 + total,)),
            ],
        ),
        out_shape=[tall, tall, tall, short, short, short] + stack,
        compiler_params=pltpu.CompilerParams(vmem_limit_bytes=VMEM_LIMIT),
        cost_estimate=cost(0.018, 20),
        name="project",
    )(rows, pos, tokens, vectors, *pieces)


def masked_kernel(
    place_ref,
    tm_ref,
    cm_ref,
    cot_ref,
    vec_ref,
    w_any,
    gr_ref,
    gc_ref,
    gv_ref,
    *rest,
):
    *dws, w_ref, up_ref, act_ref, hid_ref, stage_ref, in_sem, out_sem = rest
    parts = 1 + 2 * UP_ROWS
    loads = [
        pltpu.make_async_copy(
            w_any.at[pl.ds((3 + i) * WIDTH, WIDTH)], w_ref.at[i], in_sem.at[i]
        )
        for i in range(parts)
    ]
    for load in loads:
        load.start()
    per = WIDTH // ROWS

    def keep(part, value):
        stage_ref[pl.ds(part * per, per)] = value.astype(BF).reshape(per, ROWS, WIDTH)

    gain_one, shift_one = vec_ref[8:9], vec_ref[9:10]
    gain_two = vec_ref[10:11]
    cm = cm_ref[...]
    loads[0].wait()
    resid_one = tm_ref[...].astype(F32) + mm(cm, w_ref[0]) + vec_ref[2:3]
    unit_one, inv_one = unit_of(resid_one)
    hidden_one = unit_one * gain_one + shift_one
    hid_ref[...] = hidden_one.astype(BF)
    hid = hid_ref[...]
    for c in range(UP_ROWS):
        cols = slice(c * WIDTH, (c + 1) * WIDTH)
        loads[1 + c].wait()
        up = mm_last(hid, w_ref[1 + c]) + vec_ref[3 + c : 4 + c]
        cdf = gelu_cdf(up)
        up_ref[:, cols] = cdf + up * jnp.exp(-0.5 * up * up) * INV_ROOT_TAU
        act_ref[:, cols] = (up * cdf).astype(BF)
    resid_two = hidden_one + vec_ref[7:8]
    for c in range(UP_ROWS):
        cols = slice(c * WIDTH, (c + 1) * WIDTH)
        loads[1 + UP_ROWS + c].wait()
        resid_two = resid_two + mm(act_ref[:, cols], w_ref[1 + UP_ROWS + c])
    unit_two, inv_two = unit_of(resid_two)
    cot = cot_ref[...].astype(F32)
    grad_two = unit_back(cot, gain_two, unit_two, inv_two)
    gv_ref[...] = jnp.zeros_like(gv_ref)
    gv_ref[10:11] = row_sum(cot * unit_two)
    gv_ref[11:12] = row_sum(cot)
    down = grad_two.astype(BF)
    gv_ref[7:8] = row_sum(down.astype(F32))
    grad_hidden = grad_two
    for c in range(UP_ROWS):
        cols = slice(c * WIDTH, (c + 1) * WIDTH)
        keep(1 + UP_ROWS + c, mm_first(act_ref[:, cols], down))
        grad_up = (mm_last(down, w_ref[1 + UP_ROWS + c]) * up_ref[:, cols]).astype(BF)
        gv_ref[3 + c : 4 + c] = row_sum(grad_up.astype(F32))
        keep(1 + c, mm_first(grad_up, hid))
        grad_hidden = grad_hidden + mm(grad_up, w_ref[1 + c])
    send_blocks(stage_ref, per, 2 * UP_ROWS * per, place_ref, 3 * per, dws, out_sem.at[1])
    gv_ref[8:9] = row_sum(grad_hidden * unit_one)
    gv_ref[9:10] = row_sum(grad_hidden)
    grad_one = unit_back(grad_hidden, gain_one, unit_one, inv_one)
    gr_ref[...] = grad_one
    attn = grad_one.astype(BF)
    gv_ref[2:3] = row_sum(attn.astype(F32))
    keep(0, mm_first(cm, attn))
    send_blocks(stage_ref, 0, per, place_ref, 3 * per, dws, out_sem.at[0])
    gc_ref[...] = mm_last(attn, w_ref[0]).astype(BF)
    wait_blocks(stage_ref, 0, per, out_sem.at[0])
    wait_blocks(stage_ref, per, 2 * UP_ROWS * per, out_sem.at[1])


def masked_part(place, sizes, tm, cm, cot, vectors, stack):
    rows = tm.shape[0]
    parts = 1 + 2 * UP_ROWS
    vm = pl.BlockSpec(memory_space=pltpu.VMEM)
    return pl.pallas_call(
        masked_kernel,
        grid_spec=pltpu.PrefetchScalarGridSpec(
            num_scalar_prefetch=1,
            grid=(),
            in_specs=[vm, vm, vm, vm, ANY],
            out_specs=[vm, vm, vm] + [ANY] * len(sizes),
            scratch_shapes=[
                pltpu.VMEM((parts, WIDTH, WIDTH), BF),
                pltpu.VMEM((rows, FF), F32),
                pltpu.VMEM((rows, FF), BF),
                pltpu.VMEM((rows, WIDTH), BF),
                pltpu.VMEM((parts * WIDTH // ROWS, ROWS, WIDTH), BF),
                pltpu.SemaphoreType.DMA((parts,)),
                pltpu.SemaphoreType.DMA((2,)),
            ],
        ),
        out_shape=[
            jax.ShapeDtypeStruct((rows, WIDTH), F32),
            jax.ShapeDtypeStruct((rows, WIDTH), BF),
            jax.ShapeDtypeStruct((16, WIDTH), F32),
        ]
        + [jax.ShapeDtypeStruct((size, ROWS, WIDTH), BF) for size in sizes],
        compiler_params=pltpu.CompilerParams(vmem_limit_bytes=VMEM_LIMIT),
        cost_estimate=cost(0.024, 30),
        name="masked",
    )(place, tm, cm, cot, vectors, stack)


def attention_back_kernel(
    place_ref,
    tok_ref,
    k_ref,
    v_ref,
    tm_ref,
    qm_ref,
    gc_ref,
    *rest,
):
    arrays = (len(rest) - 7) // 2
    dq_ref, dk_ref, dv_ref, gv_ref, *dws, sum_ref, stage_ref, out_sem = rest[arrays:]
    page, last = pl.program_id(0), pl.num_programs(0) - 1
    per = WIDTH // ROWS
    masks, low = half_masks()

    @pl.when(page == 0)
    def _():
        sum_ref[...] = jnp.zeros_like(sum_ref)
        gv_ref[...] = jnp.zeros_like(gv_ref)

    pairs = [slice(pair * 2 * HD, (pair + 1) * 2 * HD) for pair in range(HEADS // 2)]

    def begin(cols):
        qh, gh = both_heads(qm_ref[:, cols], masks), both_heads(gc_ref[:, cols], masks)
        return qh, gh, mm_last(k_ref[:, cols], qh), mm_last(v_ref[:, cols], gh)

    ahead = begin(pairs[0])
    for i, cols in enumerate(pairs):
        qh, gh, scores, grad_prob = ahead
        if i + 1 < len(pairs):
            ahead = begin(pairs[i + 1])
        top = jnp.max(scores, axis=0, keepdims=True)
        exponent = jnp.exp(scores - top)
        prob = exponent * (1.0 / jnp.sum(exponent, axis=0, keepdims=True))
        spread = jnp.sum(prob * grad_prob, axis=0, keepdims=True)
        grad_s = (prob * (grad_prob - spread)).astype(BF)
        dv_ref[:, cols] = mm(prob.astype(BF), gh).astype(BF)
        dk_ref[:, cols] = mm(grad_s, qh).astype(BF)
        dq = own_lanes(mm_first(grad_s, k_ref[:, cols]), low)
        dq_ref[:, cols] = dq.astype(BF) * QUERY_SCALE
    dq, dk, dv = dq_ref[...], dk_ref[...], dv_ref[...]
    gv_ref[0:1] += row_sum(dq.astype(F32))
    gv_ref[1:2] += row_sum(dv.astype(F32))
    tok = tok_ref[...]
    sum_ref[0] += mm_first(tm_ref[...], dq)
    sum_ref[1] += mm_first(tok, dk)
    sum_ref[2] += mm_first(tok, dv)

    @pl.when(page == last)
    def _():
        for i in range(3):
            stage_ref[pl.ds(i * per, per)] = (
                sum_ref[i].astype(BF).reshape(per, ROWS, WIDTH)
            )

            send_blocks(stage_ref, i * per, per, place_ref, 0, dws, out_sem.at[i])
        for i in range(3):
            wait_blocks(stage_ref, i * per, per, out_sem.at[i])


def attention_back(place, tokens, k, v, tm, qm, gc, dws):
    pages = tokens.shape[0] // PAGE
    page = pl.BlockSpec((PAGE, WIDTH), lambda i, s: (i, 0))
    few = pl.BlockSpec((PAD, WIDTH), lambda i, s: (i, 0))
    tall = jax.ShapeDtypeStruct((pages * PAGE, WIDTH), BF)
    return pl.pallas_call(
        attention_back_kernel,
        grid_spec=pltpu.PrefetchScalarGridSpec(
            num_scalar_prefetch=1,
            grid=(pages,),
            in_specs=[page, page, page, few, few, few] + [ANY] * len(dws),
            out_specs=[few, page, page, pl.BlockSpec((8, WIDTH), lambda i, s: (0, 0))]
            + [ANY] * len(dws),
            scratch_shapes=[
                pltpu.VMEM((3, WIDTH, WIDTH), F32),
                pltpu.VMEM((3 * WIDTH // ROWS, ROWS, WIDTH), BF),
                pltpu.SemaphoreType.DMA((3,)),
            ],
        ),
        out_shape=[
            jax.ShapeDtypeStruct((pages * PAD, WIDTH), BF),
            tall,
            tall,
            jax.ShapeDtypeStruct((8, WIDTH), F32),
        ]
        + [jax.ShapeDtypeStruct(dw.shape, BF) for dw in dws],
        input_output_aliases={7 + i: 4 + i for i in range(len(dws))},
        compiler_params=pltpu.CompilerParams(vmem_limit_bytes=VMEM_LIMIT),
        cost_estimate=cost(0.025, 30),
        name="attention_back",
    )(place, tokens, k, v, tm, qm, gc, *dws)


def forward_kernel(tok_ref, q_ref, k_ref, v_ref, vec_ref, w_any, *rest):
    out_ref, w_ref, ctx_ref, sem = rest[-4:]
    parts = 1 + 2 * UP_ROWS
    load = pltpu.make_async_copy(w_any.at[pl.ds(3 * WIDTH, parts * WIDTH)], w_ref, sem)
    load.start()

    masks, low = half_masks()
    pairs = [slice(pair * 2 * HD, (pair + 1) * 2 * HD) for pair in range(HEADS // 2)]

    def scores_of(cols):
        return mm_last(both_heads(q_ref[:, cols], masks), k_ref[:, cols])

    ahead = scores_of(pairs[0])
    for i, cols in enumerate(pairs):
        scores = ahead
        if i + 1 < len(pairs):
            ahead = scores_of(pairs[i + 1])
        prob = softmax(scores).astype(BF)
        ctx_ref[:, cols] = own_lanes(mm(prob, v_ref[:, cols]), low).astype(BF)
    load.wait()
    resid_one = tok_ref[...].astype(F32) + mm(ctx_ref[...], w_ref[0:WIDTH]) + vec_ref[2:3]
    unit_one, _ = unit_of(resid_one)
    hidden_one = unit_one * vec_ref[8:9] + vec_ref[9:10]
    hid = hidden_one.astype(BF)
    resid_two = hidden_one + vec_ref[7:8]
    for c in range(UP_ROWS):
        at, to = (1 + c) * WIDTH, (1 + UP_ROWS + c) * WIDTH
        up = mm_last(hid, w_ref[at : at + WIDTH]) + vec_ref[3 + c : 4 + c]
        act = (up * gelu_cdf(up)).astype(BF)
        resid_two = resid_two + mm(act, w_ref[to : to + WIDTH])
    unit_two, _ = unit_of(resid_two)
    out_ref[...] = (unit_two * vec_ref[10:11] + vec_ref[11:12]).astype(BF)


def forward_page(index, tokens, q, k, v, vectors, stack, before, *after):
    extra = before + after
    page = pl.BlockSpec((PAGE, WIDTH), lambda i: (index, 0))
    whole = pl.BlockSpec((12, WIDTH), lambda i: (0, 0))
    return pl.pallas_call(
        forward_kernel,
        grid=(1,),
        in_specs=[page, page, page, page, whole, ANY] + [ANY] * len(extra),
        out_specs=page,
        out_shape=jax.ShapeDtypeStruct(tokens.shape, BF),
        scratch_shapes=[
            pltpu.VMEM(((1 + 2 * UP_ROWS) * WIDTH, WIDTH), BF),
            pltpu.VMEM((PAGE, WIDTH), BF),
            pltpu.SemaphoreType.DMA,
        ],
        input_output_aliases={6: 0} if before else {},
        compiler_params=pltpu.CompilerParams(vmem_limit_bytes=VMEM_LIMIT),
        cost_estimate=cost(0.0, 0.001),
        name="forward_page",
    )(tokens, q, k, v, vectors, stack, *extra)


def input_grad_kernel(pos_ref, dq_ref, dk_ref, dv_ref, gr_ref, w_any, *rest):
    out_ref, w_ref, sem = rest[-3:]

    @pl.when(pl.program_id(0) == 0)
    def _():
        copy = pltpu.make_async_copy(w_any.at[pl.ds(0, 3 * WIDTH)], w_ref, sem)
        copy.start()
        copy.wait()

    few = gr_ref[...] + mm_last(dq_ref[...], w_ref[0:WIDTH])
    high = few.astype(BF)
    rest = (few - high.astype(F32)).astype(BF)
    pick = one_hot_rows(pos_ref[0])
    out_ref[...] = (
        mm_last(dk_ref[...], w_ref[WIDTH : 2 * WIDTH])
        + mm_last(dv_ref[...], w_ref[2 * WIDTH : 3 * WIDTH])
        + (mm_first(pick, high) + mm_first(pick, rest))
    )


def input_grad(pos, dq, dk, dv, gr, stack, *after):
    pages = dk.shape[0] // PAGE
    page = pl.BlockSpec((PAGE, WIDTH), lambda i: (i, 0))
    few = pl.BlockSpec((PAD, WIDTH), lambda i: (i, 0))
    return pl.pallas_call(
        input_grad_kernel,
        grid=(pages,),
        in_specs=[pl.BlockSpec((1, PAD, 1), lambda i: (i, 0, 0)), few, page, page, few, ANY]
        + [ANY] * len(after),
        out_specs=page,
        out_shape=jax.ShapeDtypeStruct(dk.shape, F32),
        scratch_shapes=[pltpu.VMEM((3 * WIDTH, WIDTH), BF), pltpu.SemaphoreType.DMA],
        compiler_params=pltpu.CompilerParams(vmem_limit_bytes=VMEM_LIMIT),
        cost_estimate=cost(0.0, 0.001),
        name="input_grad",
    )(pos, dq, dk, dv, gr, stack, *after)


def adam_step(parameter, moment_one, moment_two, gradient, rate):
    moment_one = FIRST_DECAY * moment_one + (1.0 - FIRST_DECAY) * gradient
    moment_two = SECOND_DECAY * moment_two + (1.0 - SECOND_DECAY) * gradient * gradient
    ascent = (
        moment_one
        / (1.0 - FIRST_DECAY**STEP)
        / (jnp.sqrt(moment_two / (1.0 - SECOND_DECAY**STEP)) + ADAM_EPSILON)
    )
    return (parameter - rate * (ascent + WEIGHT_DECAY * parameter), moment_one, moment_two)


ORDER = (2, 1, 3, 0)
SIZES = (96, 24, 24, 24, 24)


def swap_dp(x):
    return lax.ppermute(x, "dp", [(0, 1), (1, 0)])


def swap_y(x):
    return lax.ppermute(x, "fsdp", [(f, f ^ 2) for f in range(16)])


def swap_core(x):
    return lax.ppermute(x, "fsdp", [(f, f ^ 1) for f in range(16)])


def up_z(x, steps):
    return lax.ppermute(x, "fsdp", [(f, (f + 4 * steps) % 16) for f in range(16)])


def apart(group, spot):
    me_d, me_f = lax.axis_index("dp"), lax.axis_index("fsdp")
    steps = (spot // 4 - me_f // 4) % 4
    dy = (spot // 2 % 2 + me_f // 2) % 2
    return steps, (group + me_d) % 2, dy, (spot + me_f) % 2


def relative_place(group, spot, turn):
    steps, dx, dy, core = apart(group, spot)
    half, third = turn // 3, turn % 3
    first = jnp.where(dx == 1, 0, 12) + dy * 3
    second = jnp.where(dy == 1, 6, 18) + dx * 3
    inner = jnp.where(half == 0, first, second) + third
    rank = jnp.where(steps == 2, 0, jnp.where(steps == 0, 3, jnp.where(steps == 1, 1, 2)))
    return core * 96 + rank * 24 + inner


def blocks_spec(shape, first=0):
    return pl.BlockSpec(shape, lambda i: (i + first,) + (0,) * (len(shape) - 1))


def core_sum_kernel(count, keep_ref, *rest):
    for i in range(count):

        @pl.when(pl.program_id(0) == i)
        def _(i=i):
            for part, out in enumerate(rest[-4:]):
                out[0] = keep_ref[0, part] + rest[i][0, part]


def core_sum(keep, got, first, *after):
    count = len(got)
    whole, six = (1, 4, 6, ROWS, WIDTH), (1, 6, ROWS, WIDTH)
    part = pl.BlockSpec(whole, lambda i: (0, 0, 0, 0, 0))
    return pl.pallas_call(
        functools.partial(core_sum_kernel, count),
        grid=(count,),
        in_specs=[blocks_spec(whole, first)] + [part] * count + [ANY] * len(after),
        out_specs=[blocks_spec(six)] * 4,
        out_shape=[jax.ShapeDtypeStruct((count,) + six[1:], BF)] * 4,
        compiler_params=pltpu.CompilerParams(vmem_limit_bytes=VMEM_LIMIT),
        cost_estimate=cost(0.0, 0.001),
        name="core_sum",
    )(keep.reshape((4,) + whole[1:]), *[x.reshape(whole) for x in got], *after)


def first_sum_kernel(a_ref, b_ref, to_a_ref, to_b_ref, *rest):
    keep_a, keep_b, send_a, send_b = rest[-4:]
    half_a, half_b = a_ref[0] + to_a_ref[0], b_ref[0] + to_b_ref[0]
    keep_a[0], keep_b[0], send_a[0], send_b[0] = half_a[:3], half_b[:3], half_a[3:], half_b[3:]


def first_sum(a, b, to_a, to_b, *after, weight=0.001):
    count, six, three = a.shape[0], (1, 6, ROWS, WIDTH), (1, 3, ROWS, WIDTH)
    return pl.pallas_call(
        first_sum_kernel,
        grid=(count,),
        in_specs=[blocks_spec(six)] * 4 + [ANY] * len(after),
        out_specs=[blocks_spec(three)] * 4,
        out_shape=[jax.ShapeDtypeStruct((count,) + three[1:], BF)] * 4,
        compiler_params=pltpu.CompilerParams(vmem_limit_bytes=VMEM_LIMIT),
        cost_estimate=cost(0.0, weight),
        name="first_sum",
    )(a, b, to_a, to_b, *after)


def last_sum_kernel(count, passing, a_ref, b_ref, to_a_ref, to_b_ref, *rest):
    for i, out in enumerate(rest[-count:]):
        for low, one, two in ((0, a_ref, to_a_ref), (3, b_ref, to_b_ref)):
            total = one[i].astype(F32) + two[i].astype(F32)
            if i == 0 and passing:
                total = total + rest[0][low : low + 3].astype(F32)
            out[low : low + 3] = total.astype(BF)


def last_sum(a, b, to_a, to_b, passing, *after):
    count = a.shape[0]
    return pl.pallas_call(
        functools.partial(last_sum_kernel, count, len(passing)),
        in_specs=[VM] * (4 + len(passing)) + [ANY] * len(after),
        out_specs=[VM] * count,
        out_shape=[jax.ShapeDtypeStruct((6, ROWS, WIDTH), BF)] * count,
        compiler_params=pltpu.CompilerParams(vmem_limit_bytes=VMEM_LIMIT),
        cost_estimate=cost(0.0, 0.001),
        name="last_sum",
    )(a, b, to_a, to_b, *passing, *after)


def reduce_blocks(dws, tasks, early):
    keep = dws[0]
    got = [swap_core(send) for send in dws[1:]]
    xs_far, ys_far, a_far, b_far = core_sum(keep, got[:1], 0)
    to_far = swap_dp(xs_far), swap_y(ys_far)
    a_far, b_far, ys_far, xs_far = first_sum(a_far, b_far, *to_far)
    to_far = swap_y(ys_far), swap_dp(xs_far)
    xs_near, ys_near, a_near, b_near = core_sum(keep, got[1:3], 1, ys_far, early)
    to_near = swap_dp(xs_near), swap_y(ys_near)
    done = tasks[0](xs_near)
    a_near, b_near, ys_near, xs_near = first_sum(a_near, b_near, *to_near, done)
    to_near = swap_y(ys_near), swap_dp(xs_near)
    (far,) = last_sum(a_far, b_far, *to_far, (), ys_near)
    xs_own, ys_own, a_own, b_own = core_sum(keep, got[3:], 3, far)
    far = up_z(far, 1)
    to_own = swap_dp(xs_own), swap_y(ys_own)
    up, down = last_sum(a_near, b_near, *to_near, (far,), xs_own)
    near = up_z(up, 1), up_z(down, 3)
    a_own, b_own, ys_own, xs_own = first_sum(a_own, b_own, *to_own, up)
    to_own = swap_y(ys_own), swap_dp(xs_own)
    done = tasks[1](ys_own)
    return (a_own, to_own[0], b_own, to_own[1]), near, done


def weight_step_kernel(halves, wholes, from_ref, *refs):
    half_refs, refs = refs[:halves], refs[halves:]
    whole_refs, refs = refs[:wholes], refs[wholes:]
    states, (grad_out, new_out, state_ref, sem) = refs[0], refs[-4:]
    count = grad_out.shape[0]
    loads = [
        pltpu.make_async_copy(states.at[from_ref[i]], state_ref.at[i], sem.at[i])
        for i in range(count)
    ]
    for load in loads:
        load.start()
    for i in range(count):
        parts = [ref[i] for ref in whole_refs]
        if halves:
            first = 2 * (i // 3)
            parts += [ref[0, i % 3] for ref in half_refs[first : first + 2]]
        total = parts[0].astype(F32)
        for part in parts[1:]:
            total = total + part.astype(F32)
        grad_out[i] = total.astype(BF)
    for i in range(count):
        loads[i].wait()
        new, _, _ = adam_step(
            state_ref[i, 0].astype(F32),
            state_ref[i, 1].astype(F32),
            state_ref[i, 2].astype(F32),
            grad_out[i].astype(F32),
            LEARN_RATE,
        )
        new_out[i] = new.astype(BF)


def weight_step(source, halves, wholes, states, *after):
    count = source.shape[0]
    shape = jax.ShapeDtypeStruct((count, ROWS, WIDTH), BF)
    return pl.pallas_call(
        functools.partial(weight_step_kernel, len(halves), len(wholes)),
        grid_spec=pltpu.PrefetchScalarGridSpec(
            num_scalar_prefetch=1,
            grid=(),
            in_specs=[VM] * (len(halves) + len(wholes)) + [ANY] * (1 + len(after)),
            out_specs=[VM] * 2,
            scratch_shapes=[
                pltpu.VMEM((count, 3, ROWS, WIDTH), BF),
                pltpu.SemaphoreType.DMA((count,)),
            ],
        ),
        out_shape=[shape, shape],
        compiler_params=pltpu.CompilerParams(vmem_limit_bytes=VMEM_LIMIT),
        cost_estimate=cost(0.0, 0.001),
        name="weight_step",
    )(source, *halves, *wholes, states, *after)


def moment_step_kernel(info_ref, grad_ref, first_ref, second_ref, *rest):
    one_ref, two_ref = rest[-2:]
    count = first_ref.shape[0]
    for i in range(count):
        slot = 2 * (pl.program_id(0) * count + i) + info_ref[0]
        grad = jnp.where(slot < info_ref[1], grad_ref[i].astype(F32), 0.0)
        one_ref[i, 0] = FIRST_DECAY * first_ref[i, 0] + (1.0 - FIRST_DECAY) * grad
        two_ref[i, 0] = SECOND_DECAY * second_ref[i, 0] + (1.0 - SECOND_DECAY) * grad * grad


def moment_step(info, grads, first, second, before, *after):
    half = grads.shape[0]
    each = 4 if half % 4 == 0 else 2
    pairs = (half, 2, ROWS, WIDTH)
    slots = pl.BlockSpec((each, 1, ROWS, WIDTH), lambda i, s: (i, s[0], 0, 0))
    shape = jax.ShapeDtypeStruct(pairs, F32)
    extra = before + after
    return tuple(
        pl.pallas_call(
            moment_step_kernel,
            grid_spec=pltpu.PrefetchScalarGridSpec(
                num_scalar_prefetch=1,
                grid=(half // each,),
                in_specs=[pl.BlockSpec((each, ROWS, WIDTH), lambda i, s: (i, 0, 0)), slots, slots]
                + [ANY] * len(extra),
                out_specs=[slots, slots],
            ),
            out_shape=[shape, shape],
            input_output_aliases={4: 0, 5: 1} if before else {},
            compiler_params=pltpu.CompilerParams(vmem_limit_bytes=VMEM_LIMIT),
            cost_estimate=cost(0.0, 0.001),
            name="moment_step",
        )(info, grads, first.reshape(pairs), second.reshape(pairs), *extra)
    )


def pick_kernel(sizes, arrays, from_ref, *refs):
    outs, sem = refs[-1 - len(sizes) : -1], refs[-1]
    slot = 0
    for out, size in zip(outs, sizes):

        @pl.loop(0, size)
        def _(i, out=out, slot=slot):
            number, low = from_ref[slot + i], 0
            for array in refs[:arrays]:
                high = low + array.shape[0]

                @pl.when((number >= low) & (number < high))
                def _(array=array, low=low):
                    pltpu.make_async_copy(
                        array.at[number - low], out.at[i], sem.at[slot + i]
                    ).start()

                low = high

        slot += size
    slot = 0
    for out, size in zip(outs, sizes):

        @pl.loop(0, size)
        def _(i, out=out, slot=slot):
            pltpu.make_async_copy(refs[0].at[0], out.at[i], sem.at[slot + i]).wait()

        slot += size


def pick_blocks(source, arrays, sizes, *after):
    arrays = [array.reshape(-1, ROWS, WIDTH) for array in arrays]
    return pl.pallas_call(
        functools.partial(pick_kernel, sizes, len(arrays)),
        grid_spec=pltpu.PrefetchScalarGridSpec(
            num_scalar_prefetch=1,
            grid=(),
            in_specs=[ANY] * (len(arrays) + len(after)),
            out_specs=[VM] * len(sizes),
            scratch_shapes=[pltpu.SemaphoreType.DMA((sum(sizes),))],
        ),
        out_shape=[jax.ShapeDtypeStruct((size, ROWS, WIDTH), BF) for size in sizes],
        compiler_params=pltpu.CompilerParams(vmem_limit_bytes=VMEM_LIMIT),
        cost_estimate=cost(0.0, 0.001),
        name="pick_blocks",
    )(source, *arrays, *after)


def move_kernel(plan, *refs):
    for out, pieces in zip(refs[-len(plan) :], plan):
        at = 0
        for source, low, high in pieces:
            out[at : at + high - low] = refs[source][low:high]
            at += high - low


def move(plan, arrays, *after):
    return pl.pallas_call(
        functools.partial(move_kernel, plan),
        in_specs=[VM] * len(arrays) + [ANY] * len(after),
        out_specs=[VM] * len(plan),
        out_shape=[
            jax.ShapeDtypeStruct((sum(high - low for _, low, high in pieces), ROWS, WIDTH), BF)
            for pieces in plan
        ],
        compiler_params=pltpu.CompilerParams(vmem_limit_bytes=VMEM_LIMIT),
        cost_estimate=cost(0.0, 0.001),
        name="move",
    )(*arrays, *after)


ENDS = (((0, 0, 3),), ((1, 3, 6),))
TWO_ENDS = (((0, 0, 3), (0, 6, 9)), ((1, 3, 6), (1, 9, 12)))


def gather_blocks(mine, tasks):
    up, down = up_z(mine, 1), up_z(mine, 3)
    far = up_z(up, 1)
    own_x, own_y = swap_dp(mine), swap_y(mine)
    done = tasks[0](mine)
    end_x, end_y = move(ENDS, [own_x, own_y], *done)
    own = [mine, own_x, own_y, swap_y(end_x), swap_dp(end_y)]
    (near,) = move((((0, 0, 6), (1, 0, 6)),), [up, down], end_x)
    near_x, near_y = swap_dp(near), swap_y(near)
    done = tasks[1](near)
    if len(tasks) == 2:
        far_x, far_y = swap_dp(far), swap_y(far)
        end_x, end_y = move(TWO_ENDS, [near_x, near_y], *done, far)
        near = [near, near_x, near_y, swap_y(end_x), swap_dp(end_y)]
        end_x, end_y = move(ENDS, [far_x, far_y], end_x)
    else:
        (far,) = move((((0, 0, 6),),), [far], *done)
        far_x, far_y = swap_dp(far), swap_y(far)
        end_x, end_y = move(TWO_ENDS, [near_x, near_y], far, *own[3:])
        near = [near, near_x, near_y, swap_y(end_x), swap_dp(end_y)]
        done = tasks[2](end_x)
        end_x, end_y = move(ENDS, [far_x, far_y], *done)
    far = [far, far_x, far_y, swap_y(end_x), swap_dp(end_y)]
    return own + far + near, end_x


PIECES = ((1, 288), (1, 288), (1, 288), (1, 144), (1, 144))
PIECES += PIECES + tuple((2 * number, rows) for number, rows in PIECES)
PIECES += PIECES


def piece_rows():
    me_d, me_f = lax.axis_index("dp"), lax.axis_index("fsdp")
    rows = []
    for core in (0, 1):
        for steps in ((0,), (2,), (1, 3)):
            for dx, dy, low in ((0, 0, 0), (1, 0, 0), (0, 1, 0), (1, 1, 0), (1, 1, 144)):
                for step in steps:
                    z = (me_f // 4 - step) % 4
                    y, c = (me_f // 2 + dy) % 2, (me_f + core) % 2
                    rows.append((((z * 2 + y) * 2 + c) * 2 + (me_d + dx) % 2) * 288 + low)
    return jnp.stack(rows).astype(jnp.int32)


def gather_stack(weights, early):
    half = weights.shape[0] // 2
    mine = lax.dynamic_slice(weights, (lax.axis_index("dp") * half, 0), (half, WIDTH))
    tasks = [lambda *after: early, lambda *after: after]
    arrays, done = gather_blocks(mine.reshape(-1, ROWS, WIDTH), tasks)
    arrays += [swap_core(array) for array in arrays]
    return [array.reshape(-1, WIDTH) for array in arrays], done


def gathered_place(group, spot, turn):
    ahead, dx, dy, core = apart(group, spot)
    steps = (4 - ahead) % 4
    side, pair = dx + 2 * dy, steps // 2
    plain = jnp.where(steps == 2, 24, 0) + side * 6 + turn
    corner = jnp.where(turn < 3, 84 + pair * 3 + turn, 90 + pair * 3 + turn - 3)
    near = jnp.where(side == 3, corner, 48 + side * 12 + pair * 6 + turn)
    steps_odd = steps % 2 == 1
    return jnp.where(steps_odd, near, plain), core == 0


def local(
    groups,
    tokens,
    masked_pos,
    masked_count,
    out_grad,
    weights,
    vectors,
    owner_list,
    master_slots,
    first_slots,
    second_slots,
    vector_first,
    vector_second,
):
    pages = masked_pos.shape[0]
    capacity = master_slots.shape[0]
    held = weights.shape[0] // ROWS
    spread = lax.axis_size("fsdp")
    me_f = lax.axis_index("fsdp")
    ids = groups * spread
    each = NBLK // ids
    lanes = -(-capacity // ids)
    my_group = lax.axis_index("dp") if groups > 1 else 0
    me = me_f * groups + my_group

    blocks = jnp.arange(NBLK, dtype=jnp.int32)
    lower = owner_list[None, :] < owner_list[:, None]
    tied = (owner_list[None, :] == owner_list[:, None]) & (blocks[None, :] < blocks[:, None])
    rank = jnp.sum((lower | tied).astype(jnp.int32), axis=1)
    group, spot, turn = rank % groups, rank % ids // groups, rank // ids
    place = (group * spread + spot) * each + turn
    direct = groups == 2 and spread == 16 and each == 6 and pages == 3
    if direct:
        sizes = SIZES
        put = relative_place(group, spot, turn)
    else:
        sizes, put = (NBLK,), place
    owners = jnp.arange(spread, dtype=jnp.int32)
    start = jnp.sum((owner_list[None, :] < owners[:, None]).astype(jnp.int32), axis=1)
    count = jnp.sum((owner_list[None, :] == owners[:, None]).astype(jnp.int32), axis=1)
    lane = jnp.arange(lanes, dtype=jnp.int32) * ids

    my_start, my_count = start[me_f], count[me_f]
    slot_to = ((owners * groups + my_group - my_start) % ids)[:, None] + lane[None, :]
    slot_to = jnp.minimum(slot_to, capacity - 1).reshape(-1)
    slot_at = ((me - start) % ids)[:, None] + lane[None, :]
    send_to = jnp.clip((start[:, None] + slot_at) // ids, 0, each - 1).reshape(-1)
    my_rank = me + ids * jnp.arange(each, dtype=jnp.int32)
    my_owner = jnp.sum((start + count)[None, :] <= my_rank[:, None], axis=1).astype(jnp.int32)
    my_lane = (my_rank - start[my_owner]) // ids
    state_at = my_owner * lanes + my_lane
    lead = (my_group - my_start) % 2 if groups > 1 else 0
    slots = jnp.arange(capacity // 2, dtype=jnp.int32) * 2

    def grad_at(first):
        which = slots + first
        return ((my_start + which) % ids // groups) * lanes + which // ids

    info = [jnp.stack([jnp.asarray(side, jnp.int32), my_count]) for side in (lead, 1 - lead)]

    states = jnp.stack(
        [
            jnp.take(master_slots, slot_to, axis=0, mode="clip").astype(BF),
            jnp.take(first_slots, slot_to, axis=0, mode="clip").astype(BF),
            jnp.take(second_slots, slot_to, axis=0, mode="clip").astype(BF),
        ],
        axis=1,
    )

    live = jnp.arange(MASKM, dtype=jnp.int32)[None, :] < masked_count[:, None]
    pos = jnp.pad(
        jnp.where(live, masked_pos, -1), ((0, 0), (0, PAD - MASKM)), constant_values=-1
    )[:, :, None]
    cot = jnp.pad(
        jnp.where(live[:, :, None], out_grad, jnp.zeros((), BF)), ((0, 0), (0, PAD - MASKM), (0, 0))
    ).reshape(pages * PAD, WIDTH)

    if direct:
        pieces, done = gather_stack(weights, (states, cot))
        rows, counts = piece_rows(), PIECES
        done, states = lax.optimization_barrier((done, states))
    else:
        pieces, rows, counts = [lax.all_gather(weights, "fsdp", axis=0, tiled=True)], jnp.zeros((1,), jnp.int32), ()
    states = lax.all_to_all(states, "fsdp", 0, 0, tiled=True)
    q, k, v, tm, qm, cm, *stack = project(tokens, pos, vectors, pieces, rows, counts)
    stack = stack[0] if direct else pieces[0]
    gr, gc, gv, *dws = masked_part(put, sizes, tm, cm, cot, vectors, stack)
    dq, dk, dv, gv_attn, *dws = attention_back(put, tokens, k, v, tm, qm, gc, dws)
    grad_vectors = jnp.concatenate([gv_attn[0:2], gv[2:12]], axis=0)
    layer_out, token_grad = [], []

    def page_task(page, *after):
        layer_out[:] = [
            forward_page(page, tokens, q, k, v, vectors, stack, tuple(layer_out), *after)
        ]
        return layer_out[0]

    def grad_task(*after):
        token_grad.append(input_grad(pos, dq, dk, dv, gr, stack, *after))
        return token_grad[0]

    tasks = [functools.partial(page_task, page) for page in range(pages)] + [grad_task]
    if direct:
        halves, wholes, done = reduce_blocks(dws, tasks, states)
    else:
        if groups > 1:
            mine = lax.psum_scatter(dws[0], ("dp", "fsdp"), scatter_dimension=0, tiled=True)
        else:
            mine = lax.psum_scatter(dws[0], "fsdp", scatter_dimension=0, tiled=True)
            mine = lax.psum(mine, "dp")
        for task in tasks:
            done = task()
        halves, wholes = (), (mine,)
    mine, new_mine = weight_step(state_at, halves, wholes, states, done)
    mine, grad_vectors = lax.optimization_barrier((mine, grad_vectors))
    grad_vectors = jnp.sum(lax.all_gather(grad_vectors, ("dp", "fsdp")), axis=0)

    held_first = me_f * held

    def held_table(table, first):
        return lax.dynamic_slice(table, (first,), (held,))

    def exchange(*after):
        (send,) = pick_blocks(send_to, [mine], (spread * lanes,), *after)
        return send, lax.all_to_all(send, "fsdp", 0, 0, tiled=True)

    if direct:
        kept = []

        def send_task(*after):
            send, owned = exchange(*after)
            kept.append(owned)
            return (tasks[pages](tasks[2](send)),)

        def swap_task(*after):
            (even,) = pick_blocks(grad_at(lead), kept, (capacity // 2,), *after)
            kept[:] = even, swap_dp(even)
            return (even,)

        arrays, done = gather_blocks(new_mine, (lambda *after: (), send_task, swap_task))
        at, near = gathered_place(group, spot, turn)
        at = jnp.where(near, at, 0)
        sibling = (me_f + 1 - 2 * (me_f % 2)) * held
        table = jnp.concatenate([held_table(at, held_first), held_table(at, sibling)])
        moments = moment_step(info[0], kept[0], first_slots, second_slots, (), done)
        mine, handed = pick_blocks(table, arrays, (held, held), moments[0])
        new_first, new_second = moment_step(
            info[1], kept[1], first_slots, second_slots, moments, mine
        )
        handed = swap_core(handed)
        ours = held_table(near, held_first)
        new_weights = jnp.where(ours[:, None, None], mine, handed).astype(F32)
    else:
        _, owned = exchange()
        axes = ("dp", "fsdp") if groups > 1 else "fsdp"
        new_all = lax.all_gather(new_mine, axes, axis=0, tiled=True)
        (kept,) = pick_blocks(held_table(place, held_first), [new_all], (held,))
        new_weights = kept.astype(F32)
        if groups > 1:
            (even,) = pick_blocks(grad_at(lead), [owned], (capacity // 2,))
            odd = swap_dp(even)
        else:
            even, odd = pick_blocks(
                jnp.concatenate([grad_at(0), grad_at(1)]), [owned], (capacity // 2, capacity // 2)
            )
        moments = moment_step(info[0], even, first_slots, second_slots, ())
        new_first, new_second = moment_step(info[1], odd, first_slots, second_slots, moments)
    (layer_out,), (token_grad,) = layer_out, token_grad
    new_weights = new_weights.reshape(held * ROWS, WIDTH)
    new_first, new_second = (x.reshape(first_slots.shape) for x in (new_first, new_second))
    new_vectors, new_vector_first, new_vector_second = adam_step(
        vectors, vector_first, vector_second, grad_vectors, VECTOR_RATE
    )
    return (
        layer_out,
        token_grad,
        new_weights,
        new_first,
        new_second,
        new_vectors,
        new_vector_first,
        new_vector_second,
    )


def solution(mesh):
    dp, fsdp = mesh.shape["dp"], mesh.shape["fsdp"]
    groups = 2 if dp == 2 and NBLK % (2 * fsdp) == 0 else 1
    both = ("dp", "fsdp")
    return jax.shard_map(
        functools.partial(local, groups),
        mesh=mesh,
        in_specs=(
            P(both, None),
            P(both, None),
            P(both),
            P(both, None, None),
            P("fsdp", None),
            P(),
            P(),
            P("fsdp", None, None),
            P("fsdp", None, None),
            P("fsdp", None, None),
            P(),
            P(),
        ),
        out_specs=(
            P(both, None),
            P(both, None),
            P("fsdp", None),
            P("fsdp", None, None),
            P("fsdp", None, None),
            P(),
            P(),
            P(),
        ),
        check_vma=False,
    )
```
